32 devices in a mesh: seq: 32 (over z, y, x, core).
Axes of the slice: x: 2, y: 2, z: 4, core: 2. Of those that a mesh axis runs over, the one named last changes fastest.
Arguments:
- inputs: bfloat16 [2, 8192, 1024], P(None, 'seq'), may hold values from -6 to 6
- doc_start: int32 [2, 8192], P(None, 'seq'), may hold values from 0 to 8191, as said below
- norm_gain: float32 [1024], replicated, may hold values from 0.5 to 1.5
- w_in: bfloat16 [1024, 3072], P('seq'), may hold values from -0.1875 to 0.1875
- conv_weight: float32 [4, 2048], replicated, may hold values from -3 to 3
- w_low: bfloat16 [1024, 16], replicated, may hold values from -0.1875 to 0.1875
- w_high: float32 [16, 512], replicated, may hold values from -1.5 to 1.5
- gate_bias: float32 [512], replicated, may hold values from 0 to 6
- head_gain: float32 [256], replicated, may hold values from 0.5 to 1.5
- w_out: bfloat16 [1024, 1024], P('seq'), may hold values from -0.375 to 0.375
- ffn_gain: float32 [1024], replicated, may hold values from 0.5 to 1.5
- w_gate_up: bfloat16 [1024, 5632], P('seq'), may hold values from -0.1875 to 0.1875
- w_down: bfloat16 [2816, 1024], P('seq'), may hold values from -0.3125 to 0.3125
- out_grad: bfloat16 [2, 8192, 1024], P(None, 'seq'), may hold values from -6 to 6
Outputs:
- layer_out: float32 [2, 8192, 1024], P(None, 'seq')
- input_grad: float32 [2, 8192, 1024], P(None, 'seq')
- norm_gain_grad: float32 [1024], replicated
- w_in_grad: float32 [1024, 3072], P('seq')
- conv_weight_grad: float32 [4, 2048], replicated
- w_low_grad: float32 [1024, 16], replicated
- w_high_grad: float32 [16, 512], replicated
- gate_bias_grad: float32 [512], replicated
- head_gain_grad: float32 [256], replicated
- w_out_grad: float32 [1024, 1024], P('seq')
- ffn_gain_grad: float32 [1024], replicated
- w_gate_up_grad: float32 [1024, 5632], P('seq')
- w_down_grad: float32 [2816, 1024], P('seq')
The draws below stay inside these ranges and needn't reach their ends.
Inputs may be any that keep to these rules, and one draw needn't show every extreme that they name: `doc_start`: each entry is the position within its sequence of the first token of the token's document, so entries never fall along a sequence and equal their own position at a document's first token; documents hold 200 to 2000 tokens, except the last of a sequence, which the sequence's end may cut.
All inputs are finite; a program needn't handle non-finite values.
Results may differ from the reference program's by a relative error of at most 0.012.
The reference program's roundings to bfloat16 on the way count: a program that leaves them out, or rounds other values in their place, can miss the bound.
Values may be sent and summed in bfloat16 or wider, within the bound.
No kernel may reach another device: no remote copies, remote signals or barrier semaphores. Data moves between devices by JAX's collectives and lax.ppermute only.
A program may use at most 576 MiB of HBM per device.

```python
import jax
import jax.numpy as jnp
from jax import lax

D = 1024
HEADS = 4
DK = 128
DV = 256
RANK = 16
FF = 2816
SPAN = 64
CONV = 4
DOC_LO = 200
DOC_HI = 2000
SEQS = 2
LEN = 8192
KEYS = 512
VALS = 1024


def draw_doc_start(key, part):
    most_docs = LEN // DOC_LO + 2
    doc_lengths = jax.random.randint(key, (SEQS, most_docs), DOC_LO, DOC_HI + 1).astype(jnp.int32)
    doc_ends = jnp.cumsum(doc_lengths, axis=1).astype(jnp.int32)
    doc_firsts = jnp.concatenate([jnp.zeros((SEQS, 1), jnp.int32), doc_ends[:, :-1]], axis=1)
    position = jnp.arange(LEN, dtype=jnp.int32)

    def locate(starts_row):
        return (jnp.searchsorted(starts_row, position, side='right') - 1).astype(jnp.int32)
    which_doc = jax.vmap(locate)(doc_firsts)
    return jnp.take_along_axis(doc_firsts, which_doc, axis=1).astype(jnp.int32)


def block_scale(stream_key, dims, split, low, top_value):
    loudness, own = 1.0, jax.random.fold_in(stream_key, 6)
    for dim, parts in split:
        draws = jnp.exp(jax.random.uniform(jax.random.fold_in(own, dim), (parts,), jnp.float32, low / len(split), top_value / len(split)))
        loudness = loudness * jnp.repeat(draws, dims[dim] // parts).reshape([-1 if axis == dim else 1 for axis in range(len(dims))])
    return loudness


def noise(rng, extent, scale, most, shards=(), held_as=jnp.bfloat16):
    drawn = jax.random.normal(rng, extent, jnp.float32) * scale
    if len(shards) > 0:
        drawn = block_scale(rng, extent, shards, -0.22, 0.18) * drawn
    return jnp.clip(drawn, min=-most, max=most).astype(held_as)


def setup_inputs(seed: int = 0) -> dict:
    streams_of = jax.random.split(jax.random.key(seed), 15)
    return {
        "inputs": noise(streams_of[0], (SEQS, LEN, D), 1.0, 6.0, ((1, 32),)),
        "doc_start": draw_doc_start(jax.random.fold_in(streams_of[14], 71), 0),
        "norm_gain": jnp.clip(1.0 + 0.1 * jax.random.normal(streams_of[2], (D,), jnp.float32), 0.5, 1.5),
        "w_in": noise(streams_of[3], (D, 2 * KEYS + 2 * VALS), D ** -0.5, 0.1875, ((0, 32),)),
        "conv_weight": noise(streams_of[4], (CONV, 2 * KEYS + VALS), 0.5, 3.0, (), jnp.float32),
        "w_low": noise(streams_of[5], (D, RANK), D ** -0.5, 0.1875),
        "w_high": noise(streams_of[6], (RANK, KEYS), RANK ** -0.5, 1.5, (), jnp.float32),
        "gate_bias": jnp.clip(jax.random.uniform(streams_of[7], (KEYS,), jnp.float32, 0.0, 6.0), 0.0, 6.0),
        "head_gain": jnp.clip(1.0 + 0.1 * jax.random.normal(streams_of[8], (DV,), jnp.float32), 0.5, 1.5),
        "w_out": noise(streams_of[9], (VALS, D), (VALS // 4) ** -0.5, 0.375, ((0, 32),)),
        "ffn_gain": jnp.clip(1.0 + 0.1 * jax.random.normal(streams_of[10], (D,), jnp.float32), 0.5, 1.5),
        "w_gate_up": noise(streams_of[11], (D, 2 * FF), D ** -0.5, 0.1875, ((0, 32),)),
        "w_down": noise(streams_of[12], (FF, D), (FF // 8) ** -0.5, 0.3125, ((0, 32),)),
        "out_grad": noise(streams_of[13], (SEQS, LEN, D), 1.0, 6.0, ((1, 32),)),
    }


@jax.custom_vjp
def low(v):
    return lax.optimization_barrier(v.astype(jnp.bfloat16)).astype(jnp.float32)

@jax.custom_vjp
def low_back(v):
    return v

def low_keep(v):
    return (low(v), None)

def low_pass(kept, grad):
    return (grad,)

def back_keep(v):
    return (v, None)

def back_low(kept, grad):
    return (low(grad),)
low.defvjp(low_keep, low_pass)
low_back.defvjp(back_keep, back_low)
epsilon = 1e-06
gate_scale = 16.0
highest = lax.Precision.HIGHEST

def product(left, right):
    return jnp.dot(left, right, precision=highest, preferred_element_type=jnp.float32)

def segment_step(memory, inputs_piece):
    query_vecs, key_vecs, value_vecs, log_decay, starts, position = inputs_piece
    first_pos = position[0]
    cumulative = jnp.cumsum(log_decay, axis=0)
    query_decayed = query_vecs * jnp.exp(cumulative)
    key_decayed = key_vecs * jnp.exp(-cumulative)
    scores = jnp.einsum('thc,uhc->htu', query_decayed, key_decayed, precision=highest)
    allowed = (position[None, :] <= position[:, None]) & (position[None, :] >= starts[:, None])
    scores = jnp.where(allowed[None, :, :], scores, 0.0)
    within = jnp.einsum('htu,uhv->thv', scores, value_vecs, precision=highest)
    carried = (starts < first_pos).astype(jnp.float32)
    across = jnp.einsum('thc,hcv->thv', query_decayed, memory, precision=highest) * carried[:, None, None]
    decay_total = cumulative[-1]
    kept_state = (starts[-1] < first_pos).astype(jnp.float32)
    same_doc = (position >= starts[-1]).astype(jnp.float32)
    key_final = key_vecs * jnp.exp(decay_total[None, :, :] - cumulative) * same_doc[:, None, None]
    updated = memory * (jnp.exp(decay_total) * kept_state)[:, :, None] + jnp.einsum('uhc,uhv->hcv', key_final, value_vecs, precision=highest)
    return (updated, within + across)

def recurrence(query_vecs, key_vecs, value_vecs, log_decay, starts, position, memory, step_function):
    span_count = starts.shape[1] // SPAN

    def per_sequence(query_seq, key_seq, value_seq, decay_seq, start_seq, memory_seq):

        def split_spans(source):
            return source.reshape((span_count, SPAN) + source.shape[1:])
        final_memory, outputs = lax.scan(step_function, memory_seq, (split_spans(query_seq), split_spans(key_seq), split_spans(value_seq), split_spans(decay_seq), split_spans(start_seq), split_spans(position)))
        return (outputs.reshape((span_count * SPAN,) + outputs.shape[2:]), final_memory)
    return jax.vmap(per_sequence)(query_vecs, key_vecs, value_vecs, log_decay, starts, memory)

def layer_sequence(inputs, starts, params):
    norm_gain, w_in, conv_weight, w_low, w_high, gate_bias, head_gain, w_out, ffn_gain, w_gate_up, w_down = params
    length = inputs.shape[0]
    position = jnp.arange(length, dtype=jnp.int32)
    conv_width = 2 * KEYS + VALS
    inv_rms = lax.rsqrt(lax.optimization_barrier(jnp.mean(inputs * inputs, axis=-1, keepdims=True)) + epsilon)
    normed = low(inputs * inv_rms * norm_gain)
    projected = low_back(low(product(normed, w_in)))
    lowrank = low_back(product(normed, w_low))
    log_decay = jax.nn.log_sigmoid(product(lowrank, w_high) + gate_bias) / gate_scale
    mixed = projected[:, :conv_width]
    convolved = conv_weight[0] * mixed
    for tap_index in range(1, CONV):
        earlier = jnp.concatenate([jnp.zeros((tap_index, conv_width), jnp.float32), mixed[:-tap_index]], axis=0)
        usable = (position - tap_index >= starts).astype(jnp.float32)[:, None]
        convolved = convolved + conv_weight[tap_index] * earlier * usable
    activated = jax.nn.silu(convolved)
    query_vecs = activated[:, :KEYS] * DK ** (-0.5)
    key_vecs = activated[:, KEYS:2 * KEYS]
    value_vecs = activated[:, 2 * KEYS:]
    memory = jnp.zeros((1, HEADS, DK, DV), jnp.float32)
    mixer_out, _ = recurrence(query_vecs.reshape(1, length, HEADS, DK), key_vecs.reshape(1, length, HEADS, DK), value_vecs.reshape(1, length, HEADS, DV), log_decay.reshape(1, length, HEADS, DK), starts[None], position, memory, jax.checkpoint(segment_step))
    mixer_out = mixer_out[0]
    head_rms = lax.rsqrt(lax.optimization_barrier(jnp.mean(mixer_out * mixer_out, axis=-1, keepdims=True)) + epsilon)
    gate_vals = projected[:, conv_width:].reshape(length, HEADS, DV)
    gated = mixer_out * head_rms * head_gain * jax.nn.silu(gate_vals)
    gated = low(gated.reshape(length, VALS))
    hidden_one = inputs + low_back(product(gated, w_out))
    ffn_rms = lax.rsqrt(lax.optimization_barrier(jnp.mean(hidden_one * hidden_one, axis=-1, keepdims=True)) + epsilon)
    ffn_in = low(hidden_one * ffn_rms * ffn_gain)
    gate_up = low_back(product(ffn_in, w_gate_up))
    activation = low(jax.nn.silu(gate_up[:, :FF]) * gate_up[:, FF:])
    return hidden_one + low_back(product(activation, w_down))

def reference(inputs, doc_start, norm_gain, w_in, conv_weight, w_low, w_high, gate_bias, head_gain, w_out, ffn_gain, w_gate_up, w_down, out_grad):
    params = tuple((tensor.astype(jnp.float32) for tensor in (norm_gain, w_in, conv_weight, w_low, w_high, gate_bias, head_gain, w_out, ffn_gain, w_gate_up, w_down)))

    def forward(layer_in, weights):

        def one_sequence(scan_carry, seq_item):
            seq_in, seq_starts = seq_item
            return (scan_carry, jax.checkpoint(layer_sequence)(seq_in, seq_starts, weights))
        _, outputs = lax.scan(one_sequence, jnp.zeros((), jnp.float32), (layer_in, doc_start))
        return outputs
    layer_out, pullback = jax.vjp(forward, inputs.astype(jnp.float32), params)
    input_grad, weight_grads = pullback(out_grad.astype(jnp.float32))
    return (layer_out, input_grad, weight_grads[0], weight_grads[1], weight_grads[2], weight_grads[3], weight_grads[4], weight_grads[5], weight_grads[6], weight_grads[7], weight_grads[8], weight_grads[9], weight_grads[10])
```

```python
import jax
import jax.numpy as jnp
from jax import lax
from jax.sharding import PartitionSpec as P

HEADS = 4
DK = 128
DV = 256
FF = 2816
SPAN = 64
CONV = 4


epsilon = 1e-06
gate_scale = 16.0
highest = lax.Precision.HIGHEST


GROUP = 8
HALO = 8


def chip_axes():
    count = lax.axis_size("seq")
    sides = {16: (4, 2, 2), 64: (4, 4, 4)}.get(count // 2, (count // 2, 1, 1))
    return (
        (sides[0], 2 * sides[1] * sides[2]),
        (sides[1], 2 * sides[2]),
        (sides[2], 2),
        (2, 1),
    )


def moved(array, size, stride, by):
    count = lax.axis_size("seq")
    pairs = [(i, i + by * stride) for i in range(count) if 0 <= (i // stride) % size + by < size]
    return lax.ppermute(array, "seq", pairs)


def swapped(array, mask):
    count = lax.axis_size("seq")
    return lax.ppermute(array, "seq", [(i, i ^ mask) for i in range(count)])


def shifted(array, by):
    count = lax.axis_size("seq")
    pairs = [(i, i + by) for i in range(count) if 0 <= i + by < count]
    return lax.ppermute(array, "seq", pairs)


def line_gather(block, size, stride, at):
    mine = (lax.axis_index("seq") // stride) % size
    if size == 2:
        other = swapped(block, stride)
        first = jnp.where(mine == 0, block, other)
        second = jnp.where(mine == 0, other, block)
        return jnp.stack([first, second], axis=at)
    below, above = [block], [block]
    for _ in range(size - 1):
        below.append(moved(below[-1], size, stride, 1))
        above.append(moved(above[-1], size, stride, -1))
    row = jnp.stack(below[:0:-1] + above, axis=at)
    return lax.dynamic_slice_in_dim(row, size - 1 - mine, size, axis=at)


def gather_rows(shard, order):
    axes, done, block = chip_axes(), [], shard
    for which in order + (3,):
        size, stride = axes[which]
        if size > 1:
            block = line_gather(block, size, stride, sum(1 for d in done if d < which))
            done.append(which)
    return block.reshape(-1, shard.shape[-1])


def line_reduce(block, size, stride, at):
    mine = (lax.axis_index("seq") // stride) % size

    def pick(index):
        return lax.dynamic_index_in_dim(block, index, at, False).astype(jnp.float32)

    if size == 2:
        return pick(mine) + swapped(pick(1 - mine).astype(jnp.bfloat16), stride).astype(jnp.float32)
    up = down = None
    for step in range(1, size):
        reach = size - step
        to_up = pick(jnp.minimum(mine + reach, size - 1))
        to_down = pick(jnp.maximum(mine - reach, 0))
        if step > 1:
            to_up, to_down = to_up + up, to_down + down
        up = moved(to_up.astype(jnp.bfloat16), size, stride, 1).astype(jnp.float32)
        down = moved(to_down.astype(jnp.bfloat16), size, stride, -1).astype(jnp.float32)
    return pick(mine) + up + down


def reduce_rows(full, order):
    axes = chip_axes()
    left = [which for which in range(4) if axes[which][0] > 1]
    block = full.reshape(tuple(axes[which][0] for which in left) + (-1, full.shape[-1]))
    for which in (3,) + order:
        size, stride = axes[which]
        if size > 1:
            block = line_reduce(block, size, stride, left.index(which))
            left.remove(which)
    return block


def small_sum(value):
    axes = chip_axes()
    for size, stride in axes[::-1]:
        if size == 2:
            value = value + swapped(value, stride)
        elif size > 1:
            total = value
            for by in range(1, size):
                total = total + moved(value, size, stride, by) + moved(value, size, stride, -by)
            value = total
    return value


def to_owners(pieces):
    mine = lax.axis_index("seq") % GROUP
    got = [lax.dynamic_index_in_dim(pieces, mine, 0, False)]
    for mask in range(1, GROUP):
        got.append(swapped(lax.dynamic_index_in_dim(pieces, mine ^ mask, 0, False), mask))
    got = jnp.stack(got)
    return [
        lax.dynamic_index_in_dim(got, mine ^ index, 0, False).astype(jnp.float32)
        for index in range(GROUP)
    ]


def packed(decay, state):
    decay = decay.reshape(GROUP, 1, DK)
    high = decay.astype(jnp.bfloat16)
    low = (decay - high.astype(jnp.float32)).astype(jnp.bfloat16)
    return jnp.concatenate(
        [
            state.reshape(GROUP, DK, DV).astype(jnp.bfloat16),
            jnp.pad(jnp.concatenate([high, low], axis=-1), ((0, 0), (0, 15), (0, 0))),
        ],
        axis=1,
    )


def carried_over(decay, state, backward):
    got = to_owners(packed(decay, state))
    order = range(GROUP)[::-1] if backward else range(GROUP)
    running = jnp.zeros((DK, DV), jnp.float32)
    reach = jnp.ones((DK, 1), jnp.float32)
    before = [None] * GROUP
    for index in order:
        before[index] = (running, reach)
        kept = (got[index][DK, :DK] + got[index][DK, DK:])[:, None]
        running = kept * running + got[index][:DK]
        reach = reach * kept
    beyond = shifted(running.astype(jnp.bfloat16), -GROUP if backward else GROUP)
    beyond = beyond.astype(jnp.float32)
    result = jnp.stack([(part + far * beyond).astype(jnp.bfloat16) for part, far in before])
    return jnp.stack(to_owners(result)).reshape(state.shape)


def segment_step(memory, inputs_piece):
    query_vecs, key_vecs, value_vecs, log_decay, starts, position = inputs_piece
    first_pos = position[0]
    cumulative = jnp.cumsum(log_decay, axis=0)
    query_decayed = query_vecs * jnp.exp(cumulative)
    key_decayed = key_vecs * jnp.exp(-cumulative)
    scores = jnp.einsum("thc,uhc->htu", query_decayed, key_decayed, precision=highest)
    allowed = (position[None, :] <= position[:, None]) & (position[None, :] >= starts[:, None])
    scores = jnp.where(allowed[None, :, :], scores, 0.0)
    within = jnp.einsum("htu,uhv->thv", scores, value_vecs, precision=highest)
    carried = (starts < first_pos).astype(jnp.float32)
    across = (
        jnp.einsum("thc,hcv->thv", query_decayed, memory, precision=highest)
        * carried[:, None, None]
    )
    decay_total = cumulative[-1]
    kept_state = (starts[-1] < first_pos).astype(jnp.float32)
    same_doc = (position >= starts[-1]).astype(jnp.float32)
    key_final = key_vecs * jnp.exp(decay_total[None, :, :] - cumulative) * same_doc[:, None, None]
    updated = memory * (jnp.exp(decay_total) * kept_state)[:, :, None] + jnp.einsum(
        "uhc,uhv->hcv", key_final, value_vecs, precision=highest
    )
    return (updated, within + across)


def recurrence(
    query_vecs, key_vecs, value_vecs, log_decay, starts, position, memory, step_function
):
    span_count = starts.shape[1] // SPAN

    def per_sequence(query_seq, key_seq, value_seq, decay_seq, start_seq, memory_seq):

        def split_spans(source):
            return source.reshape((span_count, SPAN) + source.shape[1:])

        final_memory, outputs = lax.scan(
            step_function,
            memory_seq,
            (
                split_spans(query_seq),
                split_spans(key_seq),
                split_spans(value_seq),
                split_spans(decay_seq),
                split_spans(start_seq),
                split_spans(position),
            ),
        )
        return (outputs.reshape((span_count * SPAN,) + outputs.shape[2:]), final_memory)

    return jax.vmap(per_sequence)(query_vecs, key_vecs, value_vecs, log_decay, starts, memory)


def bf_dot(left, right):
    return jnp.dot(left, right, preferred_element_type=jnp.float32)


def rms_back(grad_normed, source, inv_rms, gain_vec):
    scaled = grad_normed * gain_vec
    return inv_rms * (
        scaled - source * inv_rms * inv_rms * jnp.mean(scaled * source, axis=-1, keepdims=True)
    )


def local(
    inputs,
    doc_start,
    norm_gain,
    w_in,
    conv_weight,
    w_low,
    w_high,
    gate_bias,
    head_gain,
    w_out,
    ffn_gain,
    w_gate_up,
    w_down,
    out_grad,
):
    seq_count, block_len, model_width = inputs.shape
    row_count = seq_count * block_len
    key_width = HEADS * DK
    value_width = HEADS * DV
    conv_width = 2 * key_width + value_width
    block_start = lax.axis_index("seq") * block_len
    position = block_start + jnp.arange(block_len, dtype=jnp.int32)
    zyx, zxy, xyz, yzx = (0, 1, 2), (0, 2, 1), (2, 1, 0), (1, 0, 2)
    qk_full = gather_rows(w_in[:, : 2 * key_width], zxy)
    v_full = gather_rows(w_in[:, 2 * key_width : conv_width], xyz)
    g_full = gather_rows(w_in[:, conv_width:], yzx)
    edge = shifted(inputs[:, block_len - HALO :, :], 1)
    wide = jnp.concatenate([edge, inputs], axis=1).astype(jnp.float32)
    wide_rms = lax.rsqrt(jnp.mean(wide * wide, axis=-1, keepdims=True) + epsilon)
    wide_normed = (wide * wide_rms * norm_gain).astype(jnp.bfloat16)
    layer_in = wide[:, HALO:].reshape(row_count, model_width)
    inv_rms = wide_rms[:, HALO:].reshape(row_count, 1)
    normed = wide_normed[:, HALO:].reshape(row_count, model_width)
    wide_rows = wide_normed.reshape(-1, model_width)
    wide_mixed = jnp.concatenate([bf_dot(wide_rows, qk_full), bf_dot(wide_rows, v_full)], axis=1)
    wide_mixed = wide_mixed.astype(jnp.bfloat16).reshape(seq_count, HALO + block_len, conv_width)
    gate_cols = bf_dot(normed, g_full).astype(jnp.bfloat16)
    out_full = gather_rows(w_out, zyx)
    gate_full = gather_rows(w_gate_up[:, :FF], zxy)
    up_full = gather_rows(w_gate_up[:, FF:], zyx)
    half = model_width // 2
    down_left = gather_rows(w_down[:, :half], zxy)
    down_right = gather_rows(w_down[:, half:], zyx)
    lowrank = bf_dot(normed, w_low)
    gate_logit = (
        jnp.dot(lowrank, w_high, precision=highest, preferred_element_type=jnp.float32) + gate_bias
    )
    log_decay = jax.nn.log_sigmoid(gate_logit) / gate_scale
    padded = wide_mixed[:, HALO - (CONV - 1) :].astype(jnp.float32)
    usables = [
        (position[None, :] - tap_index >= doc_start).astype(jnp.float32)[:, :, None]
        for tap_index in range(CONV)
    ]
    convolved = conv_weight[0] * padded[:, CONV - 1 :, :]
    for tap_index in range(1, CONV):
        offset = CONV - 1 - tap_index
        convolved = (
            convolved
            + conv_weight[tap_index]
            * padded[:, offset : offset + block_len, :]
            * usables[tap_index]
        )
    conv_sig = jax.nn.sigmoid(convolved)
    activated = convolved * conv_sig
    query_vecs = (activated[..., :key_width] * DK ** (-0.5)).reshape(
        seq_count, block_len, HEADS, DK
    )
    key_vecs = activated[..., key_width : 2 * key_width].reshape(seq_count, block_len, HEADS, DK)
    value_vecs = activated[..., 2 * key_width :].reshape(seq_count, block_len, HEADS, DV)
    decay_rows = log_decay.reshape(seq_count, block_len, HEADS, DK)
    zero_memory = jnp.zeros((seq_count, HEADS, DK, DV), jnp.float32)
    local_out, local_state = recurrence(
        query_vecs, key_vecs, value_vecs, decay_rows, doc_start, position, zero_memory, segment_step
    )
    cumulative = jnp.cumsum(decay_rows, axis=1)
    reach_in = (doc_start < block_start).astype(jnp.float32)
    block_decay = jnp.exp(cumulative[:, -1]) * reach_in[:, -1][:, None, None]
    incoming = carried_over(block_decay, local_state, False)
    query_reach = query_vecs * jnp.exp(cumulative) * reach_in[:, :, None, None]
    mixer_out = local_out + jnp.einsum("sbhc,shcv->sbhv", query_reach, incoming, precision=highest)
    mixer_rows = mixer_out.reshape(row_count, HEADS, DV)
    head_rms = lax.rsqrt(jnp.mean(mixer_rows * mixer_rows, axis=-1, keepdims=True) + epsilon)
    head_normed = mixer_rows * head_rms * head_gain
    gate_vals = gate_cols.astype(jnp.float32).reshape(row_count, HEADS, DV)
    gate_sig = jax.nn.sigmoid(gate_vals)
    swish = gate_vals * gate_sig
    gated = (head_normed * swish).reshape(row_count, value_width).astype(jnp.bfloat16)
    hidden_one = layer_in + bf_dot(gated, out_full)
    ffn_rms = lax.rsqrt(jnp.mean(hidden_one * hidden_one, axis=-1, keepdims=True) + epsilon)
    ffn_in = (hidden_one * ffn_rms * ffn_gain).astype(jnp.bfloat16)
    gate_part = bf_dot(ffn_in, gate_full)
    up_part = bf_dot(ffn_in, up_full)
    gate_act = jax.nn.sigmoid(gate_part)
    activation = (gate_part * gate_act * up_part).astype(jnp.bfloat16)
    layer_out = hidden_one + jnp.concatenate(
        [bf_dot(activation, down_left), bf_dot(activation, down_right)], axis=1
    )
    out_rows = out_grad.reshape(row_count, model_width).astype(jnp.float32)
    out_rows_low = out_rows.astype(jnp.bfloat16)
    act_grad = bf_dot(out_rows_low[:, :half], down_left.T) + bf_dot(
        out_rows_low[:, half:], down_right.T
    )
    gate_grad = act_grad * up_part * gate_act * (1.0 + gate_part * (1.0 - gate_act))
    up_grad = act_grad * gate_part * gate_act
    gate_grad, up_grad = gate_grad.astype(jnp.bfloat16), up_grad.astype(jnp.bfloat16)

    def term(left, right):
        return jnp.dot(left.T, right, preferred_element_type=jnp.float32).astype(jnp.bfloat16)

    w_gate_up_grad = jnp.concatenate(
        [reduce_rows(term(ffn_in, gate_grad), (2, 1, 0)), reduce_rows(term(ffn_in, up_grad), (1, 2, 0))],
        axis=1,
    )
    w_down_grad = jnp.concatenate(
        [
            reduce_rows(term(activation, out_rows_low[:, :half]), (2, 1, 0)),
            reduce_rows(term(activation, out_rows_low[:, half:]), (1, 2, 0)),
        ],
        axis=1,
    )
    ffn_in_grad = bf_dot(gate_grad, gate_full.T) + bf_dot(up_grad, up_full.T)
    ffn_gain_grad = jnp.sum(ffn_in_grad * hidden_one * ffn_rms, axis=0)
    hidden_grad = out_rows + rms_back(ffn_in_grad, hidden_one, ffn_rms, ffn_gain)
    hidden_low = hidden_grad.astype(jnp.bfloat16)
    w_out_grad = reduce_rows(term(gated, hidden_low), (2, 1, 0))
    gated_grad = bf_dot(hidden_low, out_full.T).reshape(row_count, HEADS, DV)
    head_normed_grad = gated_grad * swish
    gate_vals_grad = gated_grad * head_normed * gate_sig * (1.0 + gate_vals * (1.0 - gate_sig))
    head_gain_grad = jnp.sum(head_normed_grad * mixer_rows * head_rms, axis=(0, 1))
    mixer_grad = rms_back(head_normed_grad, mixer_rows, head_rms, head_gain).reshape(
        seq_count, block_len, HEADS, DV
    )
    state_term = jnp.einsum("sbhc,sbhv->shcv", query_reach, mixer_grad, precision=highest)
    outgoing = carried_over(block_decay, state_term, True)

    def local_block(query_in, key_in, value_in, decay_in, memory_in):
        return recurrence(
            query_in, key_in, value_in, decay_in, doc_start, position, memory_in, segment_step
        )

    _, block_pullback = jax.vjp(local_block, query_vecs, key_vecs, value_vecs, decay_rows, incoming)
    query_grad, key_grad, value_grad, decay_grad, _ = block_pullback((mixer_grad, outgoing))
    act_in_grad = jnp.concatenate(
        [
            query_grad.reshape(seq_count, block_len, key_width) * DK ** (-0.5),
            key_grad.reshape(seq_count, block_len, key_width),
            value_grad.reshape(seq_count, block_len, value_width),
        ],
        axis=-1,
    )
    conv_pre_grad = act_in_grad * conv_sig * (1.0 + convolved * (1.0 - conv_sig))
    padded_grad = jnp.zeros_like(padded)
    tap_grads = []
    for tap_index in range(CONV):
        offset = CONV - 1 - tap_index
        masked = conv_pre_grad * usables[tap_index]
        tap_grads.append(jnp.sum(masked * padded[:, offset : offset + block_len, :], axis=(0, 1)))
        padded_grad = padded_grad + jnp.pad(
            masked * conv_weight[tap_index], ((0, 0), (offset, CONV - 1 - offset), (0, 0))
        )
    conv_weight_grad = jnp.stack(tap_grads, axis=0)
    back_edge = shifted(padded_grad[:, : CONV - 1, :].astype(jnp.bfloat16), -1).astype(
        jnp.float32
    )
    mixed_grad = padded_grad[:, CONV - 1 :, :] + jnp.pad(
        back_edge, ((0, 0), (block_len - (CONV - 1), 0), (0, 0))
    )
    mixed_grad = mixed_grad.reshape(row_count, conv_width).astype(jnp.bfloat16)
    gate_vals_grad = gate_vals_grad.reshape(row_count, value_width).astype(jnp.bfloat16)
    qk_grad, v_grad = mixed_grad[:, : 2 * key_width], mixed_grad[:, 2 * key_width :]
    w_in_grad = jnp.concatenate(
        [
            reduce_rows(term(normed, qk_grad), (1, 2, 0)),
            reduce_rows(term(normed, v_grad), (0, 1, 2)),
            reduce_rows(term(normed, gate_vals_grad), (2, 0, 1)),
        ],
        axis=1,
    )
    logit_grad = decay_grad.reshape(row_count, key_width) / gate_scale * jax.nn.sigmoid(-gate_logit)
    gate_bias_grad = jnp.sum(logit_grad, axis=0)
    w_high_grad = jnp.dot(
        lowrank.T, logit_grad, precision=highest, preferred_element_type=jnp.float32
    )
    lowrank_grad = jnp.dot(
        logit_grad, w_high.T, precision=highest, preferred_element_type=jnp.float32
    ).astype(jnp.bfloat16)
    w_low_grad = jnp.dot(normed.T, lowrank_grad, preferred_element_type=jnp.float32)
    normed_grad = (
        bf_dot(qk_grad, qk_full.T)
        + bf_dot(v_grad, v_full.T)
        + bf_dot(gate_vals_grad, g_full.T)
        + bf_dot(lowrank_grad, w_low.T)
    )
    norm_gain_grad = jnp.sum(normed_grad * layer_in * inv_rms, axis=0)
    input_grad = hidden_grad + rms_back(normed_grad, layer_in, inv_rms, norm_gain)
    small = (
        norm_gain_grad,
        conv_weight_grad,
        w_low_grad,
        w_high_grad,
        gate_bias_grad,
        head_gain_grad,
        ffn_gain_grad,
    )
    summed = small_sum(jnp.concatenate([part.reshape(-1, 128) for part in small]))
    small_grads, start = [], 0
    for part in small:
        rows = part.size // 128
        small_grads.append(summed[start : start + rows].reshape(part.shape))
        start += rows
    return (
        layer_out.reshape(seq_count, block_len, model_width),
        input_grad.reshape(seq_count, block_len, model_width),
        small_grads[0],
        w_in_grad,
        small_grads[1],
        small_grads[2],
        small_grads[3],
        small_grads[4],
        small_grads[5],
        w_out_grad,
        small_grads[6],
        w_gate_up_grad,
        w_down_grad,
    )


def solution(mesh):
    placed = (
        P(None, "seq", None),
        P(None, "seq"),
        P(),
        P("seq", None),
        P(),
        P(),
        P(),
        P(),
        P(),
        P("seq", None),
        P(),
        P("seq", None),
        P("seq", None),
        P(None, "seq", None),
    )
    return jax.shard_map(
        local,
        mesh=mesh,
        in_specs=placed,
        out_specs=(
            P(None, "seq", None),
            P(None, "seq", None),
            P(),
            P("seq", None),
            P(),
            P(),
            P(),
            P(),
            P(),
            P("seq", None),
            P(),
            P("seq", None),
            P("seq", None),
        ),
        check_vma=False,
    )
```

```python
import jax
import jax.numpy as jnp
from jax import lax
from jax.experimental import pallas as pl
from jax.experimental.pallas import tpu as pltpu
from jax.sharding import PartitionSpec as P

HEADS = 4
DK = 128
DV = 256
FF = 2816
WIDE = 128
CONV = 4


epsilon = 1e-06
gate_scale = 16.0
highest = lax.Precision.HIGHEST


GROUP = 8
HALO = 8
EXTRA = 16


def chip_axes():
    count = lax.axis_size("seq")
    sides = {16: (4, 2, 2), 64: (4, 4, 4)}.get(count // 2, (count // 2, 1, 1))
    return (
        (sides[0], 2 * sides[1] * sides[2]),
        (sides[1], 2 * sides[2]),
        (sides[2], 2),
        (2, 1),
    )


def swapped(array, mask):
    count = lax.axis_size("seq")
    return lax.ppermute(array, "seq", [(i, i ^ mask) for i in range(count)])


def shifted(array, by):
    count = lax.axis_size("seq")
    pairs = [(i, i + by) for i in range(count) if 0 <= i + by < count]
    return lax.ppermute(array, "seq", pairs)


def spread(block, axis):
    size, stride = axis
    return [block] + [swapped(block, step * stride) for step in range(1, size)]


def takes(micros):
    return pl.CostEstimate(flops=int(micros * 1e9), bytes_accessed=0, transcendentals=0)


def coordinates():
    mine = lax.axis_index("seq")
    return jnp.stack([(mine // stride) % size for size, stride in chip_axes()]).astype(jnp.int32)


def placed_blocks(pieces, one, two, cuts):
    axes = chip_axes()
    sizes = tuple(size for size, _ in axes)
    depth, sides, mine = sizes[0], sizes[one], coordinates()
    rows, columns = pieces[0].shape[2:]

    def target(step, side, me):
        spot = [0, 0, 0, 0]
        spot[one] = jnp.bitwise_xor(side, me[one])
        spot[two] = jnp.bitwise_xor(step // sizes[3], me[two])
        spot[3] = jnp.bitwise_xor(step % sizes[3], me[3])
        return tuple(spot) + (0, 0)

    def source(which):
        def index(step, side, me):
            before = jnp.where(step < which, 0, sides - 1)
            return (jnp.where(step == which, side, before), 0, 0, 0)

        return index

    def kernel(me, *refs):
        sources, outs = refs[: len(pieces)], refs[len(pieces) :]
        step = pl.program_id(0)
        for which, piece in enumerate(sources):

            @pl.when(step == which)
            def _():
                for level in range(depth):
                    block, start = piece[0, level], 0
                    for out, cut in zip(outs, cuts):
                        out[jnp.bitwise_xor(me[0], level), 0, 0, 0] = block[start : start + cut]
                        start += cut

    found = pl.pallas_call(
        kernel,
        out_shape=[jax.ShapeDtypeStruct(sizes + (cut, columns), pieces[0].dtype) for cut in cuts],
        grid_spec=pltpu.PrefetchScalarGridSpec(
            num_scalar_prefetch=1,
            grid=(len(pieces), sides),
            in_specs=[
                pl.BlockSpec((1, depth, rows, columns), source(which))
                for which in range(len(pieces))
            ],
            out_specs=[pl.BlockSpec((depth, 1, 1, 1, cut, columns), target) for cut in cuts],
        ),
        compiler_params=pltpu.CompilerParams(vmem_limit_bytes=40 * 2**20),
        cost_estimate=takes(1.0 + rows * columns * 5e-5),
    )(mine, *pieces)
    return [array.reshape(-1, columns) for array in found]


def together(*values):
    return lax.optimization_barrier(values)


def gather_all(groups):
    axis_z, axis_y, axis_x, axis_c = chip_axes()
    near = []
    for shards in groups:
        shard = jnp.concatenate(shards, axis=0) if len(shards) > 1 else shards[0]
        if near:
            shard, near[-1][1] = together(shard, near[-1][1])
        near.append(spread(shard, axis_z))
    crossed, gathered = None, []
    for pieces in near:
        if crossed is not None:
            pieces, crossed = together(pieces, crossed)
            gathered.append(crossed)
        half = pieces[0].shape[1] // 2
        stacked = jnp.stack(pieces)
        sides = [
            jnp.stack(spread(stacked[..., :half], axis_x)),
            jnp.stack(spread(stacked[..., half:], axis_y)),
        ]
        crossed = [spread(sides[0], axis_y), spread(sides[1], axis_x)]
    gathered.append(crossed)
    full = []
    for shards, crossed in zip(groups, gathered):
        cuts, halves = [shard.shape[0] for shard in shards], []
        for pieces, one, two in zip(crossed, (2, 1), (1, 2)):
            pieces = [copy for piece in pieces for copy in spread(piece, axis_c)]
            halves.append(placed_blocks(pieces, one, two, cuts))
        full.extend(zip(*halves))
    return full


def grad_products(left, right_a, right_b):
    sizes = tuple(size for size, _ in chip_axes())
    strides = tuple(stride for _, stride in chip_axes())
    (tokens, features), columns = left.shape, right_a.shape[1]
    count, mine = lax.axis_size("seq"), coordinates()
    rows = features // count
    tile = 512 if columns % 512 == 0 and features <= 1024 else 256
    chunks = next(c for c in (4, 2, 1) if features // c % 128 == 0)
    chunk = features // chunks

    def kernel(me, left_ref, a_ref, b_ref, away_a, keep_a, away_b, keep_b, flipped):
        @pl.when(pl.program_id(0) == 0)
        def _():
            flipped[...] = left_ref[...].T

        even = me[3] == 0
        for right, away, keep, order in (
            (a_ref, away_a, keep_a, (2, 1, 0)),
            (b_ref, away_b, keep_b, (1, 2, 0)),
        ):
            for part in range(chunks):
                full = jnp.dot(
                    flipped[part * chunk : (part + 1) * chunk],
                    right[...],
                    preferred_element_type=jnp.float32,
                )
                for start in range(0, chunk, 2 * rows):
                    device = (part * chunk + start) // rows
                    spot = tuple(
                        jnp.bitwise_xor(device // strides[axis] % sizes[axis], me[axis])
                        for axis in order
                    )
                    low = full[start : start + rows]
                    high = full[start + rows : start + 2 * rows]
                    away[spot] = jnp.where(even, high, low).astype(jnp.bfloat16)
                    keep[spot] = jnp.where(even, low, high).astype(jnp.bfloat16)

    def result(one, two):
        shape = (sizes[one], sizes[two], sizes[0], rows)
        return (
            jax.ShapeDtypeStruct(shape + (columns,), jnp.bfloat16),
            pl.BlockSpec(shape + (tile,), lambda i, me: (0, 0, 0, 0, i)),
        )

    results = [result(2, 1), result(2, 1), result(1, 2), result(1, 2)]
    right_spec = pl.BlockSpec((tokens, tile), lambda i, me: (0, i))
    return pl.pallas_call(
        kernel,
        out_shape=[shape for shape, _ in results],
        grid_spec=pltpu.PrefetchScalarGridSpec(
            num_scalar_prefetch=1,
            grid=(columns // tile,),
            in_specs=[
                pl.BlockSpec((tokens, features), lambda i, me: (0, 0)),
                right_spec,
                right_spec,
            ],
            out_specs=[spec for _, spec in results],
            scratch_shapes=[pltpu.VMEM((features, tokens), jnp.bfloat16)],
        ),
        compiler_params=pltpu.CompilerParams(vmem_limit_bytes=48 * 2**20),
        cost_estimate=takes(1.5 + features * columns * 4.5e-6),
    )(mine, left, right_a, right_b)


def fold(block, axis):
    total = block[0].astype(jnp.float32)
    for step in range(1, axis[0]):
        part = swapped(block[step].astype(jnp.bfloat16), step * axis[1])
        total = total + part.astype(jnp.float32)
    return total


def cores_summed(left, right_a, right_b):
    away_a, keep_a, away_b, keep_b = grad_products(left, right_a, right_b)
    return [keep_a, swapped(away_a, 1), keep_b, swapped(away_b, 1)]


def sides_summed(products):
    axes = chip_axes()
    products = [[piece.astype(jnp.float32) for piece in pieces] for pieces in products]
    end_a = jnp.concatenate([pieces[0] + pieces[1] for pieces in products], axis=3)
    end_b = jnp.concatenate([pieces[2] + pieces[3] for pieces in products], axis=3)
    ends = [fold(end_a, axes[2]), fold(end_b, axes[1])]
    return [fold(ends[0], axes[1]), fold(ends[1], axes[2])]


def levels_summed(ends):
    return fold(jnp.concatenate(ends, axis=-1), chip_axes()[0])


def small_sum(value):
    for axis in chip_axes()[::-1]:
        value = sum(spread(value, axis))
    return value


def exchanged(pieces):
    shape = pieces.shape
    pieces = pieces.reshape((2, 2, 2) + shape[1:])
    kept, sent = pieces[:, :, 0], pieces[:, :, 1]
    pieces = jnp.stack([kept, swapped(sent, 1)], axis=2)
    kept, sent = pieces[:, 0], pieces[:, 1]
    pieces = jnp.stack([kept, swapped(sent, 2)], axis=1)
    return jnp.stack([pieces[0], swapped(pieces[1], 4)]).reshape(shape)


def column(row):
    square = jnp.broadcast_to(row, (DK, DK)).T
    return jnp.concatenate([square, square], axis=1)


def packed_rows(state, decay):
    high = decay.astype(jnp.bfloat16)
    low = (decay - high.astype(jnp.float32)).astype(jnp.bfloat16)
    tail = jnp.broadcast_to(jnp.concatenate([high, low], axis=1), (EXTRA, DV))
    return jnp.concatenate([state.astype(jnp.bfloat16), tail], axis=0)


def composed(place, got, backward, beyond=None):
    order = range(GROUP)[::-1] if backward else range(GROUP)

    def kernel(place_ref, got_ref, *refs):
        mine, out = place_ref[1], refs[-1]
        running = jnp.zeros((DK, DV), jnp.float32)
        reach = jnp.ones((DK, DV), jnp.float32)
        far = None if beyond is None else refs[0][...].astype(jnp.float32)
        for index in order:
            spot = jnp.bitwise_xor(mine, index)
            piece = got_ref[spot].astype(jnp.float32)
            if beyond is not None:
                out[spot] = (running + reach * far).astype(jnp.bfloat16)
            tail = piece[DK : DK + 1]
            kept = column(tail[:, :DK] + tail[:, DK:])
            running = kept * running + piece[:DK]
            reach = reach * kept
        if beyond is None:
            out[...] = running.astype(jnp.bfloat16)

    extra = () if beyond is None else (beyond,)
    shape = (DK, DV) if beyond is None else (GROUP, DK, DV)
    return pl.pallas_call(
        kernel,
        out_shape=jax.ShapeDtypeStruct(shape, jnp.bfloat16),
        in_specs=[pl.BlockSpec(memory_space=pltpu.SMEM)]
        + [pl.BlockSpec(memory_space=pltpu.VMEM)] * (1 + len(extra)),
        out_specs=pl.BlockSpec(memory_space=pltpu.VMEM),
        cost_estimate=takes(2),
    )(place, got, *extra)


def carried_over(place, pieces, backward):
    got = exchanged(pieces)
    total = composed(place, got, backward)
    beyond = shifted(total, -GROUP if backward else GROUP)
    return exchanged(composed(place, got, backward, beyond))


def split_dot(left, right, dims):
    dims = (dims, ((), ()))
    left_high, right_high = left.astype(jnp.bfloat16), right.astype(jnp.bfloat16)
    left_low = (left - left_high.astype(jnp.float32)).astype(jnp.bfloat16)
    right_low = (right - right_high.astype(jnp.float32)).astype(jnp.bfloat16)

    def one(a, b):
        return lax.dot_general(a, b, dims, preferred_element_type=jnp.float32)

    return one(left_high, right_high) + (one(left_high, right_low) + one(left_low, right_high))


def unit_dot(unit, value, dims):
    high = value.astype(jnp.bfloat16)
    rest = value - high.astype(jnp.float32)
    middle = rest.astype(jnp.bfloat16)
    low = (rest - middle.astype(jnp.float32)).astype(jnp.bfloat16)
    unit = unit.astype(jnp.bfloat16)
    return sum(
        lax.dot_general(unit, part, (dims, ((), ())), preferred_element_type=jnp.float32)
        for part in (low, middle, high)
    )


NN, NT, TN = ((1,), (0,)), ((1,), (1,)), ((0,), (0,))


def conv_in(piece, taps, pos, starts, block_len):
    wide = piece[0].astype(jnp.float32)
    total = taps[0:1, :] * wide[HALO:]
    for tap in range(1, CONV):
        usable = (pos - tap >= starts).astype(jnp.float32)
        total = total + taps[tap : tap + 1, :] * wide[HALO - tap : HALO - tap + block_len] * usable
    return wide, total


def decays(logit):
    return (jnp.minimum(logit, 0.0) - jnp.log1p(jnp.exp(-jnp.abs(logit)))) / gate_scale


class Span:
    def __init__(self, index, first, query, key, value, decay, starts, pos):
        rows = slice(index * WIDE, (index + 1) * WIDE)
        self.rows, first_pos = rows, first + index * WIDE
        self.query, self.key, self.value = query[rows], key[rows], value[rows]
        decay, starts, pos = decay[rows], starts[rows], pos[rows]
        t = lax.broadcasted_iota(jnp.int32, (WIDE, WIDE), 0)
        u = lax.broadcasted_iota(jnp.int32, (WIDE, WIDE), 1)
        self.lower = (u <= t).astype(jnp.float32)
        self.upper = (u >= t).astype(jnp.float32)
        self.allowed = (u <= t) & (u + first_pos >= starts)
        cum = unit_dot(self.lower, decay, NN)
        self.total = cum[WIDE - 1 :]
        middle = cum[WIDE // 2 - 1 : WIDE // 2]
        self.to_query, self.to_key = jnp.exp(cum - middle), jnp.exp(middle - cum)
        self.carried = (starts < first_pos).astype(jnp.float32)
        self.kept = (starts[WIDE - 1 :] < first_pos).astype(jnp.float32)
        self.from_start = jnp.exp(cum) * self.carried
        self.to_end = jnp.exp(self.total - cum) * (pos >= starts[WIDE - 1 :]).astype(jnp.float32)
        self.query_centred = self.query * self.to_query
        self.key_centred = self.key * self.to_key
        self.query_start = self.query * self.from_start
        self.key_end = self.key * self.to_end
        self.cum = cum
        ones = jnp.ones((WIDE, DV), jnp.float32)
        total_column = unit_dot_right(decay, ones)
        self.keep_column = jnp.exp(total_column) * self.kept

    def scores(self):
        raw = split_dot(self.query_centred, self.key_centred, NT)
        return jnp.where(self.allowed, raw, 0.0)

    def next_state(self, state):
        update = split_dot(self.key_end, self.value, TN)
        return update if state is None else state * self.keep_column + update


def unit_dot_right(value, unit):
    high = value.astype(jnp.bfloat16)
    rest = value - high.astype(jnp.float32)
    middle = rest.astype(jnp.bfloat16)
    low = (rest - middle.astype(jnp.float32)).astype(jnp.bfloat16)
    unit = unit.astype(jnp.bfloat16)
    return sum(
        lax.dot_general(part, unit, (TN, ((), ())), preferred_element_type=jnp.float32)
        for part in (low, middle, high)
    )


def activations(refs, starts, first, block_len):
    pos = first + lax.broadcasted_iota(jnp.int32, (block_len, 1), 0)
    found = []
    for piece, taps in refs:
        wide, total = conv_in(piece, taps, pos, starts, block_len)
        sig = jax.nn.sigmoid(total)
        found.append((wide, total, sig))
    return pos, found


def mixer_specs(block_len):
    wide = HALO + block_len
    return [
        pl.BlockSpec((1, wide, DK), lambda s, h, first: (s, 0, h)),
        pl.BlockSpec((1, wide, DK), lambda s, h, first: (s, 0, HEADS + h)),
        pl.BlockSpec((1, wide, DV), lambda s, h, first: (s, 0, HEADS + h)),
        pl.BlockSpec((CONV, DK), lambda s, h, first: (0, h)),
        pl.BlockSpec((CONV, DK), lambda s, h, first: (0, HEADS + h)),
        pl.BlockSpec((CONV, DV), lambda s, h, first: (0, HEADS + h)),
        pl.BlockSpec((1, block_len, DK), lambda s, h, first: (s, 0, h)),
        pl.BlockSpec((1, block_len, 1), lambda s, h, first: (s, 0, 0)),
    ]


def key_spec(block_len):
    return pl.BlockSpec((1, block_len, DK), lambda s, h, first: (s, 0, h))


def value_spec(block_len):
    return pl.BlockSpec((1, block_len, DV), lambda s, h, first: (s, 0, h))


def pair_spec(rows):
    return pl.BlockSpec(
        (1, rows, DV), lambda s, h, place: (jnp.bitwise_xor(place[1], s * HEADS + h), 0, 0)
    )


decay_spec = pl.BlockSpec((1, 1, 1, DK), lambda s, h, first: (s, h, 0, 0))


def launch(kernel, inputs, in_specs, outputs, out_specs, seq_count, micros):
    return pl.pallas_call(
        kernel,
        out_shape=[jax.ShapeDtypeStruct(shape, kind) for shape, kind in outputs],
        grid_spec=pltpu.PrefetchScalarGridSpec(
            num_scalar_prefetch=1,
            grid=(seq_count, HEADS),
            in_specs=in_specs,
            out_specs=out_specs,
        ),
        compiler_params=pltpu.CompilerParams(vmem_limit_bytes=40 * 2**20),
        cost_estimate=takes(micros),
    )(*inputs)


def mixer_forward(first, wide_mixed, conv_weight, logits, starts):
    seq_count, block_len = starts.shape[:2]

    def kernel(
        first_ref, q_ref, k_ref, v_ref, tq, tk, tv, logit_ref, start_ref, out, reach, state, decay
    ):
        first, starts = first_ref[0], start_ref[0]
        pos, found = activations(
            ((q_ref, tq), (k_ref, tk), (v_ref, tv)), starts, first, block_len
        )
        query, key, value = [total * sig for _, total, sig in found]
        query = query * DK ** (-0.5)
        log_decay = decays(logit_ref[0])
        running = None
        before = jnp.zeros((1, DK), jnp.float32)
        reach_in = (starts < first).astype(jnp.float32)
        for index in range(block_len // WIDE):
            span = Span(index, first, query, key, value, log_decay, starts, pos)
            result = split_dot(span.scores(), span.value, NN)
            if running is not None:
                result = result + split_dot(span.query_start, running, NN)
            out[0, span.rows] = result
            reach[0, span.rows] = span.query * jnp.exp(before + span.cum) * reach_in[span.rows]
            before = before + span.total
            running = span.next_state(running)
        block_decay = jnp.exp(before) * reach_in[block_len - 1 :]
        state[0] = packed_rows(running, block_decay)
        decay[0, 0] = block_decay

    return launch(
        kernel,
        (first, wide_mixed, wide_mixed, wide_mixed)
        + (conv_weight, conv_weight, conv_weight, logits, starts),
        mixer_specs(block_len),
        (
            ((seq_count, block_len, HEADS * DV), jnp.float32),
            ((seq_count, block_len, HEADS * DK), jnp.float32),
            ((GROUP, DK + EXTRA, DV), jnp.bfloat16),
            ((seq_count, HEADS, 1, DK), jnp.float32),
        ),
        [value_spec(block_len), key_spec(block_len), pair_spec(DK + EXTRA), decay_spec],
        seq_count,
        13,
    )


def mixer_output(first, local_out, reach, incoming, gates, head_gain):
    seq_count, block_len = reach.shape[:2]

    def kernel(first_ref, local, reach_ref, state, gate, gain, out, gated):
        result = local[0] + split_dot(reach_ref[0], state[0].astype(jnp.float32), NN)
        out[0] = result
        rms = lax.rsqrt(jnp.mean(result * result, axis=-1, keepdims=True) + epsilon)
        value = gate[0].astype(jnp.float32)
        gated[0] = (result * rms * gain[...] * (value * jax.nn.sigmoid(value))).astype(jnp.bfloat16)

    values = value_spec(block_len)
    return launch(
        kernel,
        (first, local_out, reach, incoming, gates, head_gain),
        [values, key_spec(block_len), pair_spec(DK), values]
        + [pl.BlockSpec((1, DV), lambda s, h, first: (0, 0))],
        (
            ((seq_count, block_len, HEADS * DV), jnp.float32),
            ((seq_count, block_len, HEADS * DV), jnp.bfloat16),
        ),
        [values, values],
        seq_count,
        4,
    )


def mixer_output_back(first, mixer_out, reach, gated_grad, gates, head_gain, decay):
    seq_count, block_len = reach.shape[:2]

    def kernel(
        first_ref,
        mixed,
        reach_ref,
        grad_ref,
        gate,
        gain,
        decay_ref,
        out_grad,
        gate_grad,
        term,
        gain_grad,
    ):
        result, grad = mixed[0], grad_ref[0]
        rms = lax.rsqrt(jnp.mean(result * result, axis=-1, keepdims=True) + epsilon)
        value = gate[0].astype(jnp.float32)
        sig = jax.nn.sigmoid(value)
        inner = grad * (value * sig)
        normed = result * rms
        gate_grad[0] = (
            grad * (normed * gain[...]) * sig * (1.0 + value * (1.0 - sig))
        ).astype(jnp.bfloat16)
        gain_grad[0, 0] = jnp.sum(inner * normed, axis=0, keepdims=True)
        scaled = inner * gain[...]
        grad_out = rms * (
            scaled - normed * rms * jnp.mean(scaled * result, axis=-1, keepdims=True)
        )
        out_grad[0] = grad_out
        term[0] = packed_rows(split_dot(reach_ref[0], grad_out, TN), decay_ref[0, 0])

    values = value_spec(block_len)
    return launch(
        kernel,
        (first, mixer_out, reach, gated_grad, gates, head_gain, decay),
        [values, key_spec(block_len), values, values]
        + [pl.BlockSpec((1, DV), lambda s, h, first: (0, 0)), decay_spec],
        (
            ((seq_count, block_len, HEADS * DV), jnp.float32),
            ((seq_count, block_len, HEADS * DV), jnp.bfloat16),
            ((GROUP, DK + EXTRA, DV), jnp.bfloat16),
            ((seq_count, HEADS, 1, DV), jnp.float32),
        ),
        [values, values, pair_spec(DK + EXTRA)]
        + [pl.BlockSpec((1, 1, 1, DV), lambda s, h, first: (s, h, 0, 0))],
        seq_count,
        5,
    )


def conv_back(grad, found, taps, pos, starts, block_len):
    wide, total, sig = found
    grad = grad * sig * (1.0 + total * (1.0 - sig))
    zeros = jnp.zeros((HALO, grad.shape[1]), jnp.float32)
    spread_grad, tap_grads = None, []
    for tap in range(CONV):
        masked = grad if tap == 0 else grad * (pos - tap >= starts).astype(jnp.float32)
        source = wide[HALO - tap : HALO - tap + block_len]
        tap_grads.append(jnp.sum(masked * source, axis=0, keepdims=True))
        padded = jnp.concatenate([zeros, masked * taps[tap : tap + 1, :], zeros], axis=0)
        part = padded[tap : tap + HALO + block_len]
        spread_grad = part if spread_grad is None else spread_grad + part
    return spread_grad, jnp.concatenate(tap_grads, axis=0)


def mixer_backward(first, wide_mixed, conv_weight, logits, starts, out_grad, incoming, outgoing):
    seq_count, block_len = starts.shape[:2]
    conv_width = wide_mixed.shape[2]
    wide_len = HALO + block_len

    def kernel(first_ref, q_ref, k_ref, v_ref, tq, tk, tv, logit_ref, start_ref, *refs):
        grad_ref, in_ref, end_ref, dq, dk, dv, wq, wk, wv, dlogit, bias = refs
        first, starts = first_ref[0], start_ref[0]
        taps = (tq, tk, tv)
        pos, found = activations(
            tuple(zip((q_ref, k_ref, v_ref), taps)), starts, first, block_len
        )
        query, key, value = [total * sig for _, total, sig in found]
        query = query * DK ** (-0.5)
        logit = logit_ref[0]
        log_decay = decays(logit)
        count = block_len // WIDE
        spans, states = [], [in_ref[0].astype(jnp.float32)]
        for index in range(count):
            span = Span(index, first, query, key, value, log_decay, starts, pos)
            spans.append(span)
            if index + 1 < count:
                states.append(span.next_state(states[-1]))
        later = end_ref[0].astype(jnp.float32)
        query_grads, key_grads, value_grads, decay_grads = [], [], [], []
        for index in range(count)[::-1]:
            span, state = spans[index], states[index]
            grad = grad_ref[0, span.rows]
            score_grad = jnp.where(span.allowed, split_dot(grad, span.value, NT), 0.0)
            query_grad = split_dot(score_grad, span.key_centred, NN) * span.to_query
            query_grad = query_grad + split_dot(grad, state, NT) * span.from_start
            end_grad = split_dot(span.value, later, NT)
            key_grad = split_dot(score_grad, span.query_centred, TN) * span.to_key
            key_grad = key_grad + end_grad * span.to_end
            value_grad = split_dot(span.scores(), grad, TN) + split_dot(span.key_end, later, NN)
            kept = unit_dot(jnp.ones((8, DV), jnp.float32), state * later, NT)[:1]
            total_grad = jnp.sum(end_grad * span.key_end, axis=0, keepdims=True)
            total_grad = total_grad + kept * jnp.exp(span.total) * span.kept
            cum_grad = span.query * query_grad - span.key * key_grad
            decay_grads.append(unit_dot(span.upper, cum_grad, NN) + total_grad)
            query_grads.append(query_grad)
            key_grads.append(key_grad)
            value_grads.append(value_grad)
            if index > 0:
                later = later * span.keep_column + split_dot(span.query_start, grad, TN)
        grads = [
            jnp.concatenate(parts[::-1], axis=0) for parts in (query_grads, key_grads, value_grads)
        ]
        grads[0] = grads[0] * DK ** (-0.5)
        for grad, piece, tap, out, tap_grad in zip(
            grads, found, taps, (dq, dk, dv), (wq, wk, wv)
        ):
            out[0], tap_grad[0] = conv_back(grad, piece, tap, pos, starts, block_len)
        decay_grad = jnp.concatenate(decay_grads[::-1], axis=0)
        decay_grad = jnp.where(starts < pos, decay_grad, 0.0)
        logit_grad = decay_grad / gate_scale * jax.nn.sigmoid(-logit)
        dlogit[0] = logit_grad
        bias[0, 0] = jnp.sum(logit_grad, axis=0, keepdims=True)

    wide_keys = pl.BlockSpec((1, wide_len, DK), lambda s, h, first: (s, 0, h))
    wide_values = pl.BlockSpec((1, wide_len, DV), lambda s, h, first: (s, 0, h))
    tap_keys = pl.BlockSpec((1, CONV, DK), lambda s, h, first: (s, 0, h))
    tap_values = pl.BlockSpec((1, CONV, DV), lambda s, h, first: (s, 0, h))
    keys, values = HEADS * DK, HEADS * DV
    return launch(
        kernel,
        (first, wide_mixed, wide_mixed, wide_mixed)
        + (conv_weight, conv_weight, conv_weight, logits, starts)
        + (out_grad, incoming, outgoing),
        mixer_specs(block_len) + [value_spec(block_len), pair_spec(DK), pair_spec(DK)],
        (
            ((seq_count, wide_len, keys), jnp.float32),
            ((seq_count, wide_len, keys), jnp.float32),
            ((seq_count, wide_len, values), jnp.float32),
            ((seq_count, CONV, keys), jnp.float32),
            ((seq_count, CONV, keys), jnp.float32),
            ((seq_count, CONV, values), jnp.float32),
            ((seq_count, block_len, keys), jnp.float32),
            ((seq_count, HEADS, 1, DK), jnp.float32),
        ),
        [wide_keys, wide_keys, wide_values, tap_keys, tap_keys, tap_values]
        + [key_spec(block_len), decay_spec],
        seq_count,
        24,
    )


def bf_dot(left, right):
    return jnp.dot(left, right, preferred_element_type=jnp.float32)


def feed_forward(hidden, out_grad, gain, w_gate, w_up, down_left, down_right):
    tokens, width = hidden.shape
    inner, tile = w_gate.shape[1], 256
    half = width // 2
    steps = inner // tile

    def kernel(hid, grad, gain_ref, wg, wu, wl, wr, *refs):
        out, back, back_low, normed, act, gate_back, up_back, gain_back, total, turned = refs
        step = pl.program_id(0)

        @pl.when(step == 0)
        def _():
            value = hid[...]
            rms = lax.rsqrt(jnp.mean(value * value, axis=-1, keepdims=True) + epsilon)
            normed[...] = (value * rms * gain_ref[...]).astype(jnp.bfloat16)
            total[...] = jnp.zeros_like(total)
            turned[...] = jnp.zeros_like(turned)

        source, low = normed[...], grad[...]
        gate, up = bf_dot(source, wg[...]), bf_dot(source, wu[...])
        inner_grad = nt_dot(low[:, :half], wl[...]) + nt_dot(low[:, half:], wr[...])
        sig = jax.nn.sigmoid(gate)
        silu = gate * sig
        active = (silu * up).astype(jnp.bfloat16)
        gate_grad = (inner_grad * up * sig * (1.0 + gate * (1.0 - sig))).astype(jnp.bfloat16)
        up_grad = (inner_grad * silu).astype(jnp.bfloat16)
        act[...], gate_back[...], up_back[...] = active, gate_grad, up_grad
        total[:, :half] += bf_dot(active, wl[...])
        total[:, half:] += bf_dot(active, wr[...])
        turned[...] += nt_dot(gate_grad, wg[...]) + nt_dot(up_grad, wu[...])

        @pl.when(step == steps - 1)
        def _():
            value, back_in = hid[...], turned[...]
            rms = lax.rsqrt(jnp.mean(value * value, axis=-1, keepdims=True) + epsilon)
            out[...] = value + total[...]
            gain_back[...] = jnp.sum(back_in * value * rms, axis=0, keepdims=True)
            result = grad[...].astype(jnp.float32) + rms_back(back_in, value, rms, gain_ref[...])
            back[...] = result
            back_low[...] = result.astype(jnp.bfloat16)

    def whole(rows, columns):
        return pl.BlockSpec((rows, columns), lambda i: (0, 0))

    across = pl.BlockSpec((width, tile), lambda i: (0, i))
    along = pl.BlockSpec((tile, half), lambda i: (i, 0))
    inner_spec = pl.BlockSpec((tokens, tile), lambda i: (0, i))
    inner_shape = jax.ShapeDtypeStruct((tokens, inner), jnp.bfloat16)
    return pl.pallas_call(
        kernel,
        out_shape=[
            jax.ShapeDtypeStruct((tokens, width), jnp.float32),
            jax.ShapeDtypeStruct((tokens, width), jnp.float32),
            jax.ShapeDtypeStruct((tokens, width), jnp.bfloat16),
            jax.ShapeDtypeStruct((tokens, width), jnp.bfloat16),
            inner_shape,
            inner_shape,
            inner_shape,
            jax.ShapeDtypeStruct((1, width), jnp.float32),
        ],
        grid=(steps,),
        in_specs=[whole(tokens, width), whole(tokens, width), whole(1, width)]
        + [across, across, along, along],
        out_specs=[whole(tokens, width)] * 4 + [inner_spec] * 3 + [whole(1, width)],
        scratch_shapes=[
            pltpu.VMEM((tokens, width), jnp.float32),
            pltpu.VMEM((tokens, width), jnp.float32),
        ],
        compiler_params=pltpu.CompilerParams(vmem_limit_bytes=52 * 2**20),
        cost_estimate=takes(28),
    )(hidden, out_grad, gain, w_gate, w_up, down_left, down_right)


def nt_dot(left, right):
    return lax.dot_general(left, right, (NT, ((), ())), preferred_element_type=jnp.float32)


def rms_back(grad_normed, source, inv_rms, gain_vec):
    scaled = grad_normed * gain_vec
    return inv_rms * (
        scaled - source * inv_rms * inv_rms * jnp.mean(scaled * source, axis=-1, keepdims=True)
    )


def local(
    inputs,
    doc_start,
    norm_gain,
    w_in,
    conv_weight,
    w_low,
    w_high,
    gate_bias,
    head_gain,
    w_out,
    ffn_gain,
    w_gate_up,
    w_down,
    out_grad,
):
    seq_count, block_len, model_width = inputs.shape
    row_count = seq_count * block_len
    key_width = HEADS * DK
    value_width = HEADS * DV
    conv_width = 2 * key_width + value_width
    block_start = lax.axis_index("seq") * block_len
    half = model_width // 2
    (
        (qk_full, v_full),
        (g_left, g_right),
        (out_left, out_right),
        (down_left, down_right),
        (gate_full, up_full),
    ) = gather_all([[w_in[:, :conv_width]], [w_in[:, conv_width:], w_out, w_down], [w_gate_up]])
    edge = shifted(inputs[:, block_len - HALO :, :], 1)
    wide = jnp.concatenate([edge, inputs], axis=1).astype(jnp.float32)
    wide_rms = lax.rsqrt(jnp.mean(wide * wide, axis=-1, keepdims=True) + epsilon)
    wide_normed = (wide * wide_rms * norm_gain).astype(jnp.bfloat16)
    layer_in = wide[:, HALO:].reshape(row_count, model_width)
    inv_rms = wide_rms[:, HALO:].reshape(row_count, 1)
    normed = wide_normed[:, HALO:].reshape(row_count, model_width)
    wide_rows = wide_normed.reshape(-1, model_width)
    wide_mixed = jnp.concatenate([bf_dot(wide_rows, qk_full), bf_dot(wide_rows, v_full)], axis=1)
    wide_mixed = wide_mixed.astype(jnp.bfloat16).reshape(seq_count, HALO + block_len, conv_width)
    gate_cols = jnp.concatenate([bf_dot(normed, g_left), bf_dot(normed, g_right)], axis=1)
    gate_cols = gate_cols.astype(jnp.bfloat16)
    lowrank = bf_dot(normed, w_low)
    gate_logit = (
        jnp.dot(lowrank, w_high, precision=highest, preferred_element_type=jnp.float32) + gate_bias
    )
    first = jnp.stack([block_start, lax.axis_index("seq") % GROUP]).astype(jnp.int32)
    starts = doc_start[:, :, None]
    logits = gate_logit.reshape(seq_count, block_len, key_width)
    gates = gate_cols.reshape(seq_count, block_len, value_width)
    gain_row = head_gain[None, :]
    local_out, reach, local_state, block_decay = mixer_forward(
        first, wide_mixed, conv_weight, logits, starts
    )
    incoming = carried_over(first, local_state, False)
    mixer_out, gated = mixer_output(first, local_out, reach, incoming, gates, gain_row)
    gated = gated.reshape(row_count, value_width)
    hidden_one = layer_in + jnp.concatenate(
        [bf_dot(gated, out_left), bf_dot(gated, out_right)], axis=1
    )
    out_rows_low = out_grad.reshape(row_count, model_width)
    (
        layer_out,
        hidden_grad,
        hidden_low,
        ffn_in,
        activation,
        gate_grad,
        up_grad,
        ffn_gain_row,
    ) = feed_forward(
        hidden_one, out_rows_low, ffn_gain[None, :], gate_full, up_full, down_left, down_right
    )
    ffn_gain_grad = ffn_gain_row[0]
    gate_up_terms = cores_summed(ffn_in, gate_grad, up_grad)
    down_terms = cores_summed(activation, out_rows_low[:, :half], out_rows_low[:, half:])
    out_terms = cores_summed(gated, hidden_low[:, :half], hidden_low[:, half:])
    gated_grad = nt_dot(hidden_low[:, :half], out_left) + nt_dot(hidden_low[:, half:], out_right)
    gated_grad = gated_grad.reshape(seq_count, block_len, value_width)
    mixer_grad, gate_vals_grad, state_term, head_gain_grad = mixer_output_back(
        first, mixer_out, reach, gated_grad, gates, gain_row, block_decay
    )
    gate_vals_grad = gate_vals_grad.reshape(row_count, value_width)
    head_gain_grad = jnp.sum(head_gain_grad, axis=(0, 1, 2))
    g_terms = cores_summed(normed, gate_vals_grad[:, :half], gate_vals_grad[:, half:])
    outgoing = carried_over(first, state_term, True)
    outgoing, gate_up_terms = together(outgoing, gate_up_terms)
    gate_up_terms = sides_summed([gate_up_terms])
    q_back, k_back, v_back, q_taps, k_taps, v_taps, logit_grad, gate_bias_grad = mixer_backward(
        first, wide_mixed, conv_weight, logits, starts, mixer_grad, incoming, outgoing
    )
    conv_weight_grad = jnp.sum(jnp.concatenate([q_taps, k_taps, v_taps], axis=-1), axis=0)
    padded_grad = jnp.concatenate([q_back, k_back, v_back], axis=-1)
    back_edge = shifted(padded_grad[:, :HALO].astype(jnp.bfloat16), -1).astype(jnp.float32)
    mixed_grad = padded_grad[:, HALO:] + jnp.pad(
        back_edge, ((0, 0), (block_len - HALO, 0), (0, 0))
    )
    mixed_grad = mixed_grad.reshape(row_count, conv_width).astype(jnp.bfloat16)
    qk_grad, v_grad = mixed_grad[:, : 2 * key_width], mixed_grad[:, 2 * key_width :]
    qk_grad, gate_up_terms, down_terms = together(qk_grad, gate_up_terms, down_terms)
    w_gate_up_grad = levels_summed(gate_up_terms)
    rest_terms = sides_summed([g_terms, out_terms, down_terms])
    qkv_terms = cores_summed(normed, qk_grad, v_grad)
    rest_terms, qkv_terms = together(rest_terms, qkv_terms)
    rest = levels_summed(rest_terms)
    qkv_grad = levels_summed(sides_summed([qkv_terms]))
    w_in_rows = w_in.shape[0]
    w_out_grad = rest[w_in_rows : 2 * w_in_rows]
    w_down_grad = rest[2 * w_in_rows :]
    w_in_grad = jnp.concatenate([qkv_grad, rest[:w_in_rows]], axis=1)
    logit_grad = logit_grad.reshape(row_count, key_width)
    gate_bias_grad = jnp.sum(gate_bias_grad, axis=0).reshape(-1)
    w_high_grad = jnp.dot(
        lowrank.T, logit_grad, precision=highest, preferred_element_type=jnp.float32
    )
    lowrank_grad = jnp.dot(
        logit_grad, w_high.T, precision=highest, preferred_element_type=jnp.float32
    ).astype(jnp.bfloat16)
    w_low_grad = jnp.dot(normed.T, lowrank_grad, preferred_element_type=jnp.float32)
    normed_grad = (
        bf_dot(qk_grad, qk_full.T)
        + bf_dot(v_grad, v_full.T)
        + nt_dot(gate_vals_grad[:, :half], g_left)
        + nt_dot(gate_vals_grad[:, half:], g_right)
        + bf_dot(lowrank_grad, w_low.T)
    )
    norm_gain_grad = jnp.sum(normed_grad * layer_in * inv_rms, axis=0)
    input_grad = hidden_grad + rms_back(normed_grad, layer_in, inv_rms, norm_gain)
    small = (
        norm_gain_grad,
        conv_weight_grad,
        w_low_grad,
        w_high_grad,
        gate_bias_grad,
        head_gain_grad,
        ffn_gain_grad,
    )
    summed = small_sum(jnp.concatenate([part.reshape(-1, 128) for part in small]))
    small_grads, start = [], 0
    for part in small:
        rows = part.size // 128
        small_grads.append(summed[start : start + rows].reshape(part.shape))
        start += rows
    return (
        layer_out.reshape(seq_count, block_len, model_width),
        input_grad.reshape(seq_count, block_len, model_width),
        small_grads[0],
        w_in_grad,
        small_grads[1],
        small_grads[2],
        small_grads[3],
        small_grads[4],
        small_grads[5],
        w_out_grad,
        small_grads[6],
        w_gate_up_grad,
        w_down_grad,
    )


def solution(mesh):
    placed = (
        P(None, "seq", None),
        P(None, "seq"),
        P(),
        P("seq", None),
        P(),
        P(),
        P(),
        P(),
        P(),
        P("seq", None),
        P(),
        P("seq", None),
        P("seq", None),
        P(None, "seq", None),
    )
    return jax.shard_map(
        local,
        mesh=mesh,
        in_specs=placed,
        out_specs=(
            P(None, "seq", None),
            P(None, "seq", None),
            P(),
            P("seq", None),
            P(),
            P(),
            P(),
            P(),
            P(),
            P("seq", None),
            P(),
            P("seq", None),
            P("seq", None),
        ),
        check_vma=False,
    )
```

```python
import jax
import jax.numpy as jnp
from jax import lax
from jax.experimental import pallas as pl
from jax.experimental.pallas import tpu as pltpu
from jax.sharding import PartitionSpec as P

HEADS = 4
DK = 128
DV = 256
FF = 2816
WIDE = 128
CONV = 4


epsilon = 1e-06
gate_scale = 16.0
highest = lax.Precision.HIGHEST


GROUP = 8
HALO = 8
EXTRA = 16
SMALL = 40
PER_HEAD = 2 * DK + DV


def chip_axes():
    count = lax.axis_size("seq")
    sides = {16: (4, 2, 2), 64: (4, 4, 4)}.get(count // 2, (count // 2, 1, 1))
    return (
        (sides[0], 2 * sides[1] * sides[2]),
        (sides[1], 2 * sides[2]),
        (sides[2], 2),
        (2, 1),
    )


def swapped(array, mask):
    count = lax.axis_size("seq")
    return lax.ppermute(array, "seq", [(i, i ^ mask) for i in range(count)])


def shifted(array, by):
    count = lax.axis_size("seq")
    pairs = [(i, i + by) for i in range(count) if 0 <= i + by < count]
    return lax.ppermute(array, "seq", pairs)


def spread(block, axis):
    size, stride = axis
    return [block] + [swapped(block, step * stride) for step in range(1, size)]


def takes(micros):
    return pl.CostEstimate(flops=int(micros * 1e9), bytes_accessed=0, transcendentals=0)


def coordinates():
    mine = lax.axis_index("seq")
    return jnp.stack([(mine // stride) % size for size, stride in chip_axes()]).astype(jnp.int32)


def placed_blocks(sources, one, two, cuts):
    axes = chip_axes()
    sizes = tuple(size for size, _ in axes)
    depth, mine = sizes[0], coordinates()
    (rows, columns), kind = sources[0][0].shape[3:], sources[0][0].dtype

    def target(core, second, first, me):
        spot = [0, 0, 0, 0]
        spot[one] = jnp.bitwise_xor(first, me[one])
        spot[two] = jnp.bitwise_xor(second, me[two])
        spot[3] = jnp.bitwise_xor(core, me[3])
        return tuple(spot) + (0, 0)

    def source(mine_core, base, extent):
        def index(core, second, first, me):
            step = core * sizes[two] + second - mine_core * sizes[two] - base
            early, late = step < 0, step >= extent
            held = jnp.where(early, 0, jnp.where(late, extent - 1, step))
            return (
                held,
                jnp.where(early, 0, jnp.where(late, sizes[one] - 1, first)),
                0,
                0,
                0,
            )

        return index

    def kernel(me, *refs):
        pieces, outs = refs[: len(sources)], refs[len(sources) :]
        step = pl.program_id(0) * sizes[two] + pl.program_id(1)
        for piece, (array, core, base) in zip(pieces, sources):
            begin = core * sizes[two] + base

            @pl.when((step >= begin) & (step < begin + array.shape[0]))
            def _():
                for level in range(depth):
                    block, start = piece[0, 0, level], 0
                    for out, cut in zip(outs, cuts):
                        out[jnp.bitwise_xor(me[0], level), 0, 0, 0] = block[start : start + cut]
                        start += cut

    found = pl.pallas_call(
        kernel,
        out_shape=[jax.ShapeDtypeStruct(sizes + (cut, columns), kind) for cut in cuts],
        grid_spec=pltpu.PrefetchScalarGridSpec(
            num_scalar_prefetch=1,
            grid=(2, sizes[two], sizes[one]),
            in_specs=[
                pl.BlockSpec((1, 1, depth, rows, columns), source(core, base, array.shape[0]))
                for array, core, base in sources
            ],
            out_specs=[pl.BlockSpec((depth, 1, 1, 1, cut, columns), target) for cut in cuts],
        ),
        compiler_params=pltpu.CompilerParams(vmem_limit_bytes=40 * 2**20),
        cost_estimate=takes(1.0 + rows * columns * 5e-5),
    )(mine, *[array for array, _, _ in sources])
    return [array.reshape(-1, columns) for array in found]


def together(*values):
    return lax.optimization_barrier(values)


def gather_levels(shard):
    return spread(shard, chip_axes()[0])


def gather_first(levels):
    half = levels[0].shape[1] // 2
    stacked = jnp.stack(levels)
    axes = chip_axes()
    return [spread(stacked[..., :half], axes[2]), spread(stacked[..., half:], axes[1])]


def gather_second(sides):
    axes = chip_axes()
    return [spread(jnp.stack(sides[0]), axes[1]), spread(jnp.stack(sides[1]), axes[2])]


def gather_cores(crossed):
    found = []
    for pieces in crossed:
        own = jnp.stack(pieces)
        found.append([own, swapped(own, 1)])
    return found


def gather_done(pairs, cuts):
    halves = [
        placed_blocks([(own, 0, 0), (other, 1, 0)], one, two, cuts)
        for (own, other), one, two in zip(pairs, (2, 1), (1, 2))
    ]
    return list(zip(*halves))


def core_sources(crossed, early):
    halves = []
    for pieces, before in zip(crossed, early):
        sources = []
        for step, piece in enumerate(pieces):
            other = before if step == 0 else swapped(piece, 1)
            sources.extend([(piece[None], 0, step), (other[None], 1, step)])
        halves.append(sources)
    return halves


def assemble(held, refs, sources, me, one, two):
    for ref, (array, core, base) in zip(refs, sources):
        for second in range(array.shape[0]):
            for first in range(array.shape[1]):
                for level in range(array.shape[2]):
                    spot = [jnp.bitwise_xor(me[0], level), 0, 0, jnp.bitwise_xor(me[3], core)]
                    spot[one] = jnp.bitwise_xor(me[one], first)
                    spot[two] = jnp.bitwise_xor(me[two], base + second)
                    held[tuple(spot)] = ref[second, first, level]
    return held[...].reshape(-1, held.shape[-1])


def tile_spec(array, tile, index):
    return pl.BlockSpec(array.shape[:4] + (tile,), index)


def projected(rows, sources_a, sources_b):
    sizes, mine = tuple(size for size, _ in chip_axes()), coordinates()
    tokens, width = rows.shape
    block_rows, half = sources_a[0][0].shape[3:]
    tile = 256
    tiles = half // tile

    def kernel(me, row_ref, *refs):
        refs_a = refs[: len(sources_a)]
        refs_b = refs[len(sources_a) : -2]
        out, held = refs[-2:]

        @pl.when(pl.program_id(0) == 0)
        def _():
            assemble(held, refs_a, sources_a, me, 2, 1)

        @pl.when(pl.program_id(0) == 1)
        def _():
            assemble(held, refs_b, sources_b, me, 1, 2)

        full = held[...].reshape(width, tile)
        out[...] = bf_dot(row_ref[...], full).astype(jnp.bfloat16)

    def at_a(part, i, me):
        return (0, 0, 0, 0, jnp.where(part == 0, i, tiles - 1))

    def at_b(part, i, me):
        return (0, 0, 0, 0, jnp.where(part == 0, 0, i))

    return pl.pallas_call(
        kernel,
        out_shape=jax.ShapeDtypeStruct((tokens, 2 * half), jnp.bfloat16),
        grid_spec=pltpu.PrefetchScalarGridSpec(
            num_scalar_prefetch=1,
            grid=(2, tiles),
            in_specs=[pl.BlockSpec((tokens, width), lambda part, i, me: (0, 0))]
            + [tile_spec(array, tile, at_a) for array, _, _ in sources_a]
            + [tile_spec(array, tile, at_b) for array, _, _ in sources_b],
            out_specs=pl.BlockSpec((tokens, tile), lambda part, i, me: (0, part * tiles + i)),
            scratch_shapes=[pltpu.VMEM(sizes + (block_rows, tile), jnp.bfloat16)],
        ),
        compiler_params=pltpu.CompilerParams(vmem_limit_bytes=40 * 2**20),
        cost_estimate=takes(6),
    )(mine, rows, *[array for array, _, _ in sources_a + sources_b])


def grad_products(left, right_a, right_b=None):
    sizes = tuple(size for size, _ in chip_axes())
    strides = tuple(stride for _, stride in chip_axes())
    (tokens, features), columns = left.shape, right_a.shape[1]
    if right_b is None:
        columns = columns // 2
    count, mine = lax.axis_size("seq"), coordinates()
    rows = features // count
    tile = 512 if columns % 512 == 0 and features <= 1024 else 256
    chunks = next(c for c in (4, 2, 1) if features // c % 128 == 0)
    chunk = features // chunks

    def kernel(me, left_ref, a_ref, b_ref, away_a, keep_a, away_b, keep_b, flipped):
        @pl.when(pl.program_id(0) == 0)
        def _():
            flipped[...] = left_ref[...].T

        def products(odd):
            for right, away, keep, order in (
                (a_ref, away_a, keep_a, (2, 1, 0)),
                (b_ref, away_b, keep_b, (1, 2, 0)),
            ):
                for part in range(chunks):
                    full = jnp.dot(
                        flipped[part * chunk : (part + 1) * chunk],
                        right[...],
                        preferred_element_type=jnp.float32,
                    )
                    for start in range(0, chunk, rows):
                        device = (part * chunk + start) // rows
                        spot = tuple(
                            jnp.bitwise_xor(device // strides[axis] % sizes[axis], me[axis])
                            for axis in order
                        )
                        target = keep if device % 2 == odd else away
                        target[spot] = full[start : start + rows].astype(jnp.bfloat16)

        @pl.when(me[3] == 0)
        def _():
            products(0)

        @pl.when(me[3] == 1)
        def _():
            products(1)

    def result(one, two):
        shape = (sizes[one], sizes[two], sizes[0], rows)
        return (
            jax.ShapeDtypeStruct(shape + (columns,), jnp.bfloat16),
            pl.BlockSpec(shape + (tile,), lambda i, me: (0, 0, 0, 0, i)),
        )

    results = [result(2, 1), result(2, 1), result(1, 2), result(1, 2)]
    skip = columns // tile if right_b is None else 0
    right_b = right_a if right_b is None else right_b
    return pl.pallas_call(
        kernel,
        out_shape=[shape for shape, _ in results],
        grid_spec=pltpu.PrefetchScalarGridSpec(
            num_scalar_prefetch=1,
            grid=(columns // tile,),
            in_specs=[
                pl.BlockSpec((tokens, features), lambda i, me: (0, 0)),
                pl.BlockSpec((tokens, tile), lambda i, me: (0, i)),
                pl.BlockSpec((tokens, tile), lambda i, me: (0, i + skip)),
            ],
            out_specs=[spec for _, spec in results],
            scratch_shapes=[pltpu.VMEM((features, tokens), jnp.bfloat16)],
        ),
        compiler_params=pltpu.CompilerParams(vmem_limit_bytes=48 * 2**20),
        cost_estimate=takes(1.5 + features * columns * 4.5e-6),
    )(mine, left, right_a, right_b)


def total_of(groups):
    parts = []
    for refs, lead in groups:
        rows = [ref[(0,) * lead].astype(jnp.float32) for ref in refs]
        parts.append(jnp.concatenate(rows, axis=0) if len(rows) > 1 else rows[0])
    return sum(parts[1:], parts[0])


def flat_terms(terms):
    return [(since, arrays) for since, group in enumerate(terms) for arrays in group]


def regrouped(refs, flat):
    groups, at = [], 0
    for since, arrays in flat:
        groups.append((refs[at : at + len(arrays)], since))
        at += len(arrays)
    return groups, at


def phase_sums(pair, phase, step):
    flats = [flat_terms(terms) for terms in pair]
    depth = chip_axes()[0][0]
    second = chip_axes()[1][0] if phase == 0 else 1
    rows = sum(array.shape[-2] for array in flats[0][0][1])
    columns = flats[0][0][1][0].shape[-1]
    lead = 2 - phase

    def index(since):
        def found(i, j):
            spot = [0 if dim < phase else step if dim == phase else (i, j)[dim - 1] for dim in range(3)]
            return tuple(spot[since:]) + (0, 0)

        return found

    def kernel(*refs):
        ins, outs = refs[:-2], refs[-2:]
        at = 0
        for flat, out in zip(flats, outs):
            groups, used = regrouped(ins[at:], flat)
            at += used
            total = total_of([(part, 3 - since) for part, since in groups])
            out[(0,) * lead] = total.astype(jnp.bfloat16)

    arrays = [(array, since) for flat in flats for since, group in flat for array in group]
    shape = ((second, depth) if phase == 0 else (depth,)) + (rows, columns)
    out_spec = pl.BlockSpec(
        (1,) * lead + (rows, columns), lambda i, j: ((i, j) if phase == 0 else (j,)) + (0, 0)
    )
    return pl.pallas_call(
        kernel,
        out_shape=[jax.ShapeDtypeStruct(shape, jnp.bfloat16)] * 2,
        grid=(second, depth),
        in_specs=[
            pl.BlockSpec((1,) * (3 - since) + array.shape[-2:], index(since))
            for array, since in arrays
        ],
        out_specs=[out_spec] * 2,
        compiler_params=pltpu.CompilerParams(vmem_limit_bytes=32 * 2**20),
        cost_estimate=takes(3),
    )(*[array for array, _ in arrays])


def level_sums(pair):
    flats = [flat_terms(terms) for terms in pair]
    depth = chip_axes()[0][0]
    rows = sum(array.shape[-2] for array in flats[0][0][1])
    columns = flats[0][0][1][0].shape[-1]

    def kernel(*refs):
        ins, outs = refs[:-depth], refs[-depth:]
        at = 0
        for side, flat in enumerate(flats):
            groups, used = regrouped(ins[at:], flat)
            at += used
            cut = slice(side * columns, (side + 1) * columns)
            for level in range(depth):
                parts = []
                for part, since in groups:
                    spot = (0,) * (2 - since) + (level,)
                    values = [ref[spot].astype(jnp.float32) for ref in part]
                    parts.append(
                        jnp.concatenate(values, axis=0) if len(values) > 1 else values[0]
                    )
                total = sum(parts[1:], parts[0])
                outs[level][:, cut] = total.astype(outs[level].dtype)

    arrays = [(array, since) for flat in flats for since, group in flat for array in group]

    def spec(array, since):
        lead = (1,) * (2 - since) + (depth,)
        return pl.BlockSpec(lead + array.shape[-2:], lambda i: (0,) * (len(lead) + 2))

    shape = (rows, 2 * columns)
    return pl.pallas_call(
        kernel,
        out_shape=[jax.ShapeDtypeStruct(shape, jnp.float32)]
        + [jax.ShapeDtypeStruct(shape, jnp.bfloat16)] * (depth - 1),
        grid=(1,),
        in_specs=[spec(array, since) for array, since in arrays],
        out_specs=[pl.BlockSpec(shape, lambda i: (0, 0))] * depth,
        compiler_params=pltpu.CompilerParams(vmem_limit_bytes=40 * 2**20),
        cost_estimate=takes(3),
    )(*[array for array, _ in arrays])


def cores_send(products):
    found = []
    for keep, which in ((1, 0), (3, 2)):
        aways = [part[which] for part in products]
        away = jnp.concatenate(aways, axis=3) if len(aways) > 1 else aways[0]
        found.append([[[part[keep] for part in products], [swapped(away, 1)]]])
    return found


def phase_send(pair, phase):
    axes = chip_axes()
    size = axes[2][0]
    received = [[], []]
    for step in range(1, size):
        for side, part in enumerate(phase_sums(pair, phase, step)):
            stride = axes[((2, 1), (1, 2))[side][phase]][1]
            received[side].append([swapped(part, step * stride)])
    return [terms + [parts] for terms, parts in zip(pair, received)]


def levels_send(pair):
    own, *parts = level_sums(pair)
    stride = chip_axes()[0][1]
    return own, [swapped(part, (step + 1) * stride) for step, part in enumerate(parts)]


def reduced(own, found):
    return sum((part.astype(jnp.float32) for part in found), own)


def small_packed(logit_grad, lowrank, w_high, normed, tap_grads, bias, head_gain, ffn_gain):
    tokens, keys = logit_grad.shape
    width, rank = normed.shape[1], w_high.shape[0]

    def kernel(grad_ref, low_ref, high_ref, normed_ref, taps, bias_ref, head, ffn, out, low_grad):
        grad = grad_ref[...]
        back = split_dot(grad, high_ref[...], NT).astype(jnp.bfloat16)
        low_grad[...] = back
        out[:rank] = lax.dot_general(
            back, normed_ref[...], (TN, ((), ())), preferred_element_type=jnp.float32
        )
        tap = jnp.sum(taps[...], axis=0)
        out[rank : rank + CONV] = tap[:, :width]
        out[rank + CONV : rank + 2 * CONV] = tap[:, width:]
        high = split_dot(low_ref[...], grad, TN)
        out[24:32, :keys] = high[:8]
        out[24:32, keys:] = high[8:]
        out[32:40] = jnp.zeros((8, width), jnp.float32)
        out[32:33, :keys] = jnp.sum(bias_ref[...], axis=0, keepdims=True)
        gains = [jnp.sum(head[:, h, 0], axis=0, keepdims=True) for h in range(HEADS)]
        out[32:33, keys : keys + DV] = sum(gains)
        out[33:34] = ffn[...]

    return pl.pallas_call(
        kernel,
        out_shape=[
            jax.ShapeDtypeStruct((SMALL, width), jnp.float32),
            jax.ShapeDtypeStruct((tokens, rank), jnp.bfloat16),
        ],
        compiler_params=pltpu.CompilerParams(vmem_limit_bytes=32 * 2**20),
        cost_estimate=takes(4),
    )(logit_grad, lowrank, w_high, normed, tap_grads, bias, head_gain, ffn_gain)


def small_unpacked(parts, keys, rank):
    width = parts[0].shape[1]

    def kernel(*refs):
        ins, (norm, conv, low, high, bias, head, ffn) = refs[: len(parts)], refs[len(parts) :]
        total = sum(ref[...] for ref in ins)
        low[...] = total[:rank]
        for h in range(HEADS):
            side, at = divmod(h * PER_HEAD, width)
            block = total[rank + side * CONV : rank + (side + 1) * CONV]
            conv[:, h * DK : (h + 1) * DK] = block[:, at : at + DK]
            conv[:, keys + h * DK : keys + (h + 1) * DK] = block[:, at + DK : at + 2 * DK]
            conv[:, 2 * keys + h * DV : 2 * keys + (h + 1) * DV] = block[
                :, at + 2 * DK : at + PER_HEAD
            ]
        high[:8] = total[24:32, :keys]
        high[8:] = total[24:32, keys:]
        bias[...] = total[32:33, :keys]
        head[...] = total[32:33, keys : keys + DV]
        ffn[...] = total[33:34]
        norm[...] = total[34:35]

    shapes = ((1, width), (CONV, 2 * width), (rank, width), (rank, keys))
    shapes += ((1, keys), (1, DV), (1, width))
    return pl.pallas_call(
        kernel,
        out_shape=[jax.ShapeDtypeStruct(shape, jnp.float32) for shape in shapes],
        cost_estimate=takes(2),
    )(*parts)


def by_head(array):
    lead, (keys, values) = array.shape[:-1], (HEADS * DK, HEADS * DV)
    parts = [
        part.reshape(lead + (HEADS, -1))
        for part in (array[..., :keys], array[..., keys : 2 * keys], array[..., 2 * keys :])
    ]
    return jnp.concatenate(parts, axis=-1).reshape(lead + (2 * keys + values,))


def by_kind(array):
    lead = array.shape[:-1]
    array = array.reshape(lead + (HEADS, -1))
    parts = (array[..., :DK], array[..., DK : 2 * DK], array[..., 2 * DK :])
    return jnp.concatenate([part.reshape(lead + (-1,)) for part in parts], axis=-1)


def exchange_step(pieces, at, mask):
    kept = lax.index_in_dim(pieces, 0, at, False)
    return [kept, swapped(lax.index_in_dim(pieces, 1, at, False), mask)]


def exchanged(pieces, fillers=((), (), ())):
    shape, filled = pieces.shape, []
    pieces = pieces.reshape((2, 2, 2) + shape[1:])
    for at, mask, filler in zip((2, 1, 0), (1, 2, 4), fillers):
        pair = exchange_step(pieces, at, mask)
        if filler:
            values = filler[0](*filled[-1:])
            pair, values = together(pair, values)
            filled.append(values)
        pieces = jnp.stack(pair, axis=at)
    return pieces.reshape(shape), filled


def column(row):
    square = jnp.broadcast_to(row, (DK, DK)).T
    return jnp.concatenate([square, square], axis=1)


def packed_rows(state, decay):
    high = decay.astype(jnp.bfloat16)
    low = (decay - high.astype(jnp.float32)).astype(jnp.bfloat16)
    tail = jnp.broadcast_to(jnp.concatenate([high, low], axis=1), (EXTRA, DV))
    return jnp.concatenate([state.astype(jnp.bfloat16), tail], axis=0)


def composed(place, got, backward, beyond=None):
    order = range(GROUP)[::-1] if backward else range(GROUP)

    def kernel(place_ref, got_ref, *refs):
        mine, out = place_ref[1], refs[-1]
        running = jnp.zeros((DK, DV), jnp.float32)
        reach = jnp.ones((DK, DV), jnp.float32)
        far = None if beyond is None else refs[0][...].astype(jnp.float32)
        for index in order:
            spot = jnp.bitwise_xor(mine, index)
            piece = got_ref[spot].astype(jnp.float32)
            if beyond is not None:
                out[spot] = (running + reach * far).astype(jnp.bfloat16)
            tail = piece[DK : DK + 1]
            kept = column(tail[:, :DK] + tail[:, DK:])
            running = kept * running + piece[:DK]
            reach = reach * kept
        if beyond is None:
            out[...] = running.astype(jnp.bfloat16)

    extra = () if beyond is None else (beyond,)
    shape = (DK, DV) if beyond is None else (GROUP, DK, DV)
    return pl.pallas_call(
        kernel,
        out_shape=jax.ShapeDtypeStruct(shape, jnp.bfloat16),
        in_specs=[pl.BlockSpec(memory_space=pltpu.SMEM)]
        + [pl.BlockSpec(memory_space=pltpu.VMEM)] * (1 + len(extra)),
        out_specs=pl.BlockSpec(memory_space=pltpu.VMEM),
        cost_estimate=takes(2),
    )(place, got, *extra)


def split_dot(left, right, dims):
    dims = (dims, ((), ()))
    left_high, right_high = left.astype(jnp.bfloat16), right.astype(jnp.bfloat16)
    left_low = (left - left_high.astype(jnp.float32)).astype(jnp.bfloat16)
    right_low = (right - right_high.astype(jnp.float32)).astype(jnp.bfloat16)

    def one(a, b):
        return lax.dot_general(a, b, dims, preferred_element_type=jnp.float32)

    return one(left_high, right_high) + (one(left_high, right_low) + one(left_low, right_high))


def unit_dot(unit, value, dims):
    high = value.astype(jnp.bfloat16)
    rest = value - high.astype(jnp.float32)
    middle = rest.astype(jnp.bfloat16)
    low = (rest - middle.astype(jnp.float32)).astype(jnp.bfloat16)
    unit = unit.astype(jnp.bfloat16)
    return sum(
        lax.dot_general(unit, part, (dims, ((), ())), preferred_element_type=jnp.float32)
        for part in (low, middle, high)
    )


NN, NT, TN = ((1,), (0,)), ((1,), (1,)), ((0,), (0,))


def activations(block, taps, starts, first, block_len):
    pos = first + lax.broadcasted_iota(jnp.int32, (block_len, 1), 0)
    wide = block[0].astype(jnp.float32)
    total = taps[0:1, :] * wide[HALO:]
    for tap in range(1, CONV):
        usable = (pos - tap >= starts).astype(jnp.float32)
        total = total + taps[tap : tap + 1, :] * wide[HALO - tap : HALO - tap + block_len] * usable
    sig = jax.nn.sigmoid(total)
    active = total * sig
    query, key, value = active[:, :DK], active[:, DK : 2 * DK], active[:, 2 * DK :]
    return pos, (wide, total, sig), query * DK ** (-0.5), key, value


def decays(logit):
    return (jnp.minimum(logit, 0.0) - jnp.log1p(jnp.exp(-jnp.abs(logit)))) / gate_scale


class Span:
    def __init__(self, index, first, query, key, value, decay, starts, pos):
        rows = slice(index * WIDE, (index + 1) * WIDE)
        self.rows, first_pos = rows, first + index * WIDE
        self.query, self.key, self.value = query[rows], key[rows], value[rows]
        decay, starts, pos = decay[rows], starts[rows], pos[rows]
        t = lax.broadcasted_iota(jnp.int32, (WIDE, WIDE), 0)
        u = lax.broadcasted_iota(jnp.int32, (WIDE, WIDE), 1)
        self.lower = (u <= t).astype(jnp.float32)
        self.upper = (u >= t).astype(jnp.float32)
        self.allowed = (u <= t) & (u + first_pos >= starts)
        cum = unit_dot(self.lower, decay, NN)
        self.total = cum[WIDE - 1 :]
        middle = cum[WIDE // 2 - 1 : WIDE // 2]
        self.to_query, self.to_key = jnp.exp(cum - middle), jnp.exp(middle - cum)
        self.carried = (starts < first_pos).astype(jnp.float32)
        self.kept = (starts[WIDE - 1 :] < first_pos).astype(jnp.float32)
        self.from_start = jnp.exp(cum) * self.carried
        self.to_end = jnp.exp(self.total - cum) * (pos >= starts[WIDE - 1 :]).astype(jnp.float32)
        self.query_centred = self.query * self.to_query
        self.key_centred = self.key * self.to_key
        self.query_start = self.query * self.from_start
        self.key_end = self.key * self.to_end
        self.cum = cum
        ones = jnp.ones((WIDE, DV), jnp.float32)
        total_column = unit_dot_right(decay, ones)
        self.keep_column = jnp.exp(total_column) * self.kept

    def scores(self):
        raw = split_dot(self.query_centred, self.key_centred, NT)
        return jnp.where(self.allowed, raw, 0.0)

    def next_state(self, state):
        update = split_dot(self.key_end, self.value, TN)
        return update if state is None else state * self.keep_column + update


def unit_dot_right(value, unit):
    high = value.astype(jnp.bfloat16)
    rest = value - high.astype(jnp.float32)
    middle = rest.astype(jnp.bfloat16)
    low = (rest - middle.astype(jnp.float32)).astype(jnp.bfloat16)
    unit = unit.astype(jnp.bfloat16)
    return sum(
        lax.dot_general(part, unit, (TN, ((), ())), preferred_element_type=jnp.float32)
        for part in (low, middle, high)
    )


def mixer_specs(block_len):
    return [
        pl.BlockSpec((1, HALO + block_len, PER_HEAD), lambda s, h, first: (s, 0, h)),
        pl.BlockSpec((CONV, PER_HEAD), lambda s, h, first: (0, h)),
        pl.BlockSpec((1, block_len, DK), lambda s, h, first: (s, 0, h)),
        pl.BlockSpec((1, block_len, 1), lambda s, h, first: (s, 0, 0)),
    ]


def key_spec(block_len):
    return pl.BlockSpec((1, block_len, DK), lambda s, h, first: (s, 0, h))


def value_spec(block_len):
    return pl.BlockSpec((1, block_len, DV), lambda s, h, first: (s, 0, h))


def pair_spec(rows):
    return pl.BlockSpec(
        (1, rows, DV), lambda s, h, place: (jnp.bitwise_xor(place[1], s * HEADS + h), 0, 0)
    )


decay_spec = pl.BlockSpec((1, 1, 1, DK), lambda s, h, first: (s, h, 0, 0))


def launch(kernel, inputs, in_specs, outputs, out_specs, seq_count, micros):
    return pl.pallas_call(
        kernel,
        out_shape=[jax.ShapeDtypeStruct(shape, kind) for shape, kind in outputs],
        grid_spec=pltpu.PrefetchScalarGridSpec(
            num_scalar_prefetch=1,
            grid=(seq_count, HEADS),
            in_specs=in_specs,
            out_specs=out_specs,
        ),
        compiler_params=pltpu.CompilerParams(vmem_limit_bytes=40 * 2**20),
        cost_estimate=takes(micros),
    )(*inputs)


def mixer_forward(first, wide_mixed, conv_weight, logits, starts):
    seq_count, block_len = starts.shape[:2]

    def kernel(first_ref, block, taps, logit_ref, start_ref, out, reach, state, decay):
        first, starts = first_ref[0], start_ref[0]
        pos, _, query, key, value = activations(block, taps, starts, first, block_len)
        log_decay = decays(logit_ref[0])
        running = None
        before = jnp.zeros((1, DK), jnp.float32)
        reach_in = (starts < first).astype(jnp.float32)
        for index in range(block_len // WIDE):
            span = Span(index, first, query, key, value, log_decay, starts, pos)
            result = split_dot(span.scores(), span.value, NN)
            if running is not None:
                result = result + split_dot(span.query_start, running, NN)
            out[0, span.rows] = result
            reach[0, span.rows] = span.query * jnp.exp(before + span.cum) * reach_in[span.rows]
            before = before + span.total
            running = span.next_state(running)
        block_decay = jnp.exp(before) * reach_in[block_len - 1 :]
        state[0] = packed_rows(running, block_decay)
        decay[0, 0] = block_decay

    return launch(
        kernel,
        (first, wide_mixed, conv_weight, logits, starts),
        mixer_specs(block_len),
        (
            ((seq_count, block_len, HEADS * DV), jnp.float32),
            ((seq_count, block_len, HEADS * DK), jnp.float32),
            ((GROUP, DK + EXTRA, DV), jnp.bfloat16),
            ((seq_count, HEADS, 1, DK), jnp.float32),
        ),
        [value_spec(block_len), key_spec(block_len), pair_spec(DK + EXTRA), decay_spec],
        seq_count,
        13,
    )


def mixer_output(first, local_out, reach, incoming, gates, head_gain):
    seq_count, block_len = reach.shape[:2]

    def kernel(first_ref, local, reach_ref, state, gate, gain, out, gated):
        result = local[0] + split_dot(reach_ref[0], state[0].astype(jnp.float32), NN)
        out[0] = result
        rms = lax.rsqrt(jnp.mean(result * result, axis=-1, keepdims=True) + epsilon)
        value = gate[0].astype(jnp.float32)
        gated[0] = (result * rms * gain[...] * (value * jax.nn.sigmoid(value))).astype(jnp.bfloat16)

    values = value_spec(block_len)
    return launch(
        kernel,
        (first, local_out, reach, incoming, gates, head_gain),
        [values, key_spec(block_len), pair_spec(DK), values]
        + [pl.BlockSpec((1, DV), lambda s, h, first: (0, 0))],
        (
            ((seq_count, block_len, HEADS * DV), jnp.float32),
            ((seq_count, block_len, HEADS * DV), jnp.bfloat16),
        ),
        [values, values],
        seq_count,
        4,
    )


def mixer_output_back(first, mixer_out, reach, gated_grad, gates, head_gain, decay):
    seq_count, block_len = reach.shape[:2]

    def kernel(
        first_ref,
        mixed,
        reach_ref,
        grad_ref,
        gate,
        gain,
        decay_ref,
        out_grad,
        gate_grad,
        term,
        gain_grad,
    ):
        result, grad = mixed[0], grad_ref[0]
        rms = lax.rsqrt(jnp.mean(result * result, axis=-1, keepdims=True) + epsilon)
        value = gate[0].astype(jnp.float32)
        sig = jax.nn.sigmoid(value)
        inner = grad * (value * sig)
        normed = result * rms
        gate_grad[0] = (
            grad * (normed * gain[...]) * sig * (1.0 + value * (1.0 - sig))
        ).astype(jnp.bfloat16)
        gain_grad[0, 0] = jnp.sum(inner * normed, axis=0, keepdims=True)
        scaled = inner * gain[...]
        grad_out = rms * (
            scaled - normed * rms * jnp.mean(scaled * result, axis=-1, keepdims=True)
        )
        out_grad[0] = grad_out
        term[0] = packed_rows(split_dot(reach_ref[0], grad_out, TN), decay_ref[0, 0])

    values = value_spec(block_len)
    return launch(
        kernel,
        (first, mixer_out, reach, gated_grad, gates, head_gain, decay),
        [values, key_spec(block_len), values, values]
        + [pl.BlockSpec((1, DV), lambda s, h, first: (0, 0)), decay_spec],
        (
            ((seq_count, block_len, HEADS * DV), jnp.float32),
            ((seq_count, block_len, HEADS * DV), jnp.bfloat16),
            ((GROUP, DK + EXTRA, DV), jnp.bfloat16),
            ((seq_count, HEADS, 1, DV), jnp.float32),
        ),
        [values, values, pair_spec(DK + EXTRA)]
        + [pl.BlockSpec((1, 1, 1, DV), lambda s, h, first: (s, h, 0, 0))],
        seq_count,
        5,
    )


def conv_back(grad, found, taps, pos, starts, block_len):
    wide, total, sig = found
    grad = grad * sig * (1.0 + total * (1.0 - sig))
    zeros = jnp.zeros((HALO, grad.shape[1]), jnp.float32)
    spread_grad, tap_grads = None, []
    for tap in range(CONV):
        masked = grad if tap == 0 else grad * (pos - tap >= starts).astype(jnp.float32)
        source = wide[HALO - tap : HALO - tap + block_len]
        tap_grads.append(jnp.sum(masked * source, axis=0, keepdims=True))
        padded = jnp.concatenate([zeros, masked * taps[tap : tap + 1, :], zeros], axis=0)
        part = padded[tap : tap + HALO + block_len]
        spread_grad = part if spread_grad is None else spread_grad + part
    return spread_grad, jnp.concatenate(tap_grads, axis=0)


def mixer_backward(first, wide_mixed, conv_weight, logits, starts, out_grad, incoming, outgoing):
    seq_count, block_len = starts.shape[:2]

    def kernel(first_ref, block, taps, logit_ref, start_ref, *refs):
        grad_ref, in_ref, end_ref, main, edge, tail, tap_grad, dlogit, bias = refs
        first, starts = first_ref[0], start_ref[0]
        pos, found, query, key, value = activations(block, taps, starts, first, block_len)
        logit = logit_ref[0]
        log_decay = decays(logit)
        count = block_len // WIDE
        spans, states = [], [in_ref[0].astype(jnp.float32)]
        for index in range(count):
            span = Span(index, first, query, key, value, log_decay, starts, pos)
            spans.append(span)
            if index + 1 < count:
                states.append(span.next_state(states[-1]))
        later = end_ref[0].astype(jnp.float32)
        query_grads, key_grads, value_grads, decay_grads = [], [], [], []
        for index in range(count)[::-1]:
            span, state = spans[index], states[index]
            grad = grad_ref[0, span.rows]
            score_grad = jnp.where(span.allowed, split_dot(grad, span.value, NT), 0.0)
            query_grad = split_dot(score_grad, span.key_centred, NN) * span.to_query
            query_grad = query_grad + split_dot(grad, state, NT) * span.from_start
            end_grad = split_dot(span.value, later, NT)
            key_grad = split_dot(score_grad, span.query_centred, TN) * span.to_key
            key_grad = key_grad + end_grad * span.to_end
            value_grad = split_dot(span.scores(), grad, TN) + split_dot(span.key_end, later, NN)
            kept = unit_dot(jnp.ones((8, DV), jnp.float32), state * later, NT)[:1]
            total_grad = jnp.sum(end_grad * span.key_end, axis=0, keepdims=True)
            total_grad = total_grad + kept * jnp.exp(span.total) * span.kept
            cum_grad = span.query * query_grad - span.key * key_grad
            decay_grads.append(unit_dot(span.upper, cum_grad, NN) + total_grad)
            query_grads.append(query_grad)
            key_grads.append(key_grad)
            value_grads.append(value_grad)
            if index > 0:
                later = later * span.keep_column + split_dot(span.query_start, grad, TN)
        grads = [
            jnp.concatenate(parts[::-1], axis=0) for parts in (query_grads, key_grads, value_grads)
        ]
        grads = jnp.concatenate([grads[0] * DK ** (-0.5)] + grads[1:], axis=1)
        wide_grad, tap_grad[0] = conv_back(grads, found, taps, pos, starts, block_len)
        edge[0] = wide_grad[:HALO]
        main[0] = wide_grad[HALO:].astype(jnp.bfloat16)
        tail[0] = wide_grad[block_len:]
        decay_grad = jnp.concatenate(decay_grads[::-1], axis=0)
        decay_grad = jnp.where(starts < pos, decay_grad, 0.0)
        logit_grad = decay_grad / gate_scale * jax.nn.sigmoid(-logit)
        dlogit[0] = logit_grad
        bias[0, 0] = jnp.sum(logit_grad, axis=0, keepdims=True)

    def heads_spec(rows):
        return pl.BlockSpec((1, rows, PER_HEAD), lambda s, h, first: (s, 0, h))

    width = HEADS * PER_HEAD
    return launch(
        kernel,
        (first, wide_mixed, conv_weight, logits, starts, out_grad, incoming, outgoing),
        mixer_specs(block_len) + [value_spec(block_len), pair_spec(DK), pair_spec(DK)],
        (
            ((seq_count, block_len, width), jnp.bfloat16),
            ((seq_count, HALO, width), jnp.float32),
            ((seq_count, HALO, width), jnp.float32),
            ((seq_count, CONV, width), jnp.float32),
            ((seq_count, block_len, HEADS * DK), jnp.float32),
            ((seq_count, HEADS, 1, DK), jnp.float32),
        ),
        [heads_spec(block_len), heads_spec(HALO), heads_spec(HALO), heads_spec(CONV)]
        + [key_spec(block_len), decay_spec],
        seq_count,
        24,
    )


def bf_dot(left, right):
    return jnp.dot(left, right, preferred_element_type=jnp.float32)


def feed_forward(hidden, out_grad, gain, gate_sources, up_sources, down_left, down_right):
    tokens, width = hidden.shape
    sizes, mine = tuple(size for size, _ in chip_axes()), coordinates()
    block_rows, inner = gate_sources[0][0].shape[3:]
    count, tile = len(gate_sources), 256
    half = width // 2
    steps = inner // tile

    def kernel(me, hid, grad, gain_ref, wl, wr, *refs):
        gate_refs, up_refs, refs = refs[:count], refs[count : 2 * count], refs[2 * count :]
        out, back, back_low, normed, act, gate_back, up_back, gain_back = refs[:8]
        total, turned, gate_held, up_held = refs[8:]
        step = pl.program_id(0)
        w_gate = assemble(gate_held, gate_refs, gate_sources, me, 2, 1)
        w_up = assemble(up_held, up_refs, up_sources, me, 1, 2)

        @pl.when(step == 0)
        def _():
            value = hid[...]
            rms = lax.rsqrt(jnp.mean(value * value, axis=-1, keepdims=True) + epsilon)
            normed[...] = (value * rms * gain_ref[...]).astype(jnp.bfloat16)
            total[...] = jnp.zeros_like(total)
            turned[...] = jnp.zeros_like(turned)

        source, low = normed[...], grad[...]
        gate, up = bf_dot(source, w_gate), bf_dot(source, w_up)
        inner_grad = nt_dot(low[:, :half], wl[...]) + nt_dot(low[:, half:], wr[...])
        sig = jax.nn.sigmoid(gate)
        silu = gate * sig
        active = (silu * up).astype(jnp.bfloat16)
        gate_grad = (inner_grad * up * sig * (1.0 + gate * (1.0 - sig))).astype(jnp.bfloat16)
        up_grad = (inner_grad * silu).astype(jnp.bfloat16)
        act[...], gate_back[...], up_back[...] = active, gate_grad, up_grad
        total[:, :half] += bf_dot(active, wl[...])
        total[:, half:] += bf_dot(active, wr[...])
        turned[...] += nt_dot(gate_grad, w_gate) + nt_dot(up_grad, w_up)

        @pl.when(step == steps - 1)
        def _():
            value, back_in = hid[...], turned[...]
            rms = lax.rsqrt(jnp.mean(value * value, axis=-1, keepdims=True) + epsilon)
            out[...] = value + total[...]
            gain_back[...] = jnp.sum(back_in * value * rms, axis=0, keepdims=True)
            result = grad[...].astype(jnp.float32) + rms_back(back_in, value, rms, gain_ref[...])
            back[...] = result
            back_low[...] = result.astype(jnp.bfloat16)

    def whole(rows, columns):
        return pl.BlockSpec((rows, columns), lambda i, me: (0, 0))

    along = pl.BlockSpec((tile, half), lambda i, me: (i, 0))
    inner_spec = pl.BlockSpec((tokens, tile), lambda i, me: (0, i))
    inner_shape = jax.ShapeDtypeStruct((tokens, inner), jnp.bfloat16)
    arrays = [array for array, _, _ in gate_sources + up_sources]
    held = pltpu.VMEM(sizes + (block_rows, tile), jnp.bfloat16)
    return pl.pallas_call(
        kernel,
        out_shape=[
            jax.ShapeDtypeStruct((tokens, width), jnp.float32),
            jax.ShapeDtypeStruct((tokens, width), jnp.float32),
            jax.ShapeDtypeStruct((tokens, width), jnp.bfloat16),
            jax.ShapeDtypeStruct((tokens, width), jnp.bfloat16),
            inner_shape,
            inner_shape,
            inner_shape,
            jax.ShapeDtypeStruct((1, width), jnp.float32),
        ],
        grid_spec=pltpu.PrefetchScalarGridSpec(
            num_scalar_prefetch=1,
            grid=(steps,),
            in_specs=[whole(tokens, width), whole(tokens, width), whole(1, width), along, along]
            + [tile_spec(array, tile, lambda i, me: (0, 0, 0, 0, i)) for array in arrays],
            out_specs=[whole(tokens, width)] * 4 + [inner_spec] * 3 + [whole(1, width)],
            scratch_shapes=[
                pltpu.VMEM((tokens, width), jnp.float32),
                pltpu.VMEM((tokens, width), jnp.float32),
                held,
                held,
            ],
        ),
        compiler_params=pltpu.CompilerParams(vmem_limit_bytes=58 * 2**20),
        cost_estimate=takes(28),
    )(mine, hidden, out_grad, gain, down_left, down_right, *arrays)


def nt_dot(left, right):
    return lax.dot_general(left, right, (NT, ((), ())), preferred_element_type=jnp.float32)


def rms_back(grad_normed, source, inv_rms, gain_vec):
    scaled = grad_normed * gain_vec
    return inv_rms * (
        scaled - source * inv_rms * inv_rms * jnp.mean(scaled * source, axis=-1, keepdims=True)
    )


def local(
    inputs,
    doc_start,
    norm_gain,
    w_in,
    conv_weight,
    w_low,
    w_high,
    gate_bias,
    head_gain,
    w_out,
    ffn_gain,
    w_gate_up,
    w_down,
    out_grad,
):
    seq_count, block_len, model_width = inputs.shape
    row_count = seq_count * block_len
    key_width = HEADS * DK
    value_width = HEADS * DV
    conv_width = 2 * key_width + value_width
    block_start = lax.axis_index("seq") * block_len
    half = model_width // 2
    first_shard = by_head(w_in[:, :conv_width])
    taps = by_head(conv_weight)
    rest_shard = jnp.concatenate([w_in[:, conv_width:], w_out, w_down], axis=0)
    rest_cuts = [w_in.shape[0], w_out.shape[0], w_down.shape[0]]
    place = jnp.stack([block_start, lax.axis_index("seq") % GROUP]).astype(jnp.int32)
    starts = doc_start[:, :, None]
    gain_row = head_gain[None, :]
    axes = chip_axes()

    fast = gather_levels(first_shard)
    edge = shifted(inputs[:, block_len - HALO :, :], 1)
    wide = jnp.concatenate([edge, inputs], axis=1).astype(jnp.float32)
    wide_rms = lax.rsqrt(jnp.mean(wide * wide, axis=-1, keepdims=True) + epsilon)
    wide_normed = (wide * wide_rms * norm_gain).astype(jnp.bfloat16)
    layer_in = wide[:, HALO:].reshape(row_count, model_width)
    inv_rms = wide_rms[:, HALO:].reshape(row_count, 1)
    fast, wide_normed, rest_shard = together(fast, wide_normed, rest_shard)
    rest = gather_levels(rest_shard)
    fast = gather_first(fast)
    normed = wide_normed[:, HALO:].reshape(row_count, model_width)
    wide_rows = wide_normed.reshape(-1, model_width)
    lowrank = bf_dot(normed, w_low)
    gate_logit = (
        jnp.dot(lowrank, w_high, precision=highest, preferred_element_type=jnp.float32) + gate_bias
    )
    fast, gate_logit, rest[1] = together(fast, gate_logit, rest[1])
    fast = gather_second(fast)
    fast, rest[2], wide_shard = together(fast, rest[2], w_gate_up)
    fast = gather_cores(fast)
    wide_pieces = gather_levels(wide_shard)
    wide_mixed = projected(wide_rows, *[[(own, 0, 0), (other, 1, 0)] for own, other in fast])
    wide_mixed = wide_mixed.reshape(seq_count, HALO + block_len, conv_width)
    wide_mixed, rest = together(wide_mixed, rest)
    rest = gather_first(rest)
    logits = gate_logit.reshape(seq_count, block_len, key_width)
    local_out, reach, local_state, block_decay = mixer_forward(
        place, wide_mixed, taps, logits, starts
    )
    local_state, rest, wide_pieces[1] = together(local_state, rest, wide_pieces[1])
    got, _ = exchanged(local_state)
    got, rest = together(got, rest)
    rest = gather_second(rest)
    beyond = shifted(composed(place, got, False), GROUP)
    incoming = composed(place, got, False, beyond)
    incoming, rest, wide_pieces = together(incoming, rest, wide_pieces)
    wide_pieces = gather_first(wide_pieces)
    rest = gather_cores(rest)
    incoming, _ = exchanged(incoming)
    incoming, rest, wide_pieces = together(incoming, rest, wide_pieces)
    crossed = gather_second(wide_pieces)
    early = [swapped(pieces[0], 1) for pieces in crossed]
    incoming, fast = together(incoming, fast)
    [(left_full, right_full)] = gather_done(fast, [first_shard.shape[0]])
    (g_left, g_right), (out_left, out_right), (down_left, down_right) = gather_done(rest, rest_cuts)
    gate_cols = jnp.concatenate([bf_dot(normed, g_left), bf_dot(normed, g_right)], axis=1)
    gates = gate_cols.astype(jnp.bfloat16).reshape(seq_count, block_len, value_width)
    mixer_out, gated = mixer_output(place, local_out, reach, incoming, gates, gain_row)
    gated = gated.reshape(row_count, value_width)
    hidden_one = layer_in + jnp.concatenate(
        [bf_dot(gated, out_left), bf_dot(gated, out_right)], axis=1
    )
    hidden_one, crossed, early = together(hidden_one, crossed, early)
    gate_sources, up_sources = core_sources(crossed, early)
    out_rows_low = out_grad.reshape(row_count, model_width)
    (
        layer_out,
        hidden_grad,
        hidden_low,
        ffn_in,
        activation,
        gate_grad,
        up_grad,
        ffn_gain_row,
    ) = feed_forward(
        hidden_one, out_rows_low, ffn_gain[None, :], gate_sources, up_sources, down_left, down_right
    )
    gated_grad = nt_dot(hidden_low[:, :half], out_left) + nt_dot(hidden_low[:, half:], out_right)
    gated_grad = gated_grad.reshape(seq_count, block_len, value_width)
    mixer_grad, gate_vals_grad, state_term, head_gain_grad = mixer_output_back(
        place, mixer_out, reach, gated_grad, gates, gain_row, block_decay
    )
    gate_vals_grad = gate_vals_grad.reshape(row_count, value_width)

    state_term, gated, ffn_in, activation = together(state_term, gated, ffn_in, activation)
    got, (out_terms, wide_terms, down_terms) = exchanged(
        state_term,
        (
            (lambda: grad_products(gated, hidden_low),),
            (lambda _: grad_products(ffn_in, gate_grad, up_grad),),
            (lambda _: grad_products(activation, out_rows_low),),
        ),
    )
    wide_terms = cores_send([wide_terms])
    beyond = shifted(composed(place, got, True), -GROUP)
    g_terms = grad_products(normed, gate_vals_grad)
    beyond, g_terms = together(beyond, g_terms)
    outgoing = composed(place, got, True, beyond)
    outgoing, wide_terms = together(outgoing, wide_terms)
    wide_terms = phase_send(wide_terms, 0)
    rest_terms = cores_send([g_terms, out_terms, down_terms])
    outgoing, _ = exchanged(outgoing)
    outgoing, wide_terms, rest_terms = together(outgoing, wide_terms, rest_terms)
    wide_terms = phase_send(wide_terms, 1)
    rest_terms = phase_send(rest_terms, 0)
    backs = mixer_backward(
        place, wide_mixed, taps, logits, starts, mixer_grad, incoming, outgoing
    )
    backs, wide_terms = together(backs, wide_terms)
    wide_own, wide_last = levels_send(wide_terms)
    mixed_grad, back_edge, back_tail, tap_grads, logit_grad, gate_bias_grad = backs
    back_edge = shifted(back_edge.astype(jnp.bfloat16), -1).astype(jnp.float32)
    mixed_grad = lax.dynamic_update_slice(
        mixed_grad, (back_tail + back_edge).astype(jnp.bfloat16), (0, block_len - HALO, 0)
    )
    mixed_grad = mixed_grad.reshape(row_count, conv_width)
    mixed_grad, rest_terms = together(mixed_grad, rest_terms)
    rest_terms = phase_send(rest_terms, 1)
    fast_terms = grad_products(normed, mixed_grad)
    fast_terms, wide_last[0] = together(fast_terms, wide_last[0])
    fast_terms = cores_send([fast_terms])
    small_rows, lowrank_grad = small_packed(
        logit_grad.reshape(row_count, key_width),
        lowrank,
        w_high,
        normed,
        tap_grads,
        gate_bias_grad.reshape(seq_count, key_width),
        head_gain_grad,
        ffn_gain_row,
    )
    normed_grad = (
        nt_dot(mixed_grad[:, : conv_width // 2], left_full)
        + nt_dot(mixed_grad[:, conv_width // 2 :], right_full)
        + nt_dot(gate_vals_grad[:, :half], g_left)
        + nt_dot(gate_vals_grad[:, half:], g_right)
        + nt_dot(lowrank_grad, w_low)
    )
    norm_gain_grad = jnp.sum(normed_grad * layer_in * inv_rms, axis=0)
    input_grad = hidden_grad + rms_back(normed_grad, layer_in, inv_rms, norm_gain)
    small_rows = lax.dynamic_update_slice(small_rows, norm_gain_grad[None, :], (34, 0))
    small_rows, rest_terms, fast_terms, input_grad, wide_last[1] = together(
        small_rows, rest_terms, fast_terms, input_grad, wide_last[1]
    )
    fast_terms = phase_send(fast_terms, 0)
    rest_own, rest_last = levels_send(rest_terms)
    small_rows = spread(small_rows, axes[3])
    fast_terms, small_rows, wide_last[2], rest_last[0] = together(
        fast_terms, small_rows, wide_last[2], rest_last[0]
    )
    fast_terms = phase_send(fast_terms, 1)
    small_rows = spread(sum(small_rows), axes[2])
    fast_terms, small_rows, rest_last[1] = together(fast_terms, small_rows, rest_last[1])
    fast_own, fast_last = levels_send(fast_terms)
    small_rows = spread(sum(small_rows), axes[1])
    small_rows, fast_last[0], rest_last[2] = together(small_rows, fast_last[0], rest_last[2])
    small_parts = spread(sum(small_rows), axes[0])
    norm_gain_grad, conv_weight_grad, w_low_grad, w_high_grad, *rows_found = small_unpacked(
        small_parts, key_width, w_high.shape[0]
    )
    gate_bias_grad, head_gain_grad, ffn_gain_grad = [row[0] for row in rows_found]
    rest_grad = reduced(rest_own, rest_last)
    w_gate_up_grad = reduced(wide_own, wide_last)
    fast_grad = by_kind(reduced(fast_own, fast_last))
    ends = [rest_cuts[0], rest_cuts[0] + rest_cuts[1]]
    w_in_grad = jnp.concatenate([fast_grad, rest_grad[: ends[0]]], axis=1)
    w_out_grad = rest_grad[ends[0] : ends[1]]
    w_down_grad = rest_grad[ends[1] :]
    return (
        layer_out.reshape(seq_count, block_len, model_width),
        input_grad.reshape(seq_count, block_len, model_width),
        norm_gain_grad[0],
        w_in_grad,
        conv_weight_grad,
        w_low_grad.T,
        w_high_grad,
        gate_bias_grad,
        head_gain_grad,
        w_out_grad,
        ffn_gain_grad,
        w_gate_up_grad,
        w_down_grad,
    )


def solution(mesh):
    placed = (
        P(None, "seq", None),
        P(None, "seq"),
        P(),
        P("seq", None),
        P(),
        P(),
        P(),
        P(),
        P(),
        P("seq", None),
        P(),
        P("seq", None),
        P("seq", None),
        P(None, "seq", None),
    )
    return jax.shard_map(
        local,
        mesh=mesh,
        in_specs=placed,
        out_specs=(
            P(None, "seq", None),
            P(None, "seq", None),
            P(),
            P("seq", None),
            P(),
            P(),
            P(),
            P(),
            P(),
            P("seq", None),
            P(),
            P("seq", None),
            P("seq", None),
        ),
        check_vma=False,
    )
```

```python
import jax
import jax.numpy as jnp
from jax import lax
from jax.experimental import pallas as pl
from jax.experimental.pallas import tpu as pltpu
from jax.sharding import PartitionSpec as P

HEADS = 4
DK = 128
DV = 256
FF = 2816
WIDE = 128
CONV = 4


epsilon = 1e-06
gate_scale = 16.0
highest = lax.Precision.HIGHEST


GROUP = 8
HALO = 8
EXTRA = 16
SMALL = 40
PER_HEAD = 2 * DK + DV


def chip_axes():
    count = lax.axis_size("seq")
    sides = {16: (4, 2, 2), 64: (4, 4, 4)}.get(count // 2, (count // 2, 1, 1))
    return (
        (sides[0], 2 * sides[1] * sides[2]),
        (sides[1], 2 * sides[2]),
        (sides[2], 2),
        (2, 1),
    )


def swapped(array, mask):
    count = lax.axis_size("seq")
    return lax.ppermute(array, "seq", [(i, i ^ mask) for i in range(count)])


def shifted(array, by):
    count = lax.axis_size("seq")
    pairs = [(i, i + by) for i in range(count) if 0 <= i + by < count]
    return lax.ppermute(array, "seq", pairs)


def spread(block, axis):
    size, stride = axis
    return [block] + [swapped(block, step * stride) for step in range(1, size)]


def takes(micros):
    return pl.CostEstimate(flops=int(micros * 1e9), bytes_accessed=0, transcendentals=0)


def coordinates():
    mine = lax.axis_index("seq")
    return jnp.stack([(mine // stride) % size for size, stride in chip_axes()]).astype(jnp.int32)


def placed_blocks(sources, one, two, cuts):
    axes = chip_axes()
    sizes = tuple(size for size, _ in axes)
    depth, mine = sizes[0], coordinates()
    (rows, columns), kind = sources[0][0].shape[3:], sources[0][0].dtype

    def target(core, second, first, me):
        spot = [0, 0, 0, 0]
        spot[one] = jnp.bitwise_xor(first, me[one])
        spot[two] = jnp.bitwise_xor(second, me[two])
        spot[3] = jnp.bitwise_xor(core, me[3])
        return tuple(spot) + (0, 0)

    def source(mine_core, base, extent):
        def index(core, second, first, me):
            step = core * sizes[two] + second - mine_core * sizes[two] - base
            early, late = step < 0, step >= extent
            held = jnp.where(early, 0, jnp.where(late, extent - 1, step))
            return (
                held,
                jnp.where(early, 0, jnp.where(late, sizes[one] - 1, first)),
                0,
                0,
                0,
            )

        return index

    def kernel(me, *refs):
        pieces, outs = refs[: len(sources)], refs[len(sources) :]
        step = pl.program_id(0) * sizes[two] + pl.program_id(1)
        for piece, (array, core, base) in zip(pieces, sources):
            begin = core * sizes[two] + base

            @pl.when((step >= begin) & (step < begin + array.shape[0]))
            def _():
                for level in range(depth):
                    block, start = piece[0, 0, level], 0
                    for out, cut in zip(outs, cuts):
                        out[jnp.bitwise_xor(me[0], level), 0, 0, 0] = block[start : start + cut]
                        start += cut

    found = pl.pallas_call(
        kernel,
        out_shape=[jax.ShapeDtypeStruct(sizes + (cut, columns), kind) for cut in cuts],
        grid_spec=pltpu.PrefetchScalarGridSpec(
            num_scalar_prefetch=1,
            grid=(2, sizes[two], sizes[one]),
            in_specs=[
                pl.BlockSpec((1, 1, depth, rows, columns), source(core, base, array.shape[0]))
                for array, core, base in sources
            ],
            out_specs=[pl.BlockSpec((depth, 1, 1, 1, cut, columns), target) for cut in cuts],
        ),
        compiler_params=pltpu.CompilerParams(vmem_limit_bytes=40 * 2**20),
        cost_estimate=takes(1.0 + rows * columns * 5e-5),
    )(mine, *[array for array, _, _ in sources])
    return [array.reshape(-1, columns) for array in found]


def together(*values):
    return lax.optimization_barrier(values)


def gather_levels(shard):
    return spread(shard, chip_axes()[0])


def gather_first(levels):
    stacked = levels if isinstance(levels, jax.Array) else jnp.stack(levels)
    half = stacked.shape[2] // 2
    axes = chip_axes()
    return [spread(stacked[..., :half], axes[2]), spread(stacked[..., half:], axes[1])]


def gather_second(sides):
    axes = chip_axes()
    return [spread(jnp.stack(sides[0]), axes[1]), spread(jnp.stack(sides[1]), axes[2])]


def gather_cores(crossed):
    found = []
    for pieces in crossed:
        own = jnp.stack(pieces)
        found.append([own, swapped(own, 1)])
    return found


def gather_done(pairs, cuts):
    halves = [
        placed_blocks([(own, 0, 0), (other, 1, 0)], one, two, cuts)
        for (own, other), one, two in zip(pairs, (2, 1), (1, 2))
    ]
    return list(zip(*halves))


def core_sources(crossed, early):
    halves = []
    for pieces, before in zip(crossed, early):
        sources = []
        for step, piece in enumerate(pieces):
            other = before if step == 0 else swapped(piece, 1)
            sources.extend([(piece[None], 0, step), (other[None], 1, step)])
        halves.append(sources)
    return halves


def assemble(held, refs, sources, me, one, two):
    for ref, (array, core, base) in zip(refs, sources):
        for second in range(array.shape[0]):
            for first in range(array.shape[1]):
                for level in range(array.shape[2]):
                    spot = [jnp.bitwise_xor(me[0], level), 0, 0, jnp.bitwise_xor(me[3], core)]
                    spot[one] = jnp.bitwise_xor(me[one], first)
                    spot[two] = jnp.bitwise_xor(me[two], base + second)
                    held[tuple(spot)] = ref[second, first, level]
    return held[...].reshape(-1, held.shape[-1])


def tile_spec(array, tile, index):
    return pl.BlockSpec(array.shape[:4] + (tile,), index)


def projected(rows, sources_a, sources_b):
    sizes, mine = tuple(size for size, _ in chip_axes()), coordinates()
    tokens, width = rows.shape
    block_rows, half = sources_a[0][0].shape[3:]
    tile = 256
    tiles = half // tile

    def kernel(me, row_ref, *refs):
        refs_a = refs[: len(sources_a)]
        refs_b = refs[len(sources_a) : -2]
        out, held = refs[-2:]

        @pl.when(pl.program_id(0) == 0)
        def _():
            assemble(held, refs_a, sources_a, me, 2, 1)

        @pl.when(pl.program_id(0) == 1)
        def _():
            assemble(held, refs_b, sources_b, me, 1, 2)

        full = held[...].reshape(width, tile)
        out[...] = bf_dot(row_ref[...], full).astype(jnp.bfloat16)

    def at_a(part, i, me):
        return (0, 0, 0, 0, jnp.where(part == 0, i, tiles - 1))

    def at_b(part, i, me):
        return (0, 0, 0, 0, jnp.where(part == 0, 0, i))

    return pl.pallas_call(
        kernel,
        out_shape=jax.ShapeDtypeStruct((tokens, 2 * half), jnp.bfloat16),
        grid_spec=pltpu.PrefetchScalarGridSpec(
            num_scalar_prefetch=1,
            grid=(2, tiles),
            in_specs=[pl.BlockSpec((tokens, width), lambda part, i, me: (0, 0))]
            + [tile_spec(array, tile, at_a) for array, _, _ in sources_a]
            + [tile_spec(array, tile, at_b) for array, _, _ in sources_b],
            out_specs=pl.BlockSpec((tokens, tile), lambda part, i, me: (0, part * tiles + i)),
            scratch_shapes=[pltpu.VMEM(sizes + (block_rows, tile), jnp.bfloat16)],
        ),
        compiler_params=pltpu.CompilerParams(vmem_limit_bytes=40 * 2**20),
        cost_estimate=takes(6),
    )(mine, rows, *[array for array, _, _ in sources_a + sources_b])


def grad_products(left, right_a, right_b=None):
    sizes = tuple(size for size, _ in chip_axes())
    strides = tuple(stride for _, stride in chip_axes())
    (tokens, features), columns = left.shape, right_a.shape[1]
    if right_b is None:
        columns = columns // 2
    count, mine = lax.axis_size("seq"), coordinates()
    rows = features // count
    tile = 512 if columns % 512 == 0 and features <= 1024 else 256
    chunks = next(c for c in (4, 2, 1) if features // c % 128 == 0)
    chunk = features // chunks

    def kernel(me, left_ref, a_ref, b_ref, away_a, keep_a, away_b, keep_b, flipped):
        @pl.when(pl.program_id(0) == 0)
        def _():
            flipped[...] = left_ref[...].T

        def products(odd):
            for right, away, keep, order in (
                (a_ref, away_a, keep_a, (2, 1, 0)),
                (b_ref, away_b, keep_b, (1, 2, 0)),
            ):
                for part in range(chunks):
                    full = jnp.dot(
                        flipped[part * chunk : (part + 1) * chunk],
                        right[...],
                        preferred_element_type=jnp.float32,
                    )
                    for start in range(0, chunk, rows):
                        device = (part * chunk + start) // rows
                        spot = tuple(
                            jnp.bitwise_xor(device // strides[axis] % sizes[axis], me[axis])
                            for axis in order
                        )
                        target = keep if device % 2 == odd else away
                        target[spot] = full[start : start + rows].astype(jnp.bfloat16)

        @pl.when(me[3] == 0)
        def _():
            products(0)

        @pl.when(me[3] == 1)
        def _():
            products(1)

    def result(one, two):
        shape = (sizes[one], sizes[two], sizes[0], rows)
        return (
            jax.ShapeDtypeStruct(shape + (columns,), jnp.bfloat16),
            pl.BlockSpec(shape + (tile,), lambda i, me: (0, 0, 0, 0, i)),
        )

    results = [result(2, 1), result(2, 1), result(1, 2), result(1, 2)]
    skip = columns // tile if right_b is None else 0
    right_b = right_a if right_b is None else right_b
    return pl.pallas_call(
        kernel,
        out_shape=[shape for shape, _ in results],
        grid_spec=pltpu.PrefetchScalarGridSpec(
            num_scalar_prefetch=1,
            grid=(columns // tile,),
            in_specs=[
                pl.BlockSpec((tokens, features), lambda i, me: (0, 0)),
                pl.BlockSpec((tokens, tile), lambda i, me: (0, i)),
                pl.BlockSpec((tokens, tile), lambda i, me: (0, i + skip)),
            ],
            out_specs=[spec for _, spec in results],
            scratch_shapes=[pltpu.VMEM((features, tokens), jnp.bfloat16)],
        ),
        compiler_params=pltpu.CompilerParams(vmem_limit_bytes=48 * 2**20),
        cost_estimate=takes(1.5 + features * columns * 4.5e-6),
    )(mine, left, right_a, right_b)


def total_of(groups):
    parts = []
    for refs, lead in groups:
        rows = [ref[(0,) * lead].astype(jnp.float32) for ref in refs]
        parts.append(jnp.concatenate(rows, axis=0) if len(rows) > 1 else rows[0])
    return sum(parts[1:], parts[0])


def flat_terms(terms):
    return [(since, arrays) for since, group in enumerate(terms) for arrays in group]


def regrouped(refs, flat):
    groups, at = [], 0
    for since, arrays in flat:
        groups.append((refs[at : at + len(arrays)], since))
        at += len(arrays)
    return groups, at


def phase_sums(pair, phase, step):
    flats = [flat_terms(terms) for terms in pair]
    depth = chip_axes()[0][0]
    second = chip_axes()[1][0] if phase == 0 else 1
    rows = sum(array.shape[-2] for array in flats[0][0][1])
    columns = flats[0][0][1][0].shape[-1]
    lead = 2 - phase

    def index(since):
        def found(i, j):
            spot = [0 if dim < phase else step if dim == phase else (i, j)[dim - 1] for dim in range(3)]
            return tuple(spot[since:]) + (0, 0)

        return found

    def kernel(*refs):
        ins, outs = refs[:-2], refs[-2:]
        at = 0
        for flat, out in zip(flats, outs):
            groups, used = regrouped(ins[at:], flat)
            at += used
            total = total_of([(part, 3 - since) for part, since in groups])
            out[(0,) * lead] = total.astype(jnp.bfloat16)

    arrays = [(array, since) for flat in flats for since, group in flat for array in group]
    shape = ((second, depth) if phase == 0 else (depth,)) + (rows, columns)
    out_spec = pl.BlockSpec(
        (1,) * lead + (rows, columns), lambda i, j: ((i, j) if phase == 0 else (j,)) + (0, 0)
    )
    return pl.pallas_call(
        kernel,
        out_shape=[jax.ShapeDtypeStruct(shape, jnp.bfloat16)] * 2,
        grid=(second, depth),
        in_specs=[
            pl.BlockSpec((1,) * (3 - since) + array.shape[-2:], index(since))
            for array, since in arrays
        ],
        out_specs=[out_spec] * 2,
        compiler_params=pltpu.CompilerParams(vmem_limit_bytes=32 * 2**20),
        cost_estimate=takes(3),
    )(*[array for array, _ in arrays])


def level_sums(pair):
    flats = [flat_terms(terms) for terms in pair]
    depth = chip_axes()[0][0]
    rows = sum(array.shape[-2] for array in flats[0][0][1])
    columns = flats[0][0][1][0].shape[-1]

    def kernel(*refs):
        ins, outs = refs[:-depth], refs[-depth:]
        at = 0
        for side, flat in enumerate(flats):
            groups, used = regrouped(ins[at:], flat)
            at += used
            cut = slice(side * columns, (side + 1) * columns)
            for level in range(depth):
                parts = []
                for part, since in groups:
                    spot = (0,) * (2 - since) + (level,)
                    values = [ref[spot].astype(jnp.float32) for ref in part]
                    parts.append(
                        jnp.concatenate(values, axis=0) if len(values) > 1 else values[0]
                    )
                total = sum(parts[1:], parts[0])
                outs[level][:, cut] = total.astype(outs[level].dtype)

    arrays = [(array, since) for flat in flats for since, group in flat for array in group]

    def spec(array, since):
        lead = (1,) * (2 - since) + (depth,)
        return pl.BlockSpec(lead + array.shape[-2:], lambda i: (0,) * (len(lead) + 2))

    shape = (rows, 2 * columns)
    return pl.pallas_call(
        kernel,
        out_shape=[jax.ShapeDtypeStruct(shape, jnp.float32)]
        + [jax.ShapeDtypeStruct(shape, jnp.bfloat16)] * (depth - 1),
        grid=(1,),
        in_specs=[spec(array, since) for array, since in arrays],
        out_specs=[pl.BlockSpec(shape, lambda i: (0, 0))] * depth,
        compiler_params=pltpu.CompilerParams(vmem_limit_bytes=40 * 2**20),
        cost_estimate=takes(3),
    )(*[array for array, _ in arrays])


def cores_send(products):
    found = []
    for keep, which in ((1, 0), (3, 2)):
        aways = [part[which] for part in products]
        away = jnp.concatenate(aways, axis=3) if len(aways) > 1 else aways[0]
        found.append([[[part[keep] for part in products], [swapped(away, 1)]]])
    return found


def phase_parts(pair, phase):
    return [phase_sums(pair, phase, step) for step in range(1, chip_axes()[2][0])]


def phase_swap(pair, phase, parts):
    axes, received = chip_axes(), [[], []]
    for step, sides in enumerate(parts):
        for side, part in enumerate(sides):
            stride = axes[((2, 1), (1, 2))[side][phase]][1]
            received[side].append([swapped(part, (step + 1) * stride)])
    return [terms + [parts] for terms, parts in zip(pair, received)]


def phase_send(pair, phase):
    return phase_swap(pair, phase, phase_parts(pair, phase))


def levels_send(sums):
    own, *parts = sums
    stride = chip_axes()[0][1]
    return own, [swapped(part, (step + 1) * stride) for step, part in enumerate(parts)]


def reduced(own, found):
    return sum((part.astype(jnp.float32) for part in found), own)


def small_packed(logit_grad, lowrank, w_high, normed, tap_grads, bias, head_gain, ffn_gain):
    tokens, keys = logit_grad.shape
    width, rank = normed.shape[1], w_high.shape[0]

    def kernel(grad_ref, low_ref, high_ref, normed_ref, taps, bias_ref, head, ffn, out, low_grad):
        grad = grad_ref[...]
        back = split_dot(grad, high_ref[...], NT).astype(jnp.bfloat16)
        low_grad[...] = back
        out[:rank] = lax.dot_general(
            back, normed_ref[...], (TN, ((), ())), preferred_element_type=jnp.float32
        )
        tap = jnp.sum(taps[...], axis=0)
        out[rank : rank + CONV] = tap[:, :width]
        out[rank + CONV : rank + 2 * CONV] = tap[:, width:]
        high = split_dot(low_ref[...], grad, TN)
        out[24:32, :keys] = high[:8]
        out[24:32, keys:] = high[8:]
        out[32:40] = jnp.zeros((8, width), jnp.float32)
        out[32:33, :keys] = jnp.sum(bias_ref[...], axis=0, keepdims=True)
        gains = [jnp.sum(head[:, h, 0], axis=0, keepdims=True) for h in range(HEADS)]
        out[32:33, keys : keys + DV] = sum(gains)
        out[33:34] = ffn[...]

    return pl.pallas_call(
        kernel,
        out_shape=[
            jax.ShapeDtypeStruct((SMALL, width), jnp.float32),
            jax.ShapeDtypeStruct((tokens, rank), jnp.bfloat16),
        ],
        compiler_params=pltpu.CompilerParams(vmem_limit_bytes=32 * 2**20),
        cost_estimate=takes(4),
    )(logit_grad, lowrank, w_high, normed, tap_grads, bias, head_gain, ffn_gain)


def small_unpacked(parts, keys, rank):
    width = parts[0].shape[1]

    def kernel(*refs):
        ins, (norm, conv, low, high, bias, head, ffn) = refs[: len(parts)], refs[len(parts) :]
        total = sum((ref[...].astype(jnp.float32) for ref in ins[1:]), ins[0][...])
        low[...] = total[:rank]
        for h in range(HEADS):
            side, at = divmod(h * PER_HEAD, width)
            block = total[rank + side * CONV : rank + (side + 1) * CONV]
            conv[:, h * DK : (h + 1) * DK] = block[:, at : at + DK]
            conv[:, keys + h * DK : keys + (h + 1) * DK] = block[:, at + DK : at + 2 * DK]
            conv[:, 2 * keys + h * DV : 2 * keys + (h + 1) * DV] = block[
                :, at + 2 * DK : at + PER_HEAD
            ]
        high[:8] = total[24:32, :keys]
        high[8:] = total[24:32, keys:]
        bias[...] = total[32:33, :keys]
        head[...] = total[32:33, keys : keys + DV]
        ffn[...] = total[33:34]
        norm[...] = total[34:35]

    shapes = ((1, width), (CONV, 2 * width), (rank, width), (rank, keys))
    shapes += ((1, keys), (1, DV), (1, width))
    return pl.pallas_call(
        kernel,
        out_shape=[jax.ShapeDtypeStruct(shape, jnp.float32) for shape in shapes],
        cost_estimate=takes(2),
    )(*parts)


def by_head(array):
    lead, (keys, values) = array.shape[:-1], (HEADS * DK, HEADS * DV)
    parts = [
        part.reshape(lead + (HEADS, -1))
        for part in (array[..., :keys], array[..., keys : 2 * keys], array[..., 2 * keys :])
    ]
    return jnp.concatenate(parts, axis=-1).reshape(lead + (2 * keys + values,))


def by_kind(array):
    lead = array.shape[:-1]
    array = array.reshape(lead + (HEADS, -1))
    parts = (array[..., :DK], array[..., DK : 2 * DK], array[..., 2 * DK :])
    return jnp.concatenate([part.reshape(lead + (-1,)) for part in parts], axis=-1)


def exchange_step(pieces, at, mask):
    kept = lax.index_in_dim(pieces, 0, at, False)
    return [kept, swapped(lax.index_in_dim(pieces, 1, at, False), mask)]


def exchanged(pieces, fillers=((), (), ())):
    shape, filled = pieces.shape, []
    pieces = pieces.reshape((2, 2, 2) + shape[1:])
    for at, mask, filler in zip((2, 1, 0), (1, 2, 4), fillers):
        pair = exchange_step(pieces, at, mask)
        if filler:
            values = filler[0](*filled[-1:])
            pair, values = together(pair, values)
            filled.append(values)
        pieces = jnp.stack(pair, axis=at)
    return pieces.reshape(shape), filled


def column(row):
    square = jnp.broadcast_to(row, (DK, DK)).T
    return jnp.concatenate([square, square], axis=1)


def packed_rows(state, decay):
    high = decay.astype(jnp.bfloat16)
    low = (decay - high.astype(jnp.float32)).astype(jnp.bfloat16)
    tail = jnp.broadcast_to(jnp.concatenate([high, low], axis=1), (EXTRA, DV))
    return jnp.concatenate([state.astype(jnp.bfloat16), tail], axis=0)


def composed(place, got, backward, beyond=None):
    order = range(GROUP)[::-1] if backward else range(GROUP)

    def kernel(place_ref, got_ref, *refs):
        mine, out = place_ref[1], refs[-1]
        running = jnp.zeros((DK, DV), jnp.float32)
        reach = jnp.ones((DK, DV), jnp.float32)
        far = None if beyond is None else refs[0][...].astype(jnp.float32)
        for index in order:
            spot = jnp.bitwise_xor(mine, index)
            piece = got_ref[spot].astype(jnp.float32)
            if beyond is not None:
                out[spot] = (running + reach * far).astype(jnp.bfloat16)
            tail = piece[DK : DK + 1]
            kept = column(tail[:, :DK] + tail[:, DK:])
            running = kept * running + piece[:DK]
            reach = reach * kept
        if beyond is None:
            out[...] = running.astype(jnp.bfloat16)

    extra = () if beyond is None else (beyond,)
    shape = (DK, DV) if beyond is None else (GROUP, DK, DV)
    return pl.pallas_call(
        kernel,
        out_shape=jax.ShapeDtypeStruct(shape, jnp.bfloat16),
        in_specs=[pl.BlockSpec(memory_space=pltpu.SMEM)]
        + [pl.BlockSpec(memory_space=pltpu.VMEM)] * (1 + len(extra)),
        out_specs=pl.BlockSpec(memory_space=pltpu.VMEM),
        cost_estimate=takes(2),
    )(place, got, *extra)


def split_dot(left, right, dims):
    dims = (dims, ((), ()))
    left_high, right_high = left.astype(jnp.bfloat16), right.astype(jnp.bfloat16)
    left_low = (left - left_high.astype(jnp.float32)).astype(jnp.bfloat16)
    right_low = (right - right_high.astype(jnp.float32)).astype(jnp.bfloat16)

    def one(a, b):
        return lax.dot_general(a, b, dims, preferred_element_type=jnp.float32)

    return one(left_high, right_high) + (one(left_high, right_low) + one(left_low, right_high))


def unit_dot(unit, value, dims):
    high = value.astype(jnp.bfloat16)
    rest = value - high.astype(jnp.float32)
    middle = rest.astype(jnp.bfloat16)
    low = (rest - middle.astype(jnp.float32)).astype(jnp.bfloat16)
    unit = unit.astype(jnp.bfloat16)
    return sum(
        lax.dot_general(unit, part, (dims, ((), ())), preferred_element_type=jnp.float32)
        for part in (low, middle, high)
    )


NN, NT, TN = ((1,), (0,)), ((1,), (1,)), ((0,), (0,))


def activations(block, taps, starts, first, block_len):
    pos = first + lax.broadcasted_iota(jnp.int32, (block_len, 1), 0)
    wide = block[0].astype(jnp.float32)
    total = taps[0:1, :] * wide[HALO:]
    for tap in range(1, CONV):
        usable = (pos - tap >= starts).astype(jnp.float32)
        total = total + taps[tap : tap + 1, :] * wide[HALO - tap : HALO - tap + block_len] * usable
    sig = jax.nn.sigmoid(total)
    active = total * sig
    query, key, value = active[:, :DK], active[:, DK : 2 * DK], active[:, 2 * DK :]
    return pos, (wide, total, sig), query * DK ** (-0.5), key, value


def decays(logit):
    return (jnp.minimum(logit, 0.0) - jnp.log1p(jnp.exp(-jnp.abs(logit)))) / gate_scale


class Span:
    def __init__(self, index, first, query, key, value, decay, starts, pos):
        rows = slice(index * WIDE, (index + 1) * WIDE)
        self.rows, first_pos = rows, first + index * WIDE
        self.query, self.key, self.value = query[rows], key[rows], value[rows]
        decay, starts, pos = decay[rows], starts[rows], pos[rows]
        t = lax.broadcasted_iota(jnp.int32, (WIDE, WIDE), 0)
        u = lax.broadcasted_iota(jnp.int32, (WIDE, WIDE), 1)
        self.lower = (u <= t).astype(jnp.float32)
        self.upper = (u >= t).astype(jnp.float32)
        self.allowed = (u <= t) & (u + first_pos >= starts)
        cum = unit_dot(self.lower, decay, NN)
        self.total = cum[WIDE - 1 :]
        middle = cum[WIDE // 2 - 1 : WIDE // 2]
        self.to_query, self.to_key = jnp.exp(cum - middle), jnp.exp(middle - cum)
        self.carried = (starts < first_pos).astype(jnp.float32)
        self.kept = (starts[WIDE - 1 :] < first_pos).astype(jnp.float32)
        self.from_start = jnp.exp(cum) * self.carried
        self.to_end = jnp.exp(self.total - cum) * (pos >= starts[WIDE - 1 :]).astype(jnp.float32)
        self.query_centred = self.query * self.to_query
        self.key_centred = self.key * self.to_key
        self.query_start = self.query * self.from_start
        self.key_end = self.key * self.to_end
        self.cum = cum
        ones = jnp.ones((WIDE, DV), jnp.float32)
        total_column = unit_dot_right(decay, ones)
        self.keep_column = jnp.exp(total_column) * self.kept

    def scores(self):
        raw = split_dot(self.query_centred, self.key_centred, NT)
        return jnp.where(self.allowed, raw, 0.0)

    def next_state(self, state):
        update = split_dot(self.key_end, self.value, TN)
        return update if state is None else state * self.keep_column + update


def unit_dot_right(value, unit):
    high = value.astype(jnp.bfloat16)
    rest = value - high.astype(jnp.float32)
    middle = rest.astype(jnp.bfloat16)
    low = (rest - middle.astype(jnp.float32)).astype(jnp.bfloat16)
    unit = unit.astype(jnp.bfloat16)
    return sum(
        lax.dot_general(part, unit, (TN, ((), ())), preferred_element_type=jnp.float32)
        for part in (low, middle, high)
    )


def mixer_specs(block_len):
    return [
        pl.BlockSpec((1, HALO + block_len, PER_HEAD), lambda s, h, first: (s, 0, h)),
        pl.BlockSpec((CONV, PER_HEAD), lambda s, h, first: (0, h)),
        pl.BlockSpec((1, block_len, DK), lambda s, h, first: (s, 0, h)),
        pl.BlockSpec((1, block_len, 1), lambda s, h, first: (s, 0, 0)),
    ]


def key_spec(block_len):
    return pl.BlockSpec((1, block_len, DK), lambda s, h, first: (s, 0, h))


def value_spec(block_len):
    return pl.BlockSpec((1, block_len, DV), lambda s, h, first: (s, 0, h))


def pair_spec(rows):
    return pl.BlockSpec(
        (1, rows, DV), lambda s, h, place: (jnp.bitwise_xor(place[1], s * HEADS + h), 0, 0)
    )


decay_spec = pl.BlockSpec((1, 1, 1, DK), lambda s, h, first: (s, h, 0, 0))


def launch(kernel, inputs, in_specs, outputs, out_specs, seq_count, micros):
    return pl.pallas_call(
        kernel,
        out_shape=[jax.ShapeDtypeStruct(shape, kind) for shape, kind in outputs],
        grid_spec=pltpu.PrefetchScalarGridSpec(
            num_scalar_prefetch=1,
            grid=(seq_count, HEADS),
            in_specs=in_specs,
            out_specs=out_specs,
        ),
        compiler_params=pltpu.CompilerParams(vmem_limit_bytes=40 * 2**20),
        cost_estimate=takes(micros),
    )(*inputs)


def mixer_forward(first, wide_mixed, conv_weight, logits, starts):
    seq_count, block_len = starts.shape[:2]

    def kernel(first_ref, block, taps, logit_ref, start_ref, out, reach, state, decay):
        first, starts = first_ref[0], start_ref[0]
        pos, _, query, key, value = activations(block, taps, starts, first, block_len)
        log_decay = decays(logit_ref[0])
        running = None
        before = jnp.zeros((1, DK), jnp.float32)
        reach_in = (starts < first).astype(jnp.float32)
        for index in range(block_len // WIDE):
            span = Span(index, first, query, key, value, log_decay, starts, pos)
            result = split_dot(span.scores(), span.value, NN)
            if running is not None:
                result = result + split_dot(span.query_start, running, NN)
            out[0, span.rows] = result
            reach[0, span.rows] = span.query * jnp.exp(before + span.cum) * reach_in[span.rows]
            before = before + span.total
            running = span.next_state(running)
        block_decay = jnp.exp(before) * reach_in[block_len - 1 :]
        state[0] = packed_rows(running, block_decay)
        decay[0, 0] = block_decay

    return launch(
        kernel,
        (first, wide_mixed, conv_weight, logits, starts),
        mixer_specs(block_len),
        (
            ((seq_count, block_len, HEADS * DV), jnp.float32),
            ((seq_count, block_len, HEADS * DK), jnp.float32),
            ((GROUP, DK + EXTRA, DV), jnp.bfloat16),
            ((seq_count, HEADS, 1, DK), jnp.float32),
        ),
        [value_spec(block_len), key_spec(block_len), pair_spec(DK + EXTRA), decay_spec],
        seq_count,
        13,
    )


def mixer_output(first, local_out, reach, incoming, gates, head_gain):
    seq_count, block_len = reach.shape[:2]

    def kernel(first_ref, local, reach_ref, state, gate, gain, out, gated):
        result = local[0] + split_dot(reach_ref[0], state[0].astype(jnp.float32), NN)
        out[0] = result
        rms = lax.rsqrt(jnp.mean(result * result, axis=-1, keepdims=True) + epsilon)
        value = gate[0].astype(jnp.float32)
        gated[0] = (result * rms * gain[...] * (value * jax.nn.sigmoid(value))).astype(jnp.bfloat16)

    values = value_spec(block_len)
    return launch(
        kernel,
        (first, local_out, reach, incoming, gates, head_gain),
        [values, key_spec(block_len), pair_spec(DK), values]
        + [pl.BlockSpec((1, DV), lambda s, h, first: (0, 0))],
        (
            ((seq_count, block_len, HEADS * DV), jnp.float32),
            ((seq_count, block_len, HEADS * DV), jnp.bfloat16),
        ),
        [values, values],
        seq_count,
        4,
    )


def mixer_output_back(first, mixer_out, reach, gated_grad, gates, head_gain, decay):
    seq_count, block_len = reach.shape[:2]

    def kernel(
        first_ref,
        mixed,
        reach_ref,
        grad_ref,
        gate,
        gain,
        decay_ref,
        out_grad,
        gate_grad,
        term,
        gain_grad,
    ):
        result, grad = mixed[0], grad_ref[0]
        rms = lax.rsqrt(jnp.mean(result * result, axis=-1, keepdims=True) + epsilon)
        value = gate[0].astype(jnp.float32)
        sig = jax.nn.sigmoid(value)
        inner = grad * (value * sig)
        normed = result * rms
        gate_grad[0] = (
            grad * (normed * gain[...]) * sig * (1.0 + value * (1.0 - sig))
        ).astype(jnp.bfloat16)
        gain_grad[0, 0] = jnp.sum(inner * normed, axis=0, keepdims=True)
        scaled = inner * gain[...]
        grad_out = rms * (
            scaled - normed * rms * jnp.mean(scaled * result, axis=-1, keepdims=True)
        )
        out_grad[0] = grad_out
        term[0] = packed_rows(split_dot(reach_ref[0], grad_out, TN), decay_ref[0, 0])

    values = value_spec(block_len)
    return launch(
        kernel,
        (first, mixer_out, reach, gated_grad, gates, head_gain, decay),
        [values, key_spec(block_len), values, values]
        + [pl.BlockSpec((1, DV), lambda s, h, first: (0, 0)), decay_spec],
        (
            ((seq_count, block_len, HEADS * DV), jnp.float32),
            ((seq_count, block_len, HEADS * DV), jnp.bfloat16),
            ((GROUP, DK + EXTRA, DV), jnp.bfloat16),
            ((seq_count, HEADS, 1, DV), jnp.float32),
        ),
        [values, values, pair_spec(DK + EXTRA)]
        + [pl.BlockSpec((1, 1, 1, DV), lambda s, h, first: (s, h, 0, 0))],
        seq_count,
        5,
    )


def conv_back(grad, found, taps, pos, starts, block_len):
    wide, total, sig = found
    grad = grad * sig * (1.0 + total * (1.0 - sig))
    zeros = jnp.zeros((HALO, grad.shape[1]), jnp.float32)
    spread_grad, tap_grads = None, []
    for tap in range(CONV):
        masked = grad if tap == 0 else grad * (pos - tap >= starts).astype(jnp.float32)
        source = wide[HALO - tap : HALO - tap + block_len]
        tap_grads.append(jnp.sum(masked * source, axis=0, keepdims=True))
        padded = jnp.concatenate([zeros, masked * taps[tap : tap + 1, :], zeros], axis=0)
        part = padded[tap : tap + HALO + block_len]
        spread_grad = part if spread_grad is None else spread_grad + part
    return spread_grad, jnp.concatenate(tap_grads, axis=0)


def mixer_backward(first, wide_mixed, conv_weight, logits, starts, out_grad, incoming, outgoing):
    seq_count, block_len = starts.shape[:2]

    def kernel(first_ref, block, taps, logit_ref, start_ref, *refs):
        grad_ref, in_ref, end_ref, main, edge, tail, tap_grad, dlogit, bias = refs
        first, starts = first_ref[0], start_ref[0]
        pos, found, query, key, value = activations(block, taps, starts, first, block_len)
        logit = logit_ref[0]
        log_decay = decays(logit)
        count = block_len // WIDE
        spans, states = [], [in_ref[0].astype(jnp.float32)]
        for index in range(count):
            span = Span(index, first, query, key, value, log_decay, starts, pos)
            spans.append(span)
            if index + 1 < count:
                states.append(span.next_state(states[-1]))
        later = end_ref[0].astype(jnp.float32)
        query_grads, key_grads, value_grads, decay_grads = [], [], [], []
        for index in range(count)[::-1]:
            span, state = spans[index], states[index]
            grad = grad_ref[0, span.rows]
            score_grad = jnp.where(span.allowed, split_dot(grad, span.value, NT), 0.0)
            query_grad = split_dot(score_grad, span.key_centred, NN) * span.to_query
            query_grad = query_grad + split_dot(grad, state, NT) * span.from_start
            end_grad = split_dot(span.value, later, NT)
            key_grad = split_dot(score_grad, span.query_centred, TN) * span.to_key
            key_grad = key_grad + end_grad * span.to_end
            value_grad = split_dot(span.scores(), grad, TN) + split_dot(span.key_end, later, NN)
            kept = unit_dot(jnp.ones((8, DV), jnp.float32), state * later, NT)[:1]
            total_grad = jnp.sum(end_grad * span.key_end, axis=0, keepdims=True)
            total_grad = total_grad + kept * jnp.exp(span.total) * span.kept
            cum_grad = span.query * query_grad - span.key * key_grad
            decay_grads.append(unit_dot(span.upper, cum_grad, NN) + total_grad)
            query_grads.append(query_grad)
            key_grads.append(key_grad)
            value_grads.append(value_grad)
            if index > 0:
                later = later * span.keep_column + split_dot(span.query_start, grad, TN)
        grads = [
            jnp.concatenate(parts[::-1], axis=0) for parts in (query_grads, key_grads, value_grads)
        ]
        grads = jnp.concatenate([grads[0] * DK ** (-0.5)] + grads[1:], axis=1)
        wide_grad, tap_grad[0] = conv_back(grads, found, taps, pos, starts, block_len)
        edge[0] = wide_grad[:HALO]
        main[0] = wide_grad[HALO:].astype(jnp.bfloat16)
        tail[0] = wide_grad[block_len:]
        decay_grad = jnp.concatenate(decay_grads[::-1], axis=0)
        decay_grad = jnp.where(starts < pos, decay_grad, 0.0)
        logit_grad = decay_grad / gate_scale * jax.nn.sigmoid(-logit)
        dlogit[0] = logit_grad
        bias[0, 0] = jnp.sum(logit_grad, axis=0, keepdims=True)

    def heads_spec(rows):
        return pl.BlockSpec((1, rows, PER_HEAD), lambda s, h, first: (s, 0, h))

    width = HEADS * PER_HEAD
    return launch(
        kernel,
        (first, wide_mixed, conv_weight, logits, starts, out_grad, incoming, outgoing),
        mixer_specs(block_len) + [value_spec(block_len), pair_spec(DK), pair_spec(DK)],
        (
            ((seq_count, block_len, width), jnp.bfloat16),
            ((seq_count, HALO, width), jnp.float32),
            ((seq_count, HALO, width), jnp.float32),
            ((seq_count, CONV, width), jnp.float32),
            ((seq_count, block_len, HEADS * DK), jnp.float32),
            ((seq_count, HEADS, 1, DK), jnp.float32),
        ),
        [heads_spec(block_len), heads_spec(HALO), heads_spec(HALO), heads_spec(CONV)]
        + [key_spec(block_len), decay_spec],
        seq_count,
        24,
    )


def bf_dot(left, right):
    return jnp.dot(left, right, preferred_element_type=jnp.float32)


def feed_forward(hidden, out_grad, gain, gate_sources, up_sources, down_left, down_right):
    tokens, width = hidden.shape
    sizes, mine = tuple(size for size, _ in chip_axes()), coordinates()
    block_rows, inner = gate_sources[0][0].shape[3:]
    count, tile = len(gate_sources), 256
    half = width // 2
    steps = inner // tile

    def kernel(me, hid, grad, gain_ref, wl, wr, *refs):
        gate_refs, up_refs, refs = refs[:count], refs[count : 2 * count], refs[2 * count :]
        out, back, back_low, normed, act, gate_back, up_back, gain_back = refs[:8]
        total, turned, gate_held, up_held = refs[8:]
        step = pl.program_id(0)
        w_gate = assemble(gate_held, gate_refs, gate_sources, me, 2, 1)
        w_up = assemble(up_held, up_refs, up_sources, me, 1, 2)

        @pl.when(step == 0)
        def _():
            value = hid[...]
            rms = lax.rsqrt(jnp.mean(value * value, axis=-1, keepdims=True) + epsilon)
            normed[...] = (value * rms * gain_ref[...]).astype(jnp.bfloat16)
            total[...] = jnp.zeros_like(total)
            turned[...] = jnp.zeros_like(turned)

        source, low = normed[...], grad[...]
        gate, up = bf_dot(source, w_gate), bf_dot(source, w_up)
        inner_grad = nt_dot(low[:, :half], wl[...]) + nt_dot(low[:, half:], wr[...])
        sig = jax.nn.sigmoid(gate)
        silu = gate * sig
        active = (silu * up).astype(jnp.bfloat16)
        gate_grad = (inner_grad * up * sig * (1.0 + gate * (1.0 - sig))).astype(jnp.bfloat16)
        up_grad = (inner_grad * silu).astype(jnp.bfloat16)
        act[...], gate_back[...], up_back[...] = active, gate_grad, up_grad
        total[:, :half] += bf_dot(active, wl[...])
        total[:, half:] += bf_dot(active, wr[...])
        turned[...] += nt_dot(gate_grad, w_gate) + nt_dot(up_grad, w_up)

        @pl.when(step == steps - 1)
        def _():
            value, back_in = hid[...], turned[...]
            rms = lax.rsqrt(jnp.mean(value * value, axis=-1, keepdims=True) + epsilon)
            out[...] = value + total[...]
            gain_back[...] = jnp.sum(back_in * value * rms, axis=0, keepdims=True)
            result = grad[...].astype(jnp.float32) + rms_back(back_in, value, rms, gain_ref[...])
            back[...] = result
            back_low[...] = result.astype(jnp.bfloat16)

    def whole(rows, columns):
        return pl.BlockSpec((rows, columns), lambda i, me: (0, 0))

    along = pl.BlockSpec((tile, half), lambda i, me: (i, 0))
    inner_spec = pl.BlockSpec((tokens, tile), lambda i, me: (0, i))
    inner_shape = jax.ShapeDtypeStruct((tokens, inner), jnp.bfloat16)
    arrays = [array for array, _, _ in gate_sources + up_sources]
    held = pltpu.VMEM(sizes + (block_rows, tile), jnp.bfloat16)
    return pl.pallas_call(
        kernel,
        out_shape=[
            jax.ShapeDtypeStruct((tokens, width), jnp.float32),
            jax.ShapeDtypeStruct((tokens, width), jnp.float32),
            jax.ShapeDtypeStruct((tokens, width), jnp.bfloat16),
            jax.ShapeDtypeStruct((tokens, width), jnp.bfloat16),
            inner_shape,
            inner_shape,
            inner_shape,
            jax.ShapeDtypeStruct((1, width), jnp.float32),
        ],
        grid_spec=pltpu.PrefetchScalarGridSpec(
            num_scalar_prefetch=1,
            grid=(steps,),
            in_specs=[whole(tokens, width), whole(tokens, width), whole(1, width), along, along]
            + [tile_spec(array, tile, lambda i, me: (0, 0, 0, 0, i)) for array in arrays],
            out_specs=[whole(tokens, width)] * 4 + [inner_spec] * 3 + [whole(1, width)],
            scratch_shapes=[
                pltpu.VMEM((tokens, width), jnp.float32),
                pltpu.VMEM((tokens, width), jnp.float32),
                held,
                held,
            ],
        ),
        compiler_params=pltpu.CompilerParams(vmem_limit_bytes=58 * 2**20),
        cost_estimate=takes(28),
    )(mine, hidden, out_grad, gain, down_left, down_right, *arrays)


def nt_dot(left, right):
    return lax.dot_general(left, right, (NT, ((), ())), preferred_element_type=jnp.float32)


def rms_back(grad_normed, source, inv_rms, gain_vec):
    scaled = grad_normed * gain_vec
    return inv_rms * (
        scaled - source * inv_rms * inv_rms * jnp.mean(scaled * source, axis=-1, keepdims=True)
    )


def local(
    inputs,
    doc_start,
    norm_gain,
    w_in,
    conv_weight,
    w_low,
    w_high,
    gate_bias,
    head_gain,
    w_out,
    ffn_gain,
    w_gate_up,
    w_down,
    out_grad,
):
    seq_count, block_len, model_width = inputs.shape
    row_count = seq_count * block_len
    key_width = HEADS * DK
    value_width = HEADS * DV
    conv_width = 2 * key_width + value_width
    block_start = lax.axis_index("seq") * block_len
    half = model_width // 2
    first_shard = by_head(w_in[:, :conv_width])
    taps = by_head(conv_weight)
    rest_shard = jnp.concatenate([w_in[:, conv_width:], w_out, w_down], axis=0)
    rest_cuts = [w_in.shape[0], w_out.shape[0], w_down.shape[0]]
    place = jnp.stack([block_start, lax.axis_index("seq") % GROUP]).astype(jnp.int32)
    starts = doc_start[:, :, None]
    gain_row = head_gain[None, :]
    axes = chip_axes()

    fast = gather_levels(first_shard)
    edge = shifted(inputs[:, block_len - HALO :, :], 1)
    wide = jnp.concatenate([edge, inputs], axis=1).astype(jnp.float32)
    wide_rms = lax.rsqrt(jnp.mean(wide * wide, axis=-1, keepdims=True) + epsilon)
    wide_normed = (wide * wide_rms * norm_gain).astype(jnp.bfloat16)
    layer_in = wide[:, HALO:].reshape(row_count, model_width)
    inv_rms = wide_rms[:, HALO:].reshape(row_count, 1)
    fast, wide_normed, rest_shard = together(fast, wide_normed, rest_shard)
    rest = gather_levels(rest_shard)
    fast = gather_first(fast)
    normed = wide_normed[:, HALO:].reshape(row_count, model_width)
    wide_rows = wide_normed.reshape(-1, model_width)
    lowrank = bf_dot(normed, w_low)
    gate_logit = (
        jnp.dot(lowrank, w_high, precision=highest, preferred_element_type=jnp.float32) + gate_bias
    )
    fast, gate_logit, rest[1] = together(fast, gate_logit, rest[1])
    fast = gather_second(fast)
    fast, rest[2], wide_shard = together(fast, rest[2], w_gate_up)
    fast = gather_cores(fast)
    wide_pieces = gather_levels(wide_shard)
    wide_mixed = projected(wide_rows, *[[(own, 0, 0), (other, 1, 0)] for own, other in fast])
    wide_mixed = wide_mixed.reshape(seq_count, HALO + block_len, conv_width)
    wide_mixed, rest = together(wide_mixed, rest)
    rest = gather_first(rest)
    logits = gate_logit.reshape(seq_count, block_len, key_width)
    local_out, reach, local_state, block_decay = mixer_forward(
        place, wide_mixed, taps, logits, starts
    )
    local_state, rest, wide_pieces[1] = together(local_state, rest, wide_pieces[1])
    got, _ = exchanged(local_state)
    got, rest = together(got, rest)
    rest = gather_second(rest)
    beyond = shifted(composed(place, got, False), GROUP)
    incoming = composed(place, got, False, beyond)
    incoming, rest, wide_pieces = together(incoming, rest, wide_pieces)
    wide_pieces = gather_first(wide_pieces)
    rest = gather_cores(rest)
    incoming, _ = exchanged(incoming)
    incoming, rest, wide_pieces = together(incoming, rest, wide_pieces)
    crossed = gather_second(wide_pieces)
    early = [swapped(pieces[0], 1) for pieces in crossed]
    incoming, fast = together(incoming, fast)
    [(left_full, right_full)] = gather_done(fast, [first_shard.shape[0]])
    (g_left, g_right), (out_left, out_right), (down_left, down_right) = gather_done(rest, rest_cuts)
    gate_cols = jnp.concatenate([bf_dot(normed, g_left), bf_dot(normed, g_right)], axis=1)
    gates = gate_cols.astype(jnp.bfloat16).reshape(seq_count, block_len, value_width)
    mixer_out, gated = mixer_output(place, local_out, reach, incoming, gates, gain_row)
    gated = gated.reshape(row_count, value_width)
    hidden_one = layer_in + jnp.concatenate(
        [bf_dot(gated, out_left), bf_dot(gated, out_right)], axis=1
    )
    hidden_one, crossed, early = together(hidden_one, crossed, early)
    gate_sources, up_sources = core_sources(crossed, early)
    out_rows_low = out_grad.reshape(row_count, model_width)
    (
        layer_out,
        hidden_grad,
        hidden_low,
        ffn_in,
        activation,
        gate_grad,
        up_grad,
        ffn_gain_row,
    ) = feed_forward(
        hidden_one, out_rows_low, ffn_gain[None, :], gate_sources, up_sources, down_left, down_right
    )
    gated_grad = nt_dot(hidden_low[:, :half], out_left) + nt_dot(hidden_low[:, half:], out_right)
    gated_grad = gated_grad.reshape(seq_count, block_len, value_width)
    mixer_grad, gate_vals_grad, state_term, head_gain_grad = mixer_output_back(
        place, mixer_out, reach, gated_grad, gates, gain_row, block_decay
    )
    gate_vals_grad = gate_vals_grad.reshape(row_count, value_width)

    state_term, gated, ffn_in, activation = together(state_term, gated, ffn_in, activation)
    got, (out_terms, wide_terms, down_terms) = exchanged(
        state_term,
        (
            (lambda: grad_products(gated, hidden_low),),
            (lambda _: grad_products(ffn_in, gate_grad, up_grad),),
            (lambda _: grad_products(activation, out_rows_low),),
        ),
    )
    wide_terms = cores_send([wide_terms])
    total = composed(place, got, True)
    total, parts, wide_terms = together(total, phase_parts(wide_terms, 0), wide_terms)
    wide_terms = phase_swap(wide_terms, 0, parts)
    beyond = shifted(total, -GROUP)
    g_terms = grad_products(normed, gate_vals_grad)
    beyond, g_terms, out_terms, down_terms = together(beyond, g_terms, out_terms, down_terms)
    rest_terms = cores_send([g_terms, out_terms, down_terms])
    outgoing = composed(place, got, True, beyond)
    shape = outgoing.shape
    outgoing = outgoing.reshape((2, 2, 2) + shape[1:])
    outgoing = jnp.stack(exchange_step(outgoing, 2, 1), axis=2)
    outgoing = jnp.stack(exchange_step(outgoing, 1, 2), axis=1)
    outgoing, wide_terms, rest_terms = together(outgoing, wide_terms, rest_terms)
    wide_terms = phase_send(wide_terms, 1)
    outgoing = jnp.stack(exchange_step(outgoing, 0, 4)).reshape(shape)
    outgoing, wide_terms = together(outgoing, wide_terms)
    wide_sums = level_sums(wide_terms)
    outgoing, wide_sums, rest_terms = together(outgoing, wide_sums, rest_terms)
    wide_own, wide_last = levels_send(wide_sums)
    rest_terms = phase_send(rest_terms, 0)
    backs = mixer_backward(
        place, wide_mixed, taps, logits, starts, mixer_grad, incoming, outgoing
    )
    backs, rest_terms, wide_last[0] = together(backs, rest_terms, wide_last[0])
    rest_terms = phase_send(rest_terms, 1)
    mixed_grad, back_edge, back_tail, tap_grads, logit_grad, gate_bias_grad = backs
    back_edge = shifted(back_edge.astype(jnp.bfloat16), -1).astype(jnp.float32)
    mixed_grad = lax.dynamic_update_slice(
        mixed_grad, (back_tail + back_edge).astype(jnp.bfloat16), (0, block_len - HALO, 0)
    )
    mixed_grad = mixed_grad.reshape(row_count, conv_width)
    small_rows, lowrank_grad = small_packed(
        logit_grad.reshape(row_count, key_width),
        lowrank,
        w_high,
        normed,
        tap_grads,
        gate_bias_grad.reshape(seq_count, key_width),
        head_gain_grad,
        ffn_gain_row,
    )
    normed_grad = (
        nt_dot(mixed_grad[:, : conv_width // 2], left_full)
        + nt_dot(mixed_grad[:, conv_width // 2 :], right_full)
        + nt_dot(gate_vals_grad[:, :half], g_left)
        + nt_dot(gate_vals_grad[:, half:], g_right)
        + nt_dot(lowrank_grad, w_low)
    )
    norm_gain_grad = jnp.sum(normed_grad * layer_in * inv_rms, axis=0)
    input_grad = hidden_grad + rms_back(normed_grad, layer_in, inv_rms, norm_gain)
    small_rows = lax.dynamic_update_slice(small_rows, norm_gain_grad[None, :], (34, 0))
    mixed_grad, small_rows, rest_terms, input_grad, wide_last[1] = together(
        mixed_grad, small_rows, rest_terms, input_grad, wide_last[1]
    )
    rest_sums = level_sums(rest_terms)
    small_rows = spread(small_rows, axes[3])
    mixed_grad, rest_sums, small_rows = together(mixed_grad, rest_sums, small_rows)
    rest_own, rest_last = levels_send(rest_sums)
    fast_terms = grad_products(normed, mixed_grad)
    small_rows = spread(sum(small_rows), axes[2])
    fast_terms, small_rows, wide_last[2] = together(fast_terms, small_rows, wide_last[2])
    fast_terms = cores_send([fast_terms])
    small_rows = spread(sum(small_rows), axes[1])
    fast_terms, small_rows = together(fast_terms, small_rows)
    fast_terms = phase_send(fast_terms, 0)
    small_rows = sum(small_rows)
    fast_terms, small_rows, rest_last[0] = together(fast_terms, small_rows, rest_last[0])
    fast_terms = phase_send(fast_terms, 1)
    fast_terms, rest_last[1] = together(fast_terms, rest_last[1])
    fast_own, fast_last = levels_send(level_sums(fast_terms))
    small_rows = [small_rows]
    small_own = sum(small_rows)
    small_parts = [small_own] + spread(small_own.astype(jnp.bfloat16), axes[0])[1:]
    norm_gain_grad, conv_weight_grad, w_low_grad, w_high_grad, *rows_found = small_unpacked(
        small_parts, key_width, w_high.shape[0]
    )
    gate_bias_grad, head_gain_grad, ffn_gain_grad = [row[0] for row in rows_found]
    rest_grad = reduced(rest_own, rest_last)
    w_gate_up_grad = reduced(wide_own, wide_last)
    fast_grad = by_kind(reduced(fast_own, fast_last))
    ends = [rest_cuts[0], rest_cuts[0] + rest_cuts[1]]
    w_in_grad = jnp.concatenate([fast_grad, rest_grad[: ends[0]]], axis=1)
    w_out_grad = rest_grad[ends[0] : ends[1]]
    w_down_grad = rest_grad[ends[1] :]
    return (
        layer_out.reshape(seq_count, block_len, model_width),
        input_grad.reshape(seq_count, block_len, model_width),
        norm_gain_grad[0],
        w_in_grad,
        conv_weight_grad,
        w_low_grad.T,
        w_high_grad,
        gate_bias_grad,
        head_gain_grad,
        w_out_grad,
        ffn_gain_grad,
        w_gate_up_grad,
        w_down_grad,
    )


def solution(mesh):
    placed = (
        P(None, "seq", None),
        P(None, "seq"),
        P(),
        P("seq", None),
        P(),
        P(),
        P(),
        P(),
        P(),
        P("seq", None),
        P(),
        P("seq", None),
        P("seq", None),
        P(None, "seq", None),
    )
    return jax.shard_map(
        local,
        mesh=mesh,
        in_specs=placed,
        out_specs=(
            P(None, "seq", None),
            P(None, "seq", None),
            P(),
            P("seq", None),
            P(),
            P(),
            P(),
            P(),
            P(),
            P("seq", None),
            P(),
            P("seq", None),
            P("seq", None),
        ),
        check_vma=False,
    )
```

```python
import jax
import jax.numpy as jnp
from jax import lax
from jax.experimental import pallas as pl
from jax.experimental.pallas import tpu as pltpu
from jax.sharding import PartitionSpec as P

HEADS = 4
DK = 128
DV = 256
FF = 2816
WIDE = 128
CONV = 4


epsilon = 1e-06
gate_scale = 16.0
highest = lax.Precision.HIGHEST


GROUP = 8
HALO = 8
EXTRA = 16
SMALL = 40
PER_HEAD = 2 * DK + DV


def chip_axes():
    count = lax.axis_size("seq")
    sides = {16: (4, 2, 2), 64: (4, 4, 4)}.get(count // 2, (count // 2, 1, 1))
    return (
        (sides[0], 2 * sides[1] * sides[2]),
        (sides[1], 2 * sides[2]),
        (sides[2], 2),
        (2, 1),
    )


def swapped(array, mask):
    count = lax.axis_size("seq")
    return lax.ppermute(array, "seq", [(i, i ^ mask) for i in range(count)])


def shifted(array, by):
    count = lax.axis_size("seq")
    pairs = [(i, i + by) for i in range(count) if 0 <= i + by < count]
    return lax.ppermute(array, "seq", pairs)


def spread(block, axis):
    size, stride = axis
    return [block] + [swapped(block, step * stride) for step in range(1, size)]


def takes(micros):
    return pl.CostEstimate(flops=int(micros * 1e9), bytes_accessed=0, transcendentals=0)


def coordinates():
    mine = lax.axis_index("seq")
    return jnp.stack([(mine // stride) % size for size, stride in chip_axes()]).astype(jnp.int32)


def placed_blocks(sources, one, two, cuts):
    axes = chip_axes()
    sizes = tuple(size for size, _ in axes)
    depth, mine = sizes[0], coordinates()
    (rows, columns), kind = sources[0][0].shape[3:], sources[0][0].dtype

    def target(core, second, first, me):
        spot = [0, 0, 0, 0]
        spot[one] = jnp.bitwise_xor(first, me[one])
        spot[two] = jnp.bitwise_xor(second, me[two])
        spot[3] = jnp.bitwise_xor(core, me[3])
        return tuple(spot) + (0, 0)

    def source(mine_core, base, extent):
        def index(core, second, first, me):
            step = core * sizes[two] + second - mine_core * sizes[two] - base
            early, late = step < 0, step >= extent
            held = jnp.where(early, 0, jnp.where(late, extent - 1, step))
            return (
                held,
                jnp.where(early, 0, jnp.where(late, sizes[one] - 1, first)),
                0,
                0,
                0,
            )

        return index

    def kernel(me, *refs):
        pieces, outs = refs[: len(sources)], refs[len(sources) :]
        step = pl.program_id(0) * sizes[two] + pl.program_id(1)
        for piece, (array, core, base) in zip(pieces, sources):
            begin = core * sizes[two] + base

            @pl.when((step >= begin) & (step < begin + array.shape[0]))
            def _():
                for level in range(depth):
                    block, start = piece[0, 0, level], 0
                    for out, cut in zip(outs, cuts):
                        out[jnp.bitwise_xor(me[0], level), 0, 0, 0] = block[start : start + cut]
                        start += cut

    found = pl.pallas_call(
        kernel,
        out_shape=[jax.ShapeDtypeStruct(sizes + (cut, columns), kind) for cut in cuts],
        grid_spec=pltpu.PrefetchScalarGridSpec(
            num_scalar_prefetch=1,
            grid=(2, sizes[two], sizes[one]),
            in_specs=[
                pl.BlockSpec((1, 1, depth, rows, columns), source(core, base, array.shape[0]))
                for array, core, base in sources
            ],
            out_specs=[pl.BlockSpec((depth, 1, 1, 1, cut, columns), target) for cut in cuts],
        ),
        compiler_params=pltpu.CompilerParams(vmem_limit_bytes=40 * 2**20),
        cost_estimate=takes(1.0 + rows * columns * 5e-5),
    )(mine, *[array for array, _, _ in sources])
    return [array.reshape(-1, columns) for array in found]


def together(*values):
    return lax.optimization_barrier(values)


def gather_levels(shard):
    return spread(shard, chip_axes()[0])


def gather_first(levels):
    stacked = levels if isinstance(levels, jax.Array) else jnp.stack(levels)
    half = stacked.shape[2] // 2
    axes = chip_axes()
    return [spread(stacked[..., :half], axes[2]), spread(stacked[..., half:], axes[1])]


def gather_second(sides):
    axes = chip_axes()
    return [spread(jnp.stack(sides[0]), axes[1]), spread(jnp.stack(sides[1]), axes[2])]


def gather_cores(crossed):
    found = []
    for pieces in crossed:
        own = jnp.stack(pieces)
        found.append([own, swapped(own, 1)])
    return found


def gather_done(pairs, cuts):
    halves = [
        placed_blocks([(own, 0, 0), (other, 1, 0)], one, two, cuts)
        for (own, other), one, two in zip(pairs, (2, 1), (1, 2))
    ]
    return list(zip(*halves))


def core_sources(crossed, early):
    halves = []
    for pieces, before in zip(crossed, early):
        sources = []
        for step, piece in enumerate(pieces):
            other = before if step == 0 else swapped(piece, 1)
            sources.extend([(piece[None], 0, step), (other[None], 1, step)])
        halves.append(sources)
    return halves


def assemble(held, refs, sources, me, one, two):
    for ref, (array, core, base) in zip(refs, sources):
        for second in range(array.shape[0]):
            for first in range(array.shape[1]):
                for level in range(array.shape[2]):
                    spot = [jnp.bitwise_xor(me[0], level), 0, 0, jnp.bitwise_xor(me[3], core)]
                    spot[one] = jnp.bitwise_xor(me[one], first)
                    spot[two] = jnp.bitwise_xor(me[two], base + second)
                    held[tuple(spot)] = ref[second, first, level]
    return held[...].reshape(-1, held.shape[-1])


def tile_spec(array, tile, index):
    return pl.BlockSpec(array.shape[:4] + (tile,), index)


def projected(rows, sources_a, sources_b):
    sizes, mine = tuple(size for size, _ in chip_axes()), coordinates()
    tokens, width = rows.shape
    block_rows, half = sources_a[0][0].shape[3:]
    tile = 512
    tiles = half // tile

    def kernel(me, row_ref, *refs):
        refs_a = refs[: len(sources_a)]
        refs_b = refs[len(sources_a) : -2]
        out, held = refs[-2:]

        @pl.when(pl.program_id(0) == 0)
        def _():
            assemble(held, refs_a, sources_a, me, 2, 1)

        @pl.when(pl.program_id(0) == 1)
        def _():
            assemble(held, refs_b, sources_b, me, 1, 2)

        full = held[...].reshape(width, tile)
        out[...] = bf_dot(row_ref[...], full).astype(jnp.bfloat16)

    def at_a(part, i, me):
        return (0, 0, 0, 0, jnp.where(part == 0, i, tiles - 1))

    def at_b(part, i, me):
        return (0, 0, 0, 0, jnp.where(part == 0, 0, i))

    return pl.pallas_call(
        kernel,
        out_shape=jax.ShapeDtypeStruct((tokens, 2 * half), jnp.bfloat16),
        grid_spec=pltpu.PrefetchScalarGridSpec(
            num_scalar_prefetch=1,
            grid=(2, tiles),
            in_specs=[pl.BlockSpec((tokens, width), lambda part, i, me: (0, 0))]
            + [tile_spec(array, tile, at_a) for array, _, _ in sources_a]
            + [tile_spec(array, tile, at_b) for array, _, _ in sources_b],
            out_specs=pl.BlockSpec((tokens, tile), lambda part, i, me: (0, part * tiles + i)),
            scratch_shapes=[pltpu.VMEM(sizes + (block_rows, tile), jnp.bfloat16)],
        ),
        compiler_params=pltpu.CompilerParams(vmem_limit_bytes=40 * 2**20),
        cost_estimate=takes(6),
    )(mine, rows, *[array for array, _, _ in sources_a + sources_b])


def grad_products(left, right_a, right_b=None):
    sizes = tuple(size for size, _ in chip_axes())
    strides = tuple(stride for _, stride in chip_axes())
    (tokens, features), columns = left.shape, right_a.shape[1]
    if right_b is None:
        columns = columns // 2
    count, mine = lax.axis_size("seq"), coordinates()
    rows = features // count
    tile = next(t for t in (512, 1408, 256) if columns % t == 0)
    chunks = next(c for c in (4, 2, 1) if features // c % 128 == 0)
    chunk = features // chunks

    def kernel(me, left_ref, a_ref, b_ref, away_a, keep_a, away_b, keep_b, flipped):
        @pl.when(pl.program_id(0) == 0)
        def _():
            flipped[...] = left_ref[...].T

        def products(odd):
            for right, away, keep, order in (
                (a_ref, away_a, keep_a, (2, 1, 0)),
                (b_ref, away_b, keep_b, (1, 2, 0)),
            ):
                for part in range(chunks):
                    full = jnp.dot(
                        flipped[part * chunk : (part + 1) * chunk],
                        right[...],
                        preferred_element_type=jnp.float32,
                    )
                    for start in range(0, chunk, rows):
                        device = (part * chunk + start) // rows
                        spot = tuple(
                            jnp.bitwise_xor(device // strides[axis] % sizes[axis], me[axis])
                            for axis in order
                        )
                        target = keep if device % 2 == odd else away
                        target[spot] = full[start : start + rows].astype(jnp.bfloat16)

        @pl.when(me[3] == 0)
        def _():
            products(0)

        @pl.when(me[3] == 1)
        def _():
            products(1)

    def result(one, two):
        shape = (sizes[one], sizes[two], sizes[0], rows)
        return (
            jax.ShapeDtypeStruct(shape + (columns,), jnp.bfloat16),
            pl.BlockSpec(shape + (tile,), lambda i, me: (0, 0, 0, 0, i)),
        )

    results = [result(2, 1), result(2, 1), result(1, 2), result(1, 2)]
    skip = columns // tile if right_b is None else 0
    right_b = right_a if right_b is None else right_b
    return pl.pallas_call(
        kernel,
        out_shape=[shape for shape, _ in results],
        grid_spec=pltpu.PrefetchScalarGridSpec(
            num_scalar_prefetch=1,
            grid=(columns // tile,),
            in_specs=[
                pl.BlockSpec((tokens, features), lambda i, me: (0, 0)),
                pl.BlockSpec((tokens, tile), lambda i, me: (0, i)),
                pl.BlockSpec((tokens, tile), lambda i, me: (0, i + skip)),
            ],
            out_specs=[spec for _, spec in results],
            scratch_shapes=[pltpu.VMEM((features, tokens), jnp.bfloat16)],
        ),
        compiler_params=pltpu.CompilerParams(vmem_limit_bytes=48 * 2**20),
        cost_estimate=takes(1.5 + features * columns * 4.5e-6),
    )(mine, left, right_a, right_b)


def total_of(groups):
    parts = []
    for refs, lead in groups:
        rows = [ref[(0,) * lead].astype(jnp.float32) for ref in refs]
        parts.append(jnp.concatenate(rows, axis=0) if len(rows) > 1 else rows[0])
    return sum(parts[1:], parts[0])


def flat_terms(terms):
    return [(since, arrays) for since, group in enumerate(terms) for arrays in group]


def regrouped(refs, flat):
    groups, at = [], 0
    for since, arrays in flat:
        groups.append((refs[at : at + len(arrays)], since))
        at += len(arrays)
    return groups, at


def phase_sums(pair, phase, step):
    flats = [flat_terms(terms) for terms in pair]
    depth = chip_axes()[0][0]
    second = chip_axes()[1][0] if phase == 0 else 1
    rows = sum(array.shape[-2] for array in flats[0][0][1])
    columns = flats[0][0][1][0].shape[-1]
    lead = 2 - phase

    def index(since):
        def found(i, j):
            spot = [0 if dim < phase else step if dim == phase else (i, j)[dim - 1] for dim in range(3)]
            return tuple(spot[since:]) + (0, 0)

        return found

    def kernel(*refs):
        ins, outs = refs[:-2], refs[-2:]
        at = 0
        for flat, out in zip(flats, outs):
            groups, used = regrouped(ins[at:], flat)
            at += used
            total = total_of([(part, 3 - since) for part, since in groups])
            out[(0,) * lead] = total.astype(jnp.bfloat16)

    arrays = [(array, since) for flat in flats for since, group in flat for array in group]
    shape = ((second, depth) if phase == 0 else (depth,)) + (rows, columns)
    out_spec = pl.BlockSpec(
        (1,) * lead + (rows, columns), lambda i, j: ((i, j) if phase == 0 else (j,)) + (0, 0)
    )
    return pl.pallas_call(
        kernel,
        out_shape=[jax.ShapeDtypeStruct(shape, jnp.bfloat16)] * 2,
        grid=(second, depth),
        in_specs=[
            pl.BlockSpec((1,) * (3 - since) + array.shape[-2:], index(since))
            for array, since in arrays
        ],
        out_specs=[out_spec] * 2,
        compiler_params=pltpu.CompilerParams(vmem_limit_bytes=32 * 2**20),
        cost_estimate=takes(3),
    )(*[array for array, _ in arrays])


def level_sums(pair):
    flats = [flat_terms(terms) for terms in pair]
    depth = chip_axes()[0][0]
    rows = sum(array.shape[-2] for array in flats[0][0][1])
    columns = flats[0][0][1][0].shape[-1]

    def kernel(*refs):
        ins, outs = refs[:-depth], refs[-depth:]
        at = 0
        for side, flat in enumerate(flats):
            groups, used = regrouped(ins[at:], flat)
            at += used
            cut = slice(side * columns, (side + 1) * columns)
            for level in range(depth):
                parts = []
                for part, since in groups:
                    spot = (0,) * (2 - since) + (level,)
                    values = [ref[spot].astype(jnp.float32) for ref in part]
                    parts.append(
                        jnp.concatenate(values, axis=0) if len(values) > 1 else values[0]
                    )
                total = sum(parts[1:], parts[0])
                outs[level][:, cut] = total.astype(outs[level].dtype)

    arrays = [(array, since) for flat in flats for since, group in flat for array in group]

    def spec(array, since):
        lead = (1,) * (2 - since) + (depth,)
        return pl.BlockSpec(lead + array.shape[-2:], lambda i: (0,) * (len(lead) + 2))

    shape = (rows, 2 * columns)
    return pl.pallas_call(
        kernel,
        out_shape=[jax.ShapeDtypeStruct(shape, jnp.float32)]
        + [jax.ShapeDtypeStruct(shape, jnp.bfloat16)] * (depth - 1),
        grid=(1,),
        in_specs=[spec(array, since) for array, since in arrays],
        out_specs=[pl.BlockSpec(shape, lambda i: (0, 0))] * depth,
        compiler_params=pltpu.CompilerParams(vmem_limit_bytes=40 * 2**20),
        cost_estimate=takes(3),
    )(*[array for array, _ in arrays])


def cores_send(products):
    found = []
    for keep, which in ((1, 0), (3, 2)):
        aways = [part[which] for part in products]
        away = jnp.concatenate(aways, axis=3) if len(aways) > 1 else aways[0]
        found.append([[[part[keep] for part in products], [swapped(away, 1)]]])
    return found


def phase_parts(pair, phase):
    return [phase_sums(pair, phase, step) for step in range(1, chip_axes()[2][0])]


def phase_swap(pair, phase, parts):
    axes, received = chip_axes(), [[], []]
    for step, sides in enumerate(parts):
        for side, part in enumerate(sides):
            stride = axes[((2, 1), (1, 2))[side][phase]][1]
            received[side].append([swapped(part, (step + 1) * stride)])
    return [terms + [parts] for terms, parts in zip(pair, received)]


def phase_send(pair, phase):
    return phase_swap(pair, phase, phase_parts(pair, phase))


def levels_send(sums):
    own, *parts = sums
    stride = chip_axes()[0][1]
    return own, [swapped(part, (step + 1) * stride) for step, part in enumerate(parts)]


def reduced(own, found):
    return sum((part.astype(jnp.float32) for part in found), own)


def small_packed(logit_grad, lowrank, w_high, normed, tap_grads, bias, head_gain, ffn_gain):
    tokens, keys = logit_grad.shape
    width, rank = normed.shape[1], w_high.shape[0]

    def kernel(grad_ref, low_ref, high_ref, normed_ref, taps, bias_ref, head, ffn, out, low_grad):
        grad = grad_ref[...]
        back = split_dot(grad, high_ref[...], NT).astype(jnp.bfloat16)
        low_grad[...] = back
        out[:rank] = lax.dot_general(
            back, normed_ref[...], (TN, ((), ())), preferred_element_type=jnp.float32
        )
        tap = jnp.sum(taps[...], axis=0)
        out[rank : rank + CONV] = tap[:, :width]
        out[rank + CONV : rank + 2 * CONV] = tap[:, width:]
        high = split_dot(low_ref[...], grad, TN)
        out[24:32, :keys] = high[:8]
        out[24:32, keys:] = high[8:]
        out[32:40] = jnp.zeros((8, width), jnp.float32)
        out[32:33, :keys] = jnp.sum(bias_ref[...], axis=0, keepdims=True)
        gains = [jnp.sum(head[:, h, 0], axis=0, keepdims=True) for h in range(HEADS)]
        out[32:33, keys : keys + DV] = sum(gains)
        out[33:34] = ffn[...]

    return pl.pallas_call(
        kernel,
        out_shape=[
            jax.ShapeDtypeStruct((SMALL, width), jnp.float32),
            jax.ShapeDtypeStruct((tokens, rank), jnp.bfloat16),
        ],
        compiler_params=pltpu.CompilerParams(vmem_limit_bytes=32 * 2**20),
        cost_estimate=takes(4),
    )(logit_grad, lowrank, w_high, normed, tap_grads, bias, head_gain, ffn_gain)


def small_unpacked(parts, keys, rank):
    width = parts[0].shape[1]

    def kernel(*refs):
        ins, (norm, conv, low, high, bias, head, ffn) = refs[: len(parts)], refs[len(parts) :]
        total = sum((ref[...].astype(jnp.float32) for ref in ins[1:]), ins[0][...])
        low[...] = total[:rank]
        for h in range(HEADS):
            side, at = divmod(h * PER_HEAD, width)
            block = total[rank + side * CONV : rank + (side + 1) * CONV]
            conv[:, h * DK : (h + 1) * DK] = block[:, at : at + DK]
            conv[:, keys + h * DK : keys + (h + 1) * DK] = block[:, at + DK : at + 2 * DK]
            conv[:, 2 * keys + h * DV : 2 * keys + (h + 1) * DV] = block[
                :, at + 2 * DK : at + PER_HEAD
            ]
        high[:8] = total[24:32, :keys]
        high[8:] = total[24:32, keys:]
        bias[...] = total[32:33, :keys]
        head[...] = total[32:33, keys : keys + DV]
        ffn[...] = total[33:34]
        norm[...] = total[34:35]

    shapes = ((1, width), (CONV, 2 * width), (rank, width), (rank, keys))
    shapes += ((1, keys), (1, DV), (1, width))
    return pl.pallas_call(
        kernel,
        out_shape=[jax.ShapeDtypeStruct(shape, jnp.float32) for shape in shapes],
        cost_estimate=takes(2),
    )(*parts)


def by_head(array):
    lead, (keys, values) = array.shape[:-1], (HEADS * DK, HEADS * DV)
    parts = [
        part.reshape(lead + (HEADS, -1))
        for part in (array[..., :keys], array[..., keys : 2 * keys], array[..., 2 * keys :])
    ]
    return jnp.concatenate(parts, axis=-1).reshape(lead + (2 * keys + values,))


def by_kind(array):
    lead = array.shape[:-1]
    array = array.reshape(lead + (HEADS, -1))
    parts = (array[..., :DK], array[..., DK : 2 * DK], array[..., 2 * DK :])
    return jnp.concatenate([part.reshape(lead + (-1,)) for part in parts], axis=-1)


def exchange_step(pieces, at, mask):
    kept = lax.index_in_dim(pieces, 0, at, False)
    return [kept, swapped(lax.index_in_dim(pieces, 1, at, False), mask)]


def exchanged(pieces, fillers=((), (), ())):
    shape, filled = pieces.shape, []
    pieces = pieces.reshape((2, 2, 2) + shape[1:])
    for at, mask, filler in zip((2, 1, 0), (1, 2, 4), fillers):
        pair = exchange_step(pieces, at, mask)
        if filler:
            values = filler[0](*filled[-1:])
            pair, values = together(pair, values)
            filled.append(values)
        pieces = jnp.stack(pair, axis=at)
    return pieces.reshape(shape), filled


def column(row):
    square = jnp.broadcast_to(row, (DK, DK)).T
    return jnp.concatenate([square, square], axis=1)


def packed_rows(state, decay):
    high = decay.astype(jnp.bfloat16)
    low = (decay - high.astype(jnp.float32)).astype(jnp.bfloat16)
    tail = jnp.broadcast_to(jnp.concatenate([high, low], axis=1), (EXTRA, DV))
    return jnp.concatenate([state.astype(jnp.bfloat16), tail], axis=0)


def composed(place, got, backward, beyond=None):
    order = range(GROUP)[::-1] if backward else range(GROUP)

    def kernel(place_ref, got_ref, *refs):
        mine, out = place_ref[1], refs[-1]
        running = jnp.zeros((DK, DV), jnp.float32)
        reach = jnp.ones((DK, DV), jnp.float32)
        far = None if beyond is None else refs[0][...].astype(jnp.float32)
        for index in order:
            spot = jnp.bitwise_xor(mine, index)
            piece = got_ref[spot].astype(jnp.float32)
            if beyond is not None:
                out[spot] = (running + reach * far).astype(jnp.bfloat16)
            tail = piece[DK : DK + 1]
            kept = column(tail[:, :DK] + tail[:, DK:])
            running = kept * running + piece[:DK]
            reach = reach * kept
        if beyond is None:
            out[...] = running.astype(jnp.bfloat16)

    extra = () if beyond is None else (beyond,)
    shape = (DK, DV) if beyond is None else (GROUP, DK, DV)
    return pl.pallas_call(
        kernel,
        out_shape=jax.ShapeDtypeStruct(shape, jnp.bfloat16),
        in_specs=[pl.BlockSpec(memory_space=pltpu.SMEM)]
        + [pl.BlockSpec(memory_space=pltpu.VMEM)] * (1 + len(extra)),
        out_specs=pl.BlockSpec(memory_space=pltpu.VMEM),
        cost_estimate=takes(2),
    )(place, got, *extra)


def split_dot(left, right, dims):
    dims = (dims, ((), ()))
    left_high, right_high = left.astype(jnp.bfloat16), right.astype(jnp.bfloat16)
    left_low = (left - left_high.astype(jnp.float32)).astype(jnp.bfloat16)
    right_low = (right - right_high.astype(jnp.float32)).astype(jnp.bfloat16)

    def one(a, b):
        return lax.dot_general(a, b, dims, preferred_element_type=jnp.float32)

    return one(left_high, right_high) + (one(left_high, right_low) + one(left_low, right_high))


def unit_dot(unit, value, dims):
    high = value.astype(jnp.bfloat16)
    rest = value - high.astype(jnp.float32)
    middle = rest.astype(jnp.bfloat16)
    low = (rest - middle.astype(jnp.float32)).astype(jnp.bfloat16)
    unit = unit.astype(jnp.bfloat16)
    return sum(
        lax.dot_general(unit, part, (dims, ((), ())), preferred_element_type=jnp.float32)
        for part in (low, middle, high)
    )


NN, NT, TN = ((1,), (0,)), ((1,), (1,)), ((0,), (0,))


def activations(block, taps, starts, first, block_len):
    pos = first + lax.broadcasted_iota(jnp.int32, (block_len, 1), 0)
    wide = block[0].astype(jnp.float32)
    total = taps[0:1, :] * wide[HALO:]
    for tap in range(1, CONV):
        usable = (pos - tap >= starts).astype(jnp.float32)
        total = total + taps[tap : tap + 1, :] * wide[HALO - tap : HALO - tap + block_len] * usable
    sig = jax.nn.sigmoid(total)
    active = total * sig
    query, key, value = active[:, :DK], active[:, DK : 2 * DK], active[:, 2 * DK :]
    return pos, (wide, total, sig), query * DK ** (-0.5), key, value


def decays(logit):
    return (jnp.minimum(logit, 0.0) - jnp.log1p(jnp.exp(-jnp.abs(logit)))) / gate_scale


class Span:
    def __init__(self, index, first, query, key, value, decay, starts, pos):
        rows = slice(index * WIDE, (index + 1) * WIDE)
        self.rows, first_pos = rows, first + index * WIDE
        self.query, self.key, self.value = query[rows], key[rows], value[rows]
        decay, starts, pos = decay[rows], starts[rows], pos[rows]
        t = lax.broadcasted_iota(jnp.int32, (WIDE, WIDE), 0)
        u = lax.broadcasted_iota(jnp.int32, (WIDE, WIDE), 1)
        self.lower = (u <= t).astype(jnp.float32)
        self.upper = (u >= t).astype(jnp.float32)
        self.allowed = (u <= t) & (u + first_pos >= starts)
        cum = unit_dot(self.lower, decay, NN)
        self.total = cum[WIDE - 1 :]
        middle = cum[WIDE // 2 - 1 : WIDE // 2]
        self.to_query, self.to_key = jnp.exp(cum - middle), jnp.exp(middle - cum)
        self.carried = (starts < first_pos).astype(jnp.float32)
        self.kept = (starts[WIDE - 1 :] < first_pos).astype(jnp.float32)
        self.from_start = jnp.exp(cum) * self.carried
        self.to_end = jnp.exp(self.total - cum) * (pos >= starts[WIDE - 1 :]).astype(jnp.float32)
        self.query_centred = self.query * self.to_query
        self.key_centred = self.key * self.to_key
        self.query_start = self.query * self.from_start
        self.key_end = self.key * self.to_end
        self.cum = cum
        ones = jnp.ones((WIDE, DV), jnp.float32)
        total_column = unit_dot_right(decay, ones)
        self.keep_column = jnp.exp(total_column) * self.kept

    def scores(self):
        raw = split_dot(self.query_centred, self.key_centred, NT)
        return jnp.where(self.allowed, raw, 0.0)

    def next_state(self, state):
        update = split_dot(self.key_end, self.value, TN)
        return update if state is None else state * self.keep_column + update


def unit_dot_right(value, unit):
    high = value.astype(jnp.bfloat16)
    rest = value - high.astype(jnp.float32)
    middle = rest.astype(jnp.bfloat16)
    low = (rest - middle.astype(jnp.float32)).astype(jnp.bfloat16)
    unit = unit.astype(jnp.bfloat16)
    return sum(
        lax.dot_general(part, unit, (TN, ((), ())), preferred_element_type=jnp.float32)
        for part in (low, middle, high)
    )


def mixer_specs(block_len):
    return [
        pl.BlockSpec((1, HALO + block_len, PER_HEAD), lambda s, h, first: (s, 0, h)),
        pl.BlockSpec((CONV, PER_HEAD), lambda s, h, first: (0, h)),
        pl.BlockSpec((1, block_len, DK), lambda s, h, first: (s, 0, h)),
        pl.BlockSpec((1, block_len, 1), lambda s, h, first: (s, 0, 0)),
    ]


def key_spec(block_len):
    return pl.BlockSpec((1, block_len, DK), lambda s, h, first: (s, 0, h))


def value_spec(block_len):
    return pl.BlockSpec((1, block_len, DV), lambda s, h, first: (s, 0, h))


def pair_spec(rows):
    return pl.BlockSpec(
        (1, rows, DV), lambda s, h, place: (jnp.bitwise_xor(place[1], s * HEADS + h), 0, 0)
    )


decay_spec = pl.BlockSpec((1, 1, 1, DK), lambda s, h, first: (s, h, 0, 0))


def launch(kernel, inputs, in_specs, outputs, out_specs, seq_count, micros):
    return pl.pallas_call(
        kernel,
        out_shape=[jax.ShapeDtypeStruct(shape, kind) for shape, kind in outputs],
        grid_spec=pltpu.PrefetchScalarGridSpec(
            num_scalar_prefetch=1,
            grid=(seq_count, HEADS),
            in_specs=in_specs,
            out_specs=out_specs,
        ),
        compiler_params=pltpu.CompilerParams(vmem_limit_bytes=40 * 2**20),
        cost_estimate=takes(micros),
    )(*inputs)


def mixer_forward(first, wide_mixed, conv_weight, logits, starts):
    seq_count, block_len = starts.shape[:2]

    def kernel(first_ref, block, taps, logit_ref, start_ref, out, reach, state, decay):
        first, starts = first_ref[0], start_ref[0]
        pos, _, query, key, value = activations(block, taps, starts, first, block_len)
        log_decay = decays(logit_ref[0])
        running = None
        before = jnp.zeros((1, DK), jnp.float32)
        reach_in = (starts < first).astype(jnp.float32)
        for index in range(block_len // WIDE):
            span = Span(index, first, query, key, value, log_decay, starts, pos)
            result = split_dot(span.scores(), span.value, NN)
            if running is not None:
                result = result + split_dot(span.query_start, running, NN)
            out[0, span.rows] = result
            reach[0, span.rows] = span.query * jnp.exp(before + span.cum) * reach_in[span.rows]
            before = before + span.total
            running = span.next_state(running)
        block_decay = jnp.exp(before) * reach_in[block_len - 1 :]
        state[0] = packed_rows(running, block_decay)
        decay[0, 0] = block_decay

    return launch(
        kernel,
        (first, wide_mixed, conv_weight, logits, starts),
        mixer_specs(block_len),
        (
            ((seq_count, block_len, HEADS * DV), jnp.float32),
            ((seq_count, block_len, HEADS * DK), jnp.float32),
            ((GROUP, DK + EXTRA, DV), jnp.bfloat16),
            ((seq_count, HEADS, 1, DK), jnp.float32),
        ),
        [value_spec(block_len), key_spec(block_len), pair_spec(DK + EXTRA), decay_spec],
        seq_count,
        13,
    )


def mixer_output(first, local_out, reach, incoming, gates, head_gain):
    seq_count, block_len = reach.shape[:2]

    def kernel(first_ref, local, reach_ref, state, gate, gain, out, gated):
        result = local[0] + split_dot(reach_ref[0], state[0].astype(jnp.float32), NN)
        out[0] = result
        rms = lax.rsqrt(jnp.mean(result * result, axis=-1, keepdims=True) + epsilon)
        value = gate[0].astype(jnp.float32)
        gated[0] = (result * rms * gain[...] * (value * jax.nn.sigmoid(value))).astype(jnp.bfloat16)

    values = value_spec(block_len)
    return launch(
        kernel,
        (first, local_out, reach, incoming, gates, head_gain),
        [values, key_spec(block_len), pair_spec(DK), values]
        + [pl.BlockSpec((1, DV), lambda s, h, first: (0, 0))],
        (
            ((seq_count, block_len, HEADS * DV), jnp.float32),
            ((seq_count, block_len, HEADS * DV), jnp.bfloat16),
        ),
        [values, values],
        seq_count,
        4,
    )


def mixer_output_back(first, mixer_out, reach, gated_grad, gates, head_gain, decay):
    seq_count, block_len = reach.shape[:2]

    def kernel(
        first_ref,
        mixed,
        reach_ref,
        grad_ref,
        gate,
        gain,
        decay_ref,
        out_grad,
        gate_grad,
        term,
        gain_grad,
    ):
        result, grad = mixed[0], grad_ref[0]
        rms = lax.rsqrt(jnp.mean(result * result, axis=-1, keepdims=True) + epsilon)
        value = gate[0].astype(jnp.float32)
        sig = jax.nn.sigmoid(value)
        inner = grad * (value * sig)
        normed = result * rms
        gate_grad[0] = (
            grad * (normed * gain[...]) * sig * (1.0 + value * (1.0 - sig))
        ).astype(jnp.bfloat16)
        gain_grad[0, 0] = jnp.sum(inner * normed, axis=0, keepdims=True)
        scaled = inner * gain[...]
        grad_out = rms * (
            scaled - normed * rms * jnp.mean(scaled * result, axis=-1, keepdims=True)
        )
        out_grad[0] = grad_out
        term[0] = packed_rows(split_dot(reach_ref[0], grad_out, TN), decay_ref[0, 0])

    values = value_spec(block_len)
    return launch(
        kernel,
        (first, mixer_out, reach, gated_grad, gates, head_gain, decay),
        [values, key_spec(block_len), values, values]
        + [pl.BlockSpec((1, DV), lambda s, h, first: (0, 0)), decay_spec],
        (
            ((seq_count, block_len, HEADS * DV), jnp.float32),
            ((seq_count, block_len, HEADS * DV), jnp.bfloat16),
            ((GROUP, DK + EXTRA, DV), jnp.bfloat16),
            ((seq_count, HEADS, 1, DV), jnp.float32),
        ),
        [values, values, pair_spec(DK + EXTRA)]
        + [pl.BlockSpec((1, 1, 1, DV), lambda s, h, first: (s, h, 0, 0))],
        seq_count,
        5,
    )


def conv_back(grad, found, taps, pos, starts, block_len):
    wide, total, sig = found
    grad = grad * sig * (1.0 + total * (1.0 - sig))
    zeros = jnp.zeros((HALO, grad.shape[1]), jnp.float32)
    spread_grad, tap_grads = None, []
    for tap in range(CONV):
        masked = grad if tap == 0 else grad * (pos - tap >= starts).astype(jnp.float32)
        source = wide[HALO - tap : HALO - tap + block_len]
        tap_grads.append(jnp.sum(masked * source, axis=0, keepdims=True))
        padded = jnp.concatenate([zeros, masked * taps[tap : tap + 1, :], zeros], axis=0)
        part = padded[tap : tap + HALO + block_len]
        spread_grad = part if spread_grad is None else spread_grad + part
    return spread_grad, jnp.concatenate(tap_grads, axis=0)


def mixer_backward(first, wide_mixed, conv_weight, logits, starts, out_grad, incoming, outgoing):
    seq_count, block_len = starts.shape[:2]

    def kernel(first_ref, block, taps, logit_ref, start_ref, *refs):
        grad_ref, in_ref, end_ref, main, edge, tail, tap_grad, dlogit, bias = refs
        first, starts = first_ref[0], start_ref[0]
        pos, found, query, key, value = activations(block, taps, starts, first, block_len)
        logit = logit_ref[0]
        log_decay = decays(logit)
        count = block_len // WIDE
        spans, states = [], [in_ref[0].astype(jnp.float32)]
        for index in range(count):
            span = Span(index, first, query, key, value, log_decay, starts, pos)
            spans.append(span)
            if index + 1 < count:
                states.append(span.next_state(states[-1]))
        later = end_ref[0].astype(jnp.float32)
        query_grads, key_grads, value_grads, decay_grads = [], [], [], []
        for index in range(count)[::-1]:
            span, state = spans[index], states[index]
            grad = grad_ref[0, span.rows]
            score_grad = jnp.where(span.allowed, split_dot(grad, span.value, NT), 0.0)
            query_grad = split_dot(score_grad, span.key_centred, NN) * span.to_query
            query_grad = query_grad + split_dot(grad, state, NT) * span.from_start
            end_grad = split_dot(span.value, later, NT)
            key_grad = split_dot(score_grad, span.query_centred, TN) * span.to_key
            key_grad = key_grad + end_grad * span.to_end
            value_grad = split_dot(span.scores(), grad, TN) + split_dot(span.key_end, later, NN)
            kept = unit_dot(jnp.ones((8, DV), jnp.float32), state * later, NT)[:1]
            total_grad = jnp.sum(end_grad * span.key_end, axis=0, keepdims=True)
            total_grad = total_grad + kept * jnp.exp(span.total) * span.kept
            cum_grad = span.query * query_grad - span.key * key_grad
            decay_grads.append(unit_dot(span.upper, cum_grad, NN) + total_grad)
            query_grads.append(query_grad)
            key_grads.append(key_grad)
            value_grads.append(value_grad)
            if index > 0:
                later = later * span.keep_column + split_dot(span.query_start, grad, TN)
        grads = [
            jnp.concatenate(parts[::-1], axis=0) for parts in (query_grads, key_grads, value_grads)
        ]
        grads = jnp.concatenate([grads[0] * DK ** (-0.5)] + grads[1:], axis=1)
        wide_grad, tap_grad[0] = conv_back(grads, found, taps, pos, starts, block_len)
        edge[0] = wide_grad[:HALO]
        main[0] = wide_grad[HALO:].astype(jnp.bfloat16)
        tail[0] = wide_grad[block_len:]
        decay_grad = jnp.concatenate(decay_grads[::-1], axis=0)
        decay_grad = jnp.where(starts < pos, decay_grad, 0.0)
        logit_grad = decay_grad / gate_scale * jax.nn.sigmoid(-logit)
        dlogit[0] = logit_grad
        bias[0, 0] = jnp.sum(logit_grad, axis=0, keepdims=True)

    def heads_spec(rows):
        return pl.BlockSpec((1, rows, PER_HEAD), lambda s, h, first: (s, 0, h))

    width = HEADS * PER_HEAD
    return launch(
        kernel,
        (first, wide_mixed, conv_weight, logits, starts, out_grad, incoming, outgoing),
        mixer_specs(block_len) + [value_spec(block_len), pair_spec(DK), pair_spec(DK)],
        (
            ((seq_count, block_len, width), jnp.bfloat16),
            ((seq_count, HALO, width), jnp.float32),
            ((seq_count, HALO, width), jnp.float32),
            ((seq_count, CONV, width), jnp.float32),
            ((seq_count, block_len, HEADS * DK), jnp.float32),
            ((seq_count, HEADS, 1, DK), jnp.float32),
        ),
        [heads_spec(block_len), heads_spec(HALO), heads_spec(HALO), heads_spec(CONV)]
        + [key_spec(block_len), decay_spec],
        seq_count,
        24,
    )


def bf_dot(left, right):
    return jnp.dot(left, right, preferred_element_type=jnp.float32)


def feed_forward(hidden, out_grad, gain, gate_sources, up_sources, down_left, down_right):
    tokens, width = hidden.shape
    sizes, mine = tuple(size for size, _ in chip_axes()), coordinates()
    block_rows, inner = gate_sources[0][0].shape[3:]
    count, tile = len(gate_sources), 256
    half = width // 2
    steps = inner // tile

    def kernel(me, hid, grad, gain_ref, wl, wr, *refs):
        gate_refs, up_refs, refs = refs[:count], refs[count : 2 * count], refs[2 * count :]
        out, back, back_low, normed, act, gate_back, up_back, gain_back = refs[:8]
        total, turned, gate_held, up_held = refs[8:]
        step = pl.program_id(0)
        w_gate = assemble(gate_held, gate_refs, gate_sources, me, 2, 1)
        w_up = assemble(up_held, up_refs, up_sources, me, 1, 2)

        @pl.when(step == 0)
        def _():
            value = hid[...]
            rms = lax.rsqrt(jnp.mean(value * value, axis=-1, keepdims=True) + epsilon)
            normed[...] = (value * rms * gain_ref[...]).astype(jnp.bfloat16)
            total[...] = jnp.zeros_like(total)
            turned[...] = jnp.zeros_like(turned)

        source, low = normed[...], grad[...]
        gate, up = bf_dot(source, w_gate), bf_dot(source, w_up)
        inner_grad = nt_dot(low[:, :half], wl[...]) + nt_dot(low[:, half:], wr[...])
        sig = jax.nn.sigmoid(gate)
        silu = gate * sig
        active = (silu * up).astype(jnp.bfloat16)
        gate_grad = (inner_grad * up * sig * (1.0 + gate * (1.0 - sig))).astype(jnp.bfloat16)
        up_grad = (inner_grad * silu).astype(jnp.bfloat16)
        act[...], gate_back[...], up_back[...] = active, gate_grad, up_grad
        total[:, :half] += bf_dot(active, wl[...])
        total[:, half:] += bf_dot(active, wr[...])
        turned[...] += nt_dot(gate_grad, w_gate) + nt_dot(up_grad, w_up)

        @pl.when(step == steps - 1)
        def _():
            value, back_in = hid[...], turned[...]
            rms = lax.rsqrt(jnp.mean(value * value, axis=-1, keepdims=True) + epsilon)
            out[...] = value + total[...]
            gain_back[...] = jnp.sum(back_in * value * rms, axis=0, keepdims=True)
            result = grad[...].astype(jnp.float32) + rms_back(back_in, value, rms, gain_ref[...])
            back[...] = result
            back_low[...] = result.astype(jnp.bfloat16)

    def whole(rows, columns):
        return pl.BlockSpec((rows, columns), lambda i, me: (0, 0))

    along = pl.BlockSpec((tile, half), lambda i, me: (i, 0))
    inner_spec = pl.BlockSpec((tokens, tile), lambda i, me: (0, i))
    inner_shape = jax.ShapeDtypeStruct((tokens, inner), jnp.bfloat16)
    arrays = [array for array, _, _ in gate_sources + up_sources]
    held = pltpu.VMEM(sizes + (block_rows, tile), jnp.bfloat16)
    return pl.pallas_call(
        kernel,
        out_shape=[
            jax.ShapeDtypeStruct((tokens, width), jnp.float32),
            jax.ShapeDtypeStruct((tokens, width), jnp.float32),
            jax.ShapeDtypeStruct((tokens, width), jnp.bfloat16),
            jax.ShapeDtypeStruct((tokens, width), jnp.bfloat16),
            inner_shape,
            inner_shape,
            inner_shape,
            jax.ShapeDtypeStruct((1, width), jnp.float32),
        ],
        grid_spec=pltpu.PrefetchScalarGridSpec(
            num_scalar_prefetch=1,
            grid=(steps,),
            in_specs=[whole(tokens, width), whole(tokens, width), whole(1, width), along, along]
            + [tile_spec(array, tile, lambda i, me: (0, 0, 0, 0, i)) for array in arrays],
            out_specs=[whole(tokens, width)] * 4 + [inner_spec] * 3 + [whole(1, width)],
            scratch_shapes=[
                pltpu.VMEM((tokens, width), jnp.float32),
                pltpu.VMEM((tokens, width), jnp.float32),
                held,
                held,
            ],
        ),
        compiler_params=pltpu.CompilerParams(vmem_limit_bytes=58 * 2**20),
        cost_estimate=takes(28),
    )(mine, hidden, out_grad, gain, down_left, down_right, *arrays)


def nt_dot(left, right):
    return lax.dot_general(left, right, (NT, ((), ())), preferred_element_type=jnp.float32)


def rms_back(grad_normed, source, inv_rms, gain_vec):
    scaled = grad_normed * gain_vec
    return inv_rms * (
        scaled - source * inv_rms * inv_rms * jnp.mean(scaled * source, axis=-1, keepdims=True)
    )


def local(
    inputs,
    doc_start,
    norm_gain,
    w_in,
    conv_weight,
    w_low,
    w_high,
    gate_bias,
    head_gain,
    w_out,
    ffn_gain,
    w_gate_up,
    w_down,
    out_grad,
):
    seq_count, block_len, model_width = inputs.shape
    row_count = seq_count * block_len
    key_width = HEADS * DK
    value_width = HEADS * DV
    conv_width = 2 * key_width + value_width
    block_start = lax.axis_index("seq") * block_len
    half = model_width // 2
    first_shard = by_head(w_in[:, :conv_width])
    taps = by_head(conv_weight)
    rest_shard = jnp.concatenate([w_in[:, conv_width:], w_out, w_down], axis=0)
    rest_cuts = [w_in.shape[0], w_out.shape[0], w_down.shape[0]]
    place = jnp.stack([block_start, lax.axis_index("seq") % GROUP]).astype(jnp.int32)
    starts = doc_start[:, :, None]
    gain_row = head_gain[None, :]
    axes = chip_axes()

    fast = gather_levels(first_shard)
    edge = shifted(inputs[:, block_len - HALO :, :], 1)
    wide = jnp.concatenate([edge, inputs], axis=1).astype(jnp.float32)
    wide_rms = lax.rsqrt(jnp.mean(wide * wide, axis=-1, keepdims=True) + epsilon)
    wide_normed = (wide * wide_rms * norm_gain).astype(jnp.bfloat16)
    layer_in = wide[:, HALO:].reshape(row_count, model_width)
    inv_rms = wide_rms[:, HALO:].reshape(row_count, 1)
    fast, wide_normed, rest_shard = together(fast, wide_normed, rest_shard)
    rest = gather_levels(rest_shard)
    fast = gather_first(fast)
    normed = wide_normed[:, HALO:].reshape(row_count, model_width)
    wide_rows = wide_normed.reshape(-1, model_width)
    lowrank = bf_dot(normed, w_low)
    gate_logit = (
        jnp.dot(lowrank, w_high, precision=highest, preferred_element_type=jnp.float32) + gate_bias
    )
    fast, gate_logit, rest[1] = together(fast, gate_logit, rest[1])
    fast = gather_second(fast)
    fast, rest[2], wide_shard = together(fast, rest[2], w_gate_up)
    fast = gather_cores(fast)
    wide_pieces = gather_levels(wide_shard)
    wide_mixed = projected(wide_rows, *[[(own, 0, 0), (other, 1, 0)] for own, other in fast])
    wide_mixed = wide_mixed.reshape(seq_count, HALO + block_len, conv_width)
    wide_mixed, rest = together(wide_mixed, rest)
    rest = gather_first(rest)
    logits = gate_logit.reshape(seq_count, block_len, key_width)
    local_out, reach, local_state, block_decay = mixer_forward(
        place, wide_mixed, taps, logits, starts
    )
    local_state, rest, wide_pieces[1] = together(local_state, rest, wide_pieces[1])
    got, _ = exchanged(local_state)
    got, rest = together(got, rest)
    rest = gather_second(rest)
    beyond = shifted(composed(place, got, False), GROUP)
    incoming = composed(place, got, False, beyond)
    incoming, rest, wide_pieces = together(incoming, rest, wide_pieces)
    wide_pieces = gather_first(wide_pieces)
    rest = gather_cores(rest)
    incoming, _ = exchanged(incoming)
    incoming, rest, wide_pieces = together(incoming, rest, wide_pieces)
    crossed = gather_second(wide_pieces)
    early = [swapped(pieces[0], 1) for pieces in crossed]
    incoming, fast = together(incoming, fast)
    [(left_full, right_full)] = gather_done(fast, [first_shard.shape[0]])
    (g_left, g_right), (out_left, out_right), (down_left, down_right) = gather_done(rest, rest_cuts)
    gate_cols = jnp.concatenate([bf_dot(normed, g_left), bf_dot(normed, g_right)], axis=1)
    gates = gate_cols.astype(jnp.bfloat16).reshape(seq_count, block_len, value_width)
    mixer_out, gated = mixer_output(place, local_out, reach, incoming, gates, gain_row)
    gated = gated.reshape(row_count, value_width)
    hidden_one = layer_in + jnp.concatenate(
        [bf_dot(gated, out_left), bf_dot(gated, out_right)], axis=1
    )
    hidden_one, crossed, early = together(hidden_one, crossed, early)
    gate_sources, up_sources = core_sources(crossed, early)
    out_rows_low = out_grad.reshape(row_count, model_width)
    (
        layer_out,
        hidden_grad,
        hidden_low,
        ffn_in,
        activation,
        gate_grad,
        up_grad,
        ffn_gain_row,
    ) = feed_forward(
        hidden_one, out_rows_low, ffn_gain[None, :], gate_sources, up_sources, down_left, down_right
    )
    gated_grad = nt_dot(hidden_low[:, :half], out_left) + nt_dot(hidden_low[:, half:], out_right)
    gated_grad = gated_grad.reshape(seq_count, block_len, value_width)
    mixer_grad, gate_vals_grad, state_term, head_gain_grad = mixer_output_back(
        place, mixer_out, reach, gated_grad, gates, gain_row, block_decay
    )
    gate_vals_grad = gate_vals_grad.reshape(row_count, value_width)

    state_term, gated, ffn_in, activation = together(state_term, gated, ffn_in, activation)
    got, (out_terms, wide_terms, down_terms) = exchanged(
        state_term,
        (
            (lambda: grad_products(gated, hidden_low),),
            (lambda _: grad_products(ffn_in, gate_grad, up_grad),),
            (lambda _: grad_products(activation, out_rows_low),),
        ),
    )
    wide_terms = cores_send([wide_terms])
    total = composed(place, got, True)
    total, parts, wide_terms = together(total, phase_parts(wide_terms, 0), wide_terms)
    wide_terms = phase_swap(wide_terms, 0, parts)
    beyond = shifted(total, -GROUP)
    g_terms = grad_products(normed, gate_vals_grad)
    beyond, g_terms, out_terms, down_terms = together(beyond, g_terms, out_terms, down_terms)
    rest_terms = cores_send([g_terms, out_terms, down_terms])
    outgoing = composed(place, got, True, beyond)
    shape = outgoing.shape
    outgoing = outgoing.reshape((2, 2, 2) + shape[1:])
    outgoing = jnp.stack(exchange_step(outgoing, 2, 1), axis=2)
    outgoing = jnp.stack(exchange_step(outgoing, 1, 2), axis=1)
    outgoing, wide_terms, rest_terms = together(outgoing, wide_terms, rest_terms)
    wide_terms = phase_send(wide_terms, 1)
    outgoing = jnp.stack(exchange_step(outgoing, 0, 4)).reshape(shape)
    outgoing, wide_terms = together(outgoing, wide_terms)
    wide_sums = level_sums(wide_terms)
    outgoing, wide_sums, rest_terms = together(outgoing, wide_sums, rest_terms)
    wide_own, wide_last = levels_send(wide_sums)
    rest_terms = phase_send(rest_terms, 0)
    backs = mixer_backward(
        place, wide_mixed, taps, logits, starts, mixer_grad, incoming, outgoing
    )
    backs, rest_terms, wide_last[0] = together(backs, rest_terms, wide_last[0])
    rest_terms = phase_send(rest_terms, 1)
    mixed_grad, back_edge, back_tail, tap_grads, logit_grad, gate_bias_grad = backs
    back_edge = shifted(back_edge.astype(jnp.bfloat16), -1).astype(jnp.float32)
    mixed_grad = lax.dynamic_update_slice(
        mixed_grad, (back_tail + back_edge).astype(jnp.bfloat16), (0, block_len - HALO, 0)
    )
    mixed_grad = mixed_grad.reshape(row_count, conv_width)
    small_rows, lowrank_grad = small_packed(
        logit_grad.reshape(row_count, key_width),
        lowrank,
        w_high,
        normed,
        tap_grads,
        gate_bias_grad.reshape(seq_count, key_width),
        head_gain_grad,
        ffn_gain_row,
    )
    normed_grad = (
        nt_dot(mixed_grad[:, : conv_width // 2], left_full)
        + nt_dot(mixed_grad[:, conv_width // 2 :], right_full)
        + nt_dot(gate_vals_grad[:, :half], g_left)
        + nt_dot(gate_vals_grad[:, half:], g_right)
        + nt_dot(lowrank_grad, w_low)
    )
    norm_gain_grad = jnp.sum(normed_grad * layer_in * inv_rms, axis=0)
    input_grad = hidden_grad + rms_back(normed_grad, layer_in, inv_rms, norm_gain)
    small_rows = lax.dynamic_update_slice(small_rows, norm_gain_grad[None, :], (34, 0))
    mixed_grad, small_rows, rest_terms, input_grad, wide_last[1] = together(
        mixed_grad, small_rows, rest_terms, input_grad, wide_last[1]
    )
    rest_sums = level_sums(rest_terms)
    small_rows = spread(small_rows, axes[3])
    mixed_grad, rest_sums, small_rows = together(mixed_grad, rest_sums, small_rows)
    rest_own, rest_last = levels_send(rest_sums)
    fast_terms = grad_products(normed, mixed_grad)
    small_rows = spread(sum(small_rows), axes[2])
    fast_terms, small_rows, wide_last[2] = together(fast_terms, small_rows, wide_last[2])
    fast_terms = cores_send([fast_terms])
    small_rows = spread(sum(small_rows), axes[1])
    fast_terms, small_rows = together(fast_terms, small_rows)
    fast_terms = phase_send(fast_terms, 0)
    small_rows = sum(small_rows)
    fast_terms, small_rows, rest_last[0] = together(fast_terms, small_rows, rest_last[0])
    fast_terms = phase_send(fast_terms, 1)
    fast_terms, rest_last[1] = together(fast_terms, rest_last[1])
    fast_own, fast_last = levels_send(level_sums(fast_terms))
    small_rows = [small_rows]
    small_own = sum(small_rows)
    small_parts = [small_own] + spread(small_own.astype(jnp.bfloat16), axes[0])[1:]
    norm_gain_grad, conv_weight_grad, w_low_grad, w_high_grad, *rows_found = small_unpacked(
        small_parts, key_width, w_high.shape[0]
    )
    gate_bias_grad, head_gain_grad, ffn_gain_grad = [row[0] for row in rows_found]
    rest_grad = reduced(rest_own, rest_last)
    w_gate_up_grad = reduced(wide_own, wide_last)
    fast_grad = by_kind(reduced(fast_own, fast_last))
    ends = [rest_cuts[0], rest_cuts[0] + rest_cuts[1]]
    w_in_grad = jnp.concatenate([fast_grad, rest_grad[: ends[0]]], axis=1)
    w_out_grad = rest_grad[ends[0] : ends[1]]
    w_down_grad = rest_grad[ends[1] :]
    return (
        layer_out.reshape(seq_count, block_len, model_width),
        input_grad.reshape(seq_count, block_len, model_width),
        norm_gain_grad[0],
        w_in_grad,
        conv_weight_grad,
        w_low_grad.T,
        w_high_grad,
        gate_bias_grad,
        head_gain_grad,
        w_out_grad,
        ffn_gain_grad,
        w_gate_up_grad,
        w_down_grad,
    )


def solution(mesh):
    placed = (
        P(None, "seq", None),
        P(None, "seq"),
        P(),
        P("seq", None),
        P(),
        P(),
        P(),
        P(),
        P(),
        P("seq", None),
        P(),
        P("seq", None),
        P("seq", None),
        P(None, "seq", None),
    )
    return jax.shard_map(
        local,
        mesh=mesh,
        in_specs=placed,
        out_specs=(
            P(None, "seq", None),
            P(None, "seq", None),
            P(),
            P("seq", None),
            P(),
            P(),
            P(),
            P(),
            P(),
            P("seq", None),
            P(),
            P("seq", None),
            P("seq", None),
        ),
        check_vma=False,
    )
```

```python
import jax
import jax.numpy as jnp
from jax import lax
from jax.experimental import pallas as pl
from jax.experimental.pallas import tpu as pltpu
from jax.sharding import PartitionSpec as P

HEADS = 4
DK = 128
DV = 256
FF = 2816
WIDE = 128
CONV = 4


epsilon = 1e-06
gate_scale = 16.0
highest = lax.Precision.HIGHEST


GROUP = 8
HALO = 8
EXTRA = 16
SMALL = 40
PER_HEAD = 2 * DK + DV


def chip_axes():
    count = lax.axis_size("seq")
    sides = {16: (4, 2, 2), 64: (4, 4, 4)}.get(count // 2, (count // 2, 1, 1))
    return (
        (sides[0], 2 * sides[1] * sides[2]),
        (sides[1], 2 * sides[2]),
        (sides[2], 2),
        (2, 1),
    )


def swapped(array, mask):
    count = lax.axis_size("seq")
    return lax.ppermute(array, "seq", [(i, i ^ mask) for i in range(count)])


def shifted(array, by):
    count = lax.axis_size("seq")
    pairs = [(i, i + by) for i in range(count) if 0 <= i + by < count]
    return lax.ppermute(array, "seq", pairs)


def spread(block, axis):
    size, stride = axis
    return [block] + [swapped(block, step * stride) for step in range(1, size)]


def takes(micros):
    return pl.CostEstimate(flops=int(micros * 1e9), bytes_accessed=0, transcendentals=0)


def coordinates():
    mine = lax.axis_index("seq")
    return jnp.stack([(mine // stride) % size for size, stride in chip_axes()]).astype(jnp.int32)


def placed_blocks(sources, one, two, cuts):
    axes = chip_axes()
    sizes = tuple(size for size, _ in axes)
    depth, mine = sizes[0], coordinates()
    (rows, columns), kind = sources[0][0].shape[3:], sources[0][0].dtype

    def target(core, second, first, me):
        spot = [0, 0, 0, 0]
        spot[one] = jnp.bitwise_xor(first, me[one])
        spot[two] = jnp.bitwise_xor(second, me[two])
        spot[3] = jnp.bitwise_xor(core, me[3])
        return tuple(spot) + (0, 0)

    def source(mine_core, base, extent):
        def index(core, second, first, me):
            step = core * sizes[two] + second - mine_core * sizes[two] - base
            early, late = step < 0, step >= extent
            held = jnp.where(early, 0, jnp.where(late, extent - 1, step))
            return (
                held,
                jnp.where(early, 0, jnp.where(late, sizes[one] - 1, first)),
                0,
                0,
                0,
            )

        return index

    def kernel(me, *refs):
        pieces, outs = refs[: len(sources)], refs[len(sources) :]
        step = pl.program_id(0) * sizes[two] + pl.program_id(1)
        for piece, (array, core, base) in zip(pieces, sources):
            begin = core * sizes[two] + base

            @pl.when((step >= begin) & (step < begin + array.shape[0]))
            def _():
                for level in range(depth):
                    block, start = piece[0, 0, level], 0
                    for out, cut in zip(outs, cuts):
                        out[jnp.bitwise_xor(me[0], level), 0, 0, 0] = block[start : start + cut]
                        start += cut

    found = pl.pallas_call(
        kernel,
        out_shape=[jax.ShapeDtypeStruct(sizes + (cut, columns), kind) for cut in cuts],
        grid_spec=pltpu.PrefetchScalarGridSpec(
            num_scalar_prefetch=1,
            grid=(2, sizes[two], sizes[one]),
            in_specs=[
                pl.BlockSpec((1, 1, depth, rows, columns), source(core, base, array.shape[0]))
                for array, core, base in sources
            ],
            out_specs=[pl.BlockSpec((depth, 1, 1, 1, cut, columns), target) for cut in cuts],
        ),
        compiler_params=pltpu.CompilerParams(vmem_limit_bytes=40 * 2**20),
        cost_estimate=takes(1.0 + rows * columns * 5e-5),
    )(mine, *[array for array, _, _ in sources])
    return [array.reshape(-1, columns) for array in found]


def together(*values):
    return lax.optimization_barrier(values)


def gather_levels(shard):
    return spread(shard, chip_axes()[0])


def gather_first(levels):
    stacked = levels if isinstance(levels, jax.Array) else jnp.stack(levels)
    half = stacked.shape[2] // 2
    axes = chip_axes()
    return [spread(stacked[..., :half], axes[2]), spread(stacked[..., half:], axes[1])]


def gather_second(sides):
    axes = chip_axes()
    return [spread(jnp.stack(sides[0]), axes[1]), spread(jnp.stack(sides[1]), axes[2])]


def gather_cores(crossed):
    found = []
    for pieces in crossed:
        own = jnp.stack(pieces)
        found.append([own, swapped(own, 1)])
    return found


def gather_done(pairs, cuts):
    halves = [
        placed_blocks([(own, 0, 0), (other, 1, 0)], one, two, cuts)
        for (own, other), one, two in zip(pairs, (2, 1), (1, 2))
    ]
    return list(zip(*halves))


def core_sources(crossed, early):
    halves = []
    for pieces, before in zip(crossed, early):
        sources = []
        for step, piece in enumerate(pieces):
            other = before if step == 0 else swapped(piece, 1)
            sources.extend([(piece[None], 0, step), (other[None], 1, step)])
        halves.append(sources)
    return halves


def assemble(held, refs, sources, me, one, two):
    for ref, (array, core, base) in zip(refs, sources):
        for second in range(array.shape[0]):
            for first in range(array.shape[1]):
                for level in range(array.shape[2]):
                    spot = [jnp.bitwise_xor(me[0], level), 0, 0, jnp.bitwise_xor(me[3], core)]
                    spot[one] = jnp.bitwise_xor(me[one], first)
                    spot[two] = jnp.bitwise_xor(me[two], base + second)
                    held[tuple(spot)] = ref[second, first, level]
    return held[...].reshape(-1, held.shape[-1])


def tile_spec(array, tile, index):
    return pl.BlockSpec(array.shape[:4] + (tile,), index)


def projected(rows, sources_a, sources_b):
    sizes, mine = tuple(size for size, _ in chip_axes()), coordinates()
    tokens, width = rows.shape
    block_rows, half = sources_a[0][0].shape[3:]
    tile = 512
    tiles = half // tile

    def kernel(me, row_ref, *refs):
        refs_a = refs[: len(sources_a)]
        refs_b = refs[len(sources_a) : -2]
        out, held = refs[-2:]

        @pl.when(pl.program_id(0) == 0)
        def _():
            assemble(held, refs_a, sources_a, me, 2, 1)

        @pl.when(pl.program_id(0) == 1)
        def _():
            assemble(held, refs_b, sources_b, me, 1, 2)

        full = held[...].reshape(width, tile)
        out[...] = bf_dot(row_ref[...], full).astype(jnp.bfloat16)

    def at_a(part, i, me):
        return (0, 0, 0, 0, jnp.where(part == 0, i, tiles - 1))

    def at_b(part, i, me):
        return (0, 0, 0, 0, jnp.where(part == 0, 0, i))

    return pl.pallas_call(
        kernel,
        out_shape=jax.ShapeDtypeStruct((tokens, 2 * half), jnp.bfloat16),
        grid_spec=pltpu.PrefetchScalarGridSpec(
            num_scalar_prefetch=1,
            grid=(2, tiles),
            in_specs=[pl.BlockSpec((tokens, width), lambda part, i, me: (0, 0))]
            + [tile_spec(array, tile, at_a) for array, _, _ in sources_a]
            + [tile_spec(array, tile, at_b) for array, _, _ in sources_b],
            out_specs=pl.BlockSpec((tokens, tile), lambda part, i, me: (0, part * tiles + i)),
            scratch_shapes=[pltpu.VMEM(sizes + (block_rows, tile), jnp.bfloat16)],
        ),
        compiler_params=pltpu.CompilerParams(vmem_limit_bytes=40 * 2**20),
        cost_estimate=takes(6),
    )(mine, rows, *[array for array, _, _ in sources_a + sources_b])


def grad_products(left, right_a, right_b=None):
    sizes = tuple(size for size, _ in chip_axes())
    strides = tuple(stride for _, stride in chip_axes())
    (tokens, features), columns = left.shape, right_a.shape[1]
    if right_b is None:
        columns = columns // 2
    count, mine = lax.axis_size("seq"), coordinates()
    rows = features // count
    tile = next(t for t in (512, 1408, 256) if columns % t == 0)
    chunks = next(c for c in (4, 2, 1) if features // c % 128 == 0)
    chunk = features // chunks

    def kernel(me, left_ref, a_ref, b_ref, away_a, keep_a, away_b, keep_b, flipped):
        @pl.when(pl.program_id(0) == 0)
        def _():
            flipped[...] = left_ref[...].T

        def products(odd):
            for right, away, keep, order in (
                (a_ref, away_a, keep_a, (2, 1, 0)),
                (b_ref, away_b, keep_b, (1, 2, 0)),
            ):
                for part in range(chunks):
                    full = jnp.dot(
                        flipped[part * chunk : (part + 1) * chunk],
                        right[...],
                        preferred_element_type=jnp.float32,
                    )
                    for start in range(0, chunk, rows):
                        device = (part * chunk + start) // rows
                        spot = tuple(
                            jnp.bitwise_xor(device // strides[axis] % sizes[axis], me[axis])
                            for axis in order
                        )
                        target = keep if device % 2 == odd else away
                        target[spot] = full[start : start + rows].astype(jnp.bfloat16)

        @pl.when(me[3] == 0)
        def _():
            products(0)

        @pl.when(me[3] == 1)
        def _():
            products(1)

    def result(one, two):
        shape = (sizes[one], sizes[two], sizes[0], rows)
        return (
            jax.ShapeDtypeStruct(shape + (columns,), jnp.bfloat16),
            pl.BlockSpec(shape + (tile,), lambda i, me: (0, 0, 0, 0, i)),
        )

    results = [result(2, 1), result(2, 1), result(1, 2), result(1, 2)]
    skip = columns // tile if right_b is None else 0
    right_b = right_a if right_b is None else right_b
    return pl.pallas_call(
        kernel,
        out_shape=[shape for shape, _ in results],
        grid_spec=pltpu.PrefetchScalarGridSpec(
            num_scalar_prefetch=1,
            grid=(columns // tile,),
            in_specs=[
                pl.BlockSpec((tokens, features), lambda i, me: (0, 0)),
                pl.BlockSpec((tokens, tile), lambda i, me: (0, i)),
                pl.BlockSpec((tokens, tile), lambda i, me: (0, i + skip)),
            ],
            out_specs=[spec for _, spec in results],
            scratch_shapes=[pltpu.VMEM((features, tokens), jnp.bfloat16)],
        ),
        compiler_params=pltpu.CompilerParams(vmem_limit_bytes=48 * 2**20),
        cost_estimate=takes(1.5 + features * columns * 4.5e-6),
    )(mine, left, right_a, right_b)


def total_of(groups):
    parts = []
    for refs, lead in groups:
        rows = [ref[(0,) * lead].astype(jnp.float32) for ref in refs]
        parts.append(jnp.concatenate(rows, axis=0) if len(rows) > 1 else rows[0])
    return sum(parts[1:], parts[0])


def flat_terms(terms):
    return [(since, arrays) for since, group in enumerate(terms) for arrays in group]


def regrouped(refs, flat):
    groups, at = [], 0
    for since, arrays in flat:
        groups.append((refs[at : at + len(arrays)], since))
        at += len(arrays)
    return groups, at


def phase_sums(pair, phase, step):
    flats = [flat_terms(terms) for terms in pair]
    depth = chip_axes()[0][0]
    second = chip_axes()[1][0] if phase == 0 else 1
    rows = sum(array.shape[-2] for array in flats[0][0][1])
    columns = flats[0][0][1][0].shape[-1]
    lead = 2 - phase

    def index(since):
        def found(i, j):
            spot = [0 if dim < phase else step if dim == phase else (i, j)[dim - 1] for dim in range(3)]
            return tuple(spot[since:]) + (0, 0)

        return found

    def kernel(*refs):
        ins, outs = refs[:-2], refs[-2:]
        at = 0
        for flat, out in zip(flats, outs):
            groups, used = regrouped(ins[at:], flat)
            at += used
            total = total_of([(part, 3 - since) for part, since in groups])
            out[(0,) * lead] = total.astype(jnp.bfloat16)

    arrays = [(array, since) for flat in flats for since, group in flat for array in group]
    shape = ((second, depth) if phase == 0 else (depth,)) + (rows, columns)
    out_spec = pl.BlockSpec(
        (1,) * lead + (rows, columns), lambda i, j: ((i, j) if phase == 0 else (j,)) + (0, 0)
    )
    return pl.pallas_call(
        kernel,
        out_shape=[jax.ShapeDtypeStruct(shape, jnp.bfloat16)] * 2,
        grid=(second, depth),
        in_specs=[
            pl.BlockSpec((1,) * (3 - since) + array.shape[-2:], index(since))
            for array, since in arrays
        ],
        out_specs=[out_spec] * 2,
        compiler_params=pltpu.CompilerParams(vmem_limit_bytes=32 * 2**20),
        cost_estimate=takes(3),
    )(*[array for array, _ in arrays])


def level_sums(pair):
    flats = [flat_terms(terms) for terms in pair]
    depth = chip_axes()[0][0]
    rows = sum(array.shape[-2] for array in flats[0][0][1])
    columns = flats[0][0][1][0].shape[-1]

    def kernel(*refs):
        ins, outs = refs[:-depth], refs[-depth:]
        at = 0
        for side, flat in enumerate(flats):
            groups, used = regrouped(ins[at:], flat)
            at += used
            cut = slice(side * columns, (side + 1) * columns)
            for level in range(depth):
                parts = []
                for part, since in groups:
                    spot = (0,) * (2 - since) + (level,)
                    values = [ref[spot].astype(jnp.float32) for ref in part]
                    parts.append(
                        jnp.concatenate(values, axis=0) if len(values) > 1 else values[0]
                    )
                total = sum(parts[1:], parts[0])
                outs[level][:, cut] = total.astype(outs[level].dtype)

    arrays = [(array, since) for flat in flats for since, group in flat for array in group]

    def spec(array, since):
        lead = (1,) * (2 - since) + (depth,)
        return pl.BlockSpec(lead + array.shape[-2:], lambda i: (0,) * (len(lead) + 2))

    shape = (rows, 2 * columns)
    return pl.pallas_call(
        kernel,
        out_shape=[jax.ShapeDtypeStruct(shape, jnp.float32)]
        + [jax.ShapeDtypeStruct(shape, jnp.bfloat16)] * (depth - 1),
        grid=(1,),
        in_specs=[spec(array, since) for array, since in arrays],
        out_specs=[pl.BlockSpec(shape, lambda i: (0, 0))] * depth,
        compiler_params=pltpu.CompilerParams(vmem_limit_bytes=40 * 2**20),
        cost_estimate=takes(3),
    )(*[array for array, _ in arrays])


def cores_send(products):
    found = []
    for keep, which in ((1, 0), (3, 2)):
        aways = [part[which] for part in products]
        away = jnp.concatenate(aways, axis=3) if len(aways) > 1 else aways[0]
        found.append([[[part[keep] for part in products], [swapped(away, 1)]]])
    return found


def phase_parts(pair, phase):
    return [phase_sums(pair, phase, step) for step in range(1, chip_axes()[2][0])]


def phase_swap(pair, phase, parts):
    axes, received = chip_axes(), [[], []]
    for step, sides in enumerate(parts):
        for side, part in enumerate(sides):
            stride = axes[((2, 1), (1, 2))[side][phase]][1]
            received[side].append([swapped(part, (step + 1) * stride)])
    return [terms + [parts] for terms, parts in zip(pair, received)]


def phase_send(pair, phase):
    return phase_swap(pair, phase, phase_parts(pair, phase))


def levels_send(sums):
    own, *parts = sums
    stride = chip_axes()[0][1]
    return own, [swapped(part, (step + 1) * stride) for step, part in enumerate(parts)]


def reduced(own, found):
    return sum((part.astype(jnp.float32) for part in found), own)


def small_packed(logit_grad, lowrank, w_high, normed, tap_grads, bias, head_gain, ffn_gain):
    tokens, keys = logit_grad.shape
    width, rank = normed.shape[1], w_high.shape[0]

    def kernel(grad_ref, low_ref, high_ref, normed_ref, taps, bias_ref, head, ffn, out, low_grad):
        grad = grad_ref[...]
        back = split_dot(grad, high_ref[...], NT).astype(jnp.bfloat16)
        low_grad[...] = back
        out[:rank] = lax.dot_general(
            back, normed_ref[...], (TN, ((), ())), preferred_element_type=jnp.float32
        )
        tap = jnp.sum(taps[...], axis=0)
        out[rank : rank + CONV] = tap[:, :width]
        out[rank + CONV : rank + 2 * CONV] = tap[:, width:]
        high = split_dot(low_ref[...], grad, TN)
        out[24:32, :keys] = high[:8]
        out[24:32, keys:] = high[8:]
        out[32:40] = jnp.zeros((8, width), jnp.float32)
        out[32:33, :keys] = jnp.sum(bias_ref[...], axis=0, keepdims=True)
        gains = [jnp.sum(head[:, h, 0], axis=0, keepdims=True) for h in range(HEADS)]
        out[32:33, keys : keys + DV] = sum(gains)
        out[33:34] = ffn[...]

    return pl.pallas_call(
        kernel,
        out_shape=[
            jax.ShapeDtypeStruct((SMALL, width), jnp.float32),
            jax.ShapeDtypeStruct((tokens, rank), jnp.bfloat16),
        ],
        compiler_params=pltpu.CompilerParams(vmem_limit_bytes=32 * 2**20),
        cost_estimate=takes(4),
    )(logit_grad, lowrank, w_high, normed, tap_grads, bias, head_gain, ffn_gain)


def small_unpacked(parts, keys, rank):
    width = parts[0].shape[1]

    def kernel(*refs):
        ins, (norm, conv, low, high, bias, head, ffn) = refs[: len(parts)], refs[len(parts) :]
        values = [ref[...].astype(jnp.float32) for ref in ins]
        while len(values) > 1:
            values = [sum(values[at : at + 2]) for at in range(0, len(values), 2)]
        total = values[0]
        low[...] = total[:rank]
        for h in range(HEADS):
            side, at = divmod(h * PER_HEAD, width)
            block = total[rank + side * CONV : rank + (side + 1) * CONV]
            conv[:, h * DK : (h + 1) * DK] = block[:, at : at + DK]
            conv[:, keys + h * DK : keys + (h + 1) * DK] = block[:, at + DK : at + 2 * DK]
            conv[:, 2 * keys + h * DV : 2 * keys + (h + 1) * DV] = block[
                :, at + 2 * DK : at + PER_HEAD
            ]
        high[:8] = total[24:32, :keys]
        high[8:] = total[24:32, keys:]
        bias[...] = total[32:33, :keys]
        head[...] = total[32:33, keys : keys + DV]
        ffn[...] = total[33:34]
        norm[...] = total[34:35]

    shapes = ((1, width), (CONV, 2 * width), (rank, width), (rank, keys))
    shapes += ((1, keys), (1, DV), (1, width))
    return pl.pallas_call(
        kernel,
        out_shape=[jax.ShapeDtypeStruct(shape, jnp.float32) for shape in shapes],
        cost_estimate=takes(2),
    )(*parts)


def by_head(array):
    lead, (keys, values) = array.shape[:-1], (HEADS * DK, HEADS * DV)
    parts = [
        part.reshape(lead + (HEADS, -1))
        for part in (array[..., :keys], array[..., keys : 2 * keys], array[..., 2 * keys :])
    ]
    return jnp.concatenate(parts, axis=-1).reshape(lead + (2 * keys + values,))


def by_kind(array):
    lead = array.shape[:-1]
    array = array.reshape(lead + (HEADS, -1))
    parts = (array[..., :DK], array[..., DK : 2 * DK], array[..., 2 * DK :])
    return jnp.concatenate([part.reshape(lead + (-1,)) for part in parts], axis=-1)


def exchange_step(pieces, at, mask):
    kept = lax.index_in_dim(pieces, 0, at, False)
    return [kept, swapped(lax.index_in_dim(pieces, 1, at, False), mask)]


def exchanged(pieces, fillers=((), (), ())):
    shape, filled = pieces.shape, []
    pieces = pieces.reshape((2, 2, 2) + shape[1:])
    for at, mask, filler in zip((2, 1, 0), (1, 2, 4), fillers):
        pair = exchange_step(pieces, at, mask)
        if filler:
            values = filler[0](*filled[-1:])
            pair, values = together(pair, values)
            filled.append(values)
        pieces = jnp.stack(pair, axis=at)
    return pieces.reshape(shape), filled


def column(row):
    square = jnp.broadcast_to(row, (DK, DK)).T
    return jnp.concatenate([square, square], axis=1)


def packed_rows(state, decay):
    high = decay.astype(jnp.bfloat16)
    low = (decay - high.astype(jnp.float32)).astype(jnp.bfloat16)
    tail = jnp.broadcast_to(jnp.concatenate([high, low], axis=1), (EXTRA, DV))
    return jnp.concatenate([state.astype(jnp.bfloat16), tail], axis=0)


def composed(place, got, backward, beyond=None):
    order = range(GROUP)[::-1] if backward else range(GROUP)

    def kernel(place_ref, got_ref, *refs):
        mine, out = place_ref[1], refs[-1]
        running = jnp.zeros((DK, DV), jnp.float32)
        reach = jnp.ones((DK, DV), jnp.float32)
        far = None if beyond is None else refs[0][...].astype(jnp.float32)
        for index in order:
            spot = jnp.bitwise_xor(mine, index)
            piece = got_ref[spot].astype(jnp.float32)
            if beyond is not None:
                out[spot] = (running + reach * far).astype(jnp.bfloat16)
            tail = piece[DK : DK + 1]
            kept = column(tail[:, :DK] + tail[:, DK:])
            running = kept * running + piece[:DK]
            reach = reach * kept
        if beyond is None:
            out[...] = running.astype(jnp.bfloat16)

    extra = () if beyond is None else (beyond,)
    shape = (DK, DV) if beyond is None else (GROUP, DK, DV)
    return pl.pallas_call(
        kernel,
        out_shape=jax.ShapeDtypeStruct(shape, jnp.bfloat16),
        in_specs=[pl.BlockSpec(memory_space=pltpu.SMEM)]
        + [pl.BlockSpec(memory_space=pltpu.VMEM)] * (1 + len(extra)),
        out_specs=pl.BlockSpec(memory_space=pltpu.VMEM),
        cost_estimate=takes(2),
    )(place, got, *extra)


def split_dot(left, right, dims):
    dims = (dims, ((), ()))
    left_high, right_high = left.astype(jnp.bfloat16), right.astype(jnp.bfloat16)
    left_low = (left - left_high.astype(jnp.float32)).astype(jnp.bfloat16)
    right_low = (right - right_high.astype(jnp.float32)).astype(jnp.bfloat16)

    def one(a, b):
        return lax.dot_general(a, b, dims, preferred_element_type=jnp.float32)

    return one(left_high, right_high) + (one(left_high, right_low) + one(left_low, right_high))


def unit_dot(unit, value, dims):
    high = value.astype(jnp.bfloat16)
    rest = value - high.astype(jnp.float32)
    middle = rest.astype(jnp.bfloat16)
    low = (rest - middle.astype(jnp.float32)).astype(jnp.bfloat16)
    unit = unit.astype(jnp.bfloat16)
    return sum(
        lax.dot_general(unit, part, (dims, ((), ())), preferred_element_type=jnp.float32)
        for part in (low, middle, high)
    )


NN, NT, TN = ((1,), (0,)), ((1,), (1,)), ((0,), (0,))


def activations(block, taps, starts, first, block_len):
    pos = first + lax.broadcasted_iota(jnp.int32, (block_len, 1), 0)
    wide = block[0].astype(jnp.float32)
    total = taps[0:1, :] * wide[HALO:]
    for tap in range(1, CONV):
        usable = (pos - tap >= starts).astype(jnp.float32)
        total = total + taps[tap : tap + 1, :] * wide[HALO - tap : HALO - tap + block_len] * usable
    sig = jax.nn.sigmoid(total)
    active = total * sig
    query, key, value = active[:, :DK], active[:, DK : 2 * DK], active[:, 2 * DK :]
    return pos, (wide, total, sig), query * DK ** (-0.5), key, value


def decays(logit):
    return (jnp.minimum(logit, 0.0) - jnp.log1p(jnp.exp(-jnp.abs(logit)))) / gate_scale


class Span:
    def __init__(self, index, first, query, key, value, decay, starts, pos):
        rows = slice(index * WIDE, (index + 1) * WIDE)
        self.rows, first_pos = rows, first + index * WIDE
        self.query, self.key, self.value = query[rows], key[rows], value[rows]
        decay, starts, pos = decay[rows], starts[rows], pos[rows]
        t = lax.broadcasted_iota(jnp.int32, (WIDE, WIDE), 0)
        u = lax.broadcasted_iota(jnp.int32, (WIDE, WIDE), 1)
        self.lower = (u <= t).astype(jnp.float32)
        self.upper = (u >= t).astype(jnp.float32)
        self.allowed = (u <= t) & (u + first_pos >= starts)
        cum = unit_dot(self.lower, decay, NN)
        self.total = cum[WIDE - 1 :]
        middle = cum[WIDE // 2 - 1 : WIDE // 2]
        self.to_query, self.to_key = jnp.exp(cum - middle), jnp.exp(middle - cum)
        self.carried = (starts < first_pos).astype(jnp.float32)
        self.kept = (starts[WIDE - 1 :] < first_pos).astype(jnp.float32)
        self.from_start = jnp.exp(cum) * self.carried
        self.to_end = jnp.exp(self.total - cum) * (pos >= starts[WIDE - 1 :]).astype(jnp.float32)
        self.query_centred = self.query * self.to_query
        self.key_centred = self.key * self.to_key
        self.query_start = self.query * self.from_start
        self.key_end = self.key * self.to_end
        self.cum = cum
        ones = jnp.ones((WIDE, DV), jnp.float32)
        total_column = unit_dot_right(decay, ones)
        self.keep_column = jnp.exp(total_column) * self.kept

    def scores(self):
        raw = split_dot(self.query_centred, self.key_centred, NT)
        return jnp.where(self.allowed, raw, 0.0)

    def next_state(self, state):
        update = split_dot(self.key_end, self.value, TN)
        return update if state is None else state * self.keep_column + update


def unit_dot_right(value, unit):
    high = value.astype(jnp.bfloat16)
    rest = value - high.astype(jnp.float32)
    middle = rest.astype(jnp.bfloat16)
    low = (rest - middle.astype(jnp.float32)).astype(jnp.bfloat16)
    unit = unit.astype(jnp.bfloat16)
    return sum(
        lax.dot_general(part, unit, (TN, ((), ())), preferred_element_type=jnp.float32)
        for part in (low, middle, high)
    )


def mixer_specs(block_len):
    return [
        pl.BlockSpec((1, HALO + block_len, PER_HEAD), lambda s, h, first: (s, 0, h)),
        pl.BlockSpec((CONV, PER_HEAD), lambda s, h, first: (0, h)),
        pl.BlockSpec((1, block_len, DK), lambda s, h, first: (s, 0, h)),
        pl.BlockSpec((1, block_len, 1), lambda s, h, first: (s, 0, 0)),
    ]


def key_spec(block_len):
    return pl.BlockSpec((1, block_len, DK), lambda s, h, first: (s, 0, h))


def value_spec(block_len):
    return pl.BlockSpec((1, block_len, DV), lambda s, h, first: (s, 0, h))


def pair_spec(rows):
    return pl.BlockSpec(
        (1, rows, DV), lambda s, h, place: (jnp.bitwise_xor(place[1], s * HEADS + h), 0, 0)
    )


decay_spec = pl.BlockSpec((1, 1, 1, DK), lambda s, h, first: (s, h, 0, 0))


def launch(kernel, inputs, in_specs, outputs, out_specs, seq_count, micros):
    return pl.pallas_call(
        kernel,
        out_shape=[jax.ShapeDtypeStruct(shape, kind) for shape, kind in outputs],
        grid_spec=pltpu.PrefetchScalarGridSpec(
            num_scalar_prefetch=1,
            grid=(seq_count, HEADS),
            in_specs=in_specs,
            out_specs=out_specs,
        ),
        compiler_params=pltpu.CompilerParams(vmem_limit_bytes=40 * 2**20),
        cost_estimate=takes(micros),
    )(*inputs)


def mixer_forward(first, wide_mixed, conv_weight, logits, starts):
    seq_count, block_len = starts.shape[:2]

    def kernel(first_ref, block, taps, logit_ref, start_ref, out, reach, state, decay):
        first, starts = first_ref[0], start_ref[0]
        pos, _, query, key, value = activations(block, taps, starts, first, block_len)
        log_decay = decays(logit_ref[0])
        running = None
        before = jnp.zeros((1, DK), jnp.float32)
        reach_in = (starts < first).astype(jnp.float32)
        for index in range(block_len // WIDE):
            span = Span(index, first, query, key, value, log_decay, starts, pos)
            result = split_dot(span.scores(), span.value, NN)
            if running is not None:
                result = result + split_dot(span.query_start, running, NN)
            out[0, span.rows] = result
            reach[0, span.rows] = span.query * jnp.exp(before + span.cum) * reach_in[span.rows]
            before = before + span.total
            running = span.next_state(running)
        block_decay = jnp.exp(before) * reach_in[block_len - 1 :]
        state[0] = packed_rows(running, block_decay)
        decay[0, 0] = block_decay

    return launch(
        kernel,
        (first, wide_mixed, conv_weight, logits, starts),
        mixer_specs(block_len),
        (
            ((seq_count, block_len, HEADS * DV), jnp.float32),
            ((seq_count, block_len, HEADS * DK), jnp.float32),
            ((GROUP, DK + EXTRA, DV), jnp.bfloat16),
            ((seq_count, HEADS, 1, DK), jnp.float32),
        ),
        [value_spec(block_len), key_spec(block_len), pair_spec(DK + EXTRA), decay_spec],
        seq_count,
        13,
    )


def mixer_output(first, local_out, reach, incoming, gates, head_gain):
    seq_count, block_len = reach.shape[:2]

    def kernel(first_ref, local, reach_ref, state, gate, gain, out, gated):
        result = local[0] + split_dot(reach_ref[0], state[0].astype(jnp.float32), NN)
        out[0] = result
        rms = lax.rsqrt(jnp.mean(result * result, axis=-1, keepdims=True) + epsilon)
        value = gate[0].astype(jnp.float32)
        gated[0] = (result * rms * gain[...] * (value * jax.nn.sigmoid(value))).astype(jnp.bfloat16)

    values = value_spec(block_len)
    return launch(
        kernel,
        (first, local_out, reach, incoming, gates, head_gain),
        [values, key_spec(block_len), pair_spec(DK), values]
        + [pl.BlockSpec((1, DV), lambda s, h, first: (0, 0))],
        (
            ((seq_count, block_len, HEADS * DV), jnp.float32),
            ((seq_count, block_len, HEADS * DV), jnp.bfloat16),
        ),
        [values, values],
        seq_count,
        4,
    )


def mixer_output_back(first, mixer_out, reach, gated_grad, gates, head_gain, decay):
    seq_count, block_len = reach.shape[:2]

    def kernel(
        first_ref,
        mixed,
        reach_ref,
        grad_ref,
        gate,
        gain,
        decay_ref,
        out_grad,
        gate_grad,
        term,
        gain_grad,
    ):
        result, grad = mixed[0], grad_ref[0]
        rms = lax.rsqrt(jnp.mean(result * result, axis=-1, keepdims=True) + epsilon)
        value = gate[0].astype(jnp.float32)
        sig = jax.nn.sigmoid(value)
        inner = grad * (value * sig)
        normed = result * rms
        gate_grad[0] = (
            grad * (normed * gain[...]) * sig * (1.0 + value * (1.0 - sig))
        ).astype(jnp.bfloat16)
        gain_grad[0, 0] = jnp.sum(inner * normed, axis=0, keepdims=True)
        scaled = inner * gain[...]
        grad_out = rms * (
            scaled - normed * rms * jnp.mean(scaled * result, axis=-1, keepdims=True)
        )
        out_grad[0] = grad_out
        term[0] = packed_rows(split_dot(reach_ref[0], grad_out, TN), decay_ref[0, 0])

    values = value_spec(block_len)
    return launch(
        kernel,
        (first, mixer_out, reach, gated_grad, gates, head_gain, decay),
        [values, key_spec(block_len), values, values]
        + [pl.BlockSpec((1, DV), lambda s, h, first: (0, 0)), decay_spec],
        (
            ((seq_count, block_len, HEADS * DV), jnp.float32),
            ((seq_count, block_len, HEADS * DV), jnp.bfloat16),
            ((GROUP, DK + EXTRA, DV), jnp.bfloat16),
            ((seq_count, HEADS, 1, DV), jnp.float32),
        ),
        [values, values, pair_spec(DK + EXTRA)]
        + [pl.BlockSpec((1, 1, 1, DV), lambda s, h, first: (s, h, 0, 0))],
        seq_count,
        5,
    )


def conv_back(grad, found, taps, pos, starts, block_len):
    wide, total, sig = found
    grad = grad * sig * (1.0 + total * (1.0 - sig))
    zeros = jnp.zeros((HALO, grad.shape[1]), jnp.float32)
    spread_grad, tap_grads = None, []
    for tap in range(CONV):
        masked = grad if tap == 0 else grad * (pos - tap >= starts).astype(jnp.float32)
        source = wide[HALO - tap : HALO - tap + block_len]
        tap_grads.append(jnp.sum(masked * source, axis=0, keepdims=True))
        padded = jnp.concatenate([zeros, masked * taps[tap : tap + 1, :], zeros], axis=0)
        part = padded[tap : tap + HALO + block_len]
        spread_grad = part if spread_grad is None else spread_grad + part
    return spread_grad, jnp.concatenate(tap_grads, axis=0)


def mixer_backward(first, wide_mixed, conv_weight, logits, starts, out_grad, incoming, outgoing):
    seq_count, block_len = starts.shape[:2]

    def kernel(first_ref, block, taps, logit_ref, start_ref, *refs):
        grad_ref, in_ref, end_ref, main, edge, tail, tap_grad, dlogit, bias = refs
        first, starts = first_ref[0], start_ref[0]
        pos, found, query, key, value = activations(block, taps, starts, first, block_len)
        logit = logit_ref[0]
        log_decay = decays(logit)
        count = block_len // WIDE
        spans, states = [], [in_ref[0].astype(jnp.float32)]
        for index in range(count):
            span = Span(index, first, query, key, value, log_decay, starts, pos)
            spans.append(span)
            if index + 1 < count:
                states.append(span.next_state(states[-1]))
        later = end_ref[0].astype(jnp.float32)
        query_grads, key_grads, value_grads, decay_grads = [], [], [], []
        for index in range(count)[::-1]:
            span, state = spans[index], states[index]
            grad = grad_ref[0, span.rows]
            score_grad = jnp.where(span.allowed, split_dot(grad, span.value, NT), 0.0)
            query_grad = split_dot(score_grad, span.key_centred, NN) * span.to_query
            query_grad = query_grad + split_dot(grad, state, NT) * span.from_start
            end_grad = split_dot(span.value, later, NT)
            key_grad = split_dot(score_grad, span.query_centred, TN) * span.to_key
            key_grad = key_grad + end_grad * span.to_end
            value_grad = split_dot(span.scores(), grad, TN) + split_dot(span.key_end, later, NN)
            kept = unit_dot(jnp.ones((8, DV), jnp.float32), state * later, NT)[:1]
            total_grad = jnp.sum(end_grad * span.key_end, axis=0, keepdims=True)
            total_grad = total_grad + kept * jnp.exp(span.total) * span.kept
            cum_grad = span.query * query_grad - span.key * key_grad
            decay_grads.append(unit_dot(span.upper, cum_grad, NN) + total_grad)
            query_grads.append(query_grad)
            key_grads.append(key_grad)
            value_grads.append(value_grad)
            if index > 0:
                later = later * span.keep_column + split_dot(span.query_start, grad, TN)
        grads = [
            jnp.concatenate(parts[::-1], axis=0) for parts in (query_grads, key_grads, value_grads)
        ]
        grads = jnp.concatenate([grads[0] * DK ** (-0.5)] + grads[1:], axis=1)
        wide_grad, tap_grad[0] = conv_back(grads, found, taps, pos, starts, block_len)
        edge[0] = wide_grad[:HALO]
        main[0] = wide_grad[HALO:].astype(jnp.bfloat16)
        tail[0] = wide_grad[block_len:]
        decay_grad = jnp.concatenate(decay_grads[::-1], axis=0)
        decay_grad = jnp.where(starts < pos, decay_grad, 0.0)
        logit_grad = decay_grad / gate_scale * jax.nn.sigmoid(-logit)
        dlogit[0] = logit_grad
        bias[0, 0] = jnp.sum(logit_grad, axis=0, keepdims=True)

    def heads_spec(rows):
        return pl.BlockSpec((1, rows, PER_HEAD), lambda s, h, first: (s, 0, h))

    width = HEADS * PER_HEAD
    return launch(
        kernel,
        (first, wide_mixed, conv_weight, logits, starts, out_grad, incoming, outgoing),
        mixer_specs(block_len) + [value_spec(block_len), pair_spec(DK), pair_spec(DK)],
        (
            ((seq_count, block_len, width), jnp.bfloat16),
            ((seq_count, HALO, width), jnp.float32),
            ((seq_count, HALO, width), jnp.float32),
            ((seq_count, CONV, width), jnp.float32),
            ((seq_count, block_len, HEADS * DK), jnp.float32),
            ((seq_count, HEADS, 1, DK), jnp.float32),
        ),
        [heads_spec(block_len), heads_spec(HALO), heads_spec(HALO), heads_spec(CONV)]
        + [key_spec(block_len), decay_spec],
        seq_count,
        24,
    )


def bf_dot(left, right):
    return jnp.dot(left, right, preferred_element_type=jnp.float32)


def feed_forward(hidden, out_grad, gain, gate_sources, up_sources, down_left, down_right):
    tokens, width = hidden.shape
    sizes, mine = tuple(size for size, _ in chip_axes()), coordinates()
    block_rows, inner = gate_sources[0][0].shape[3:]
    count, tile = len(gate_sources), 256
    half = width // 2
    steps = inner // tile

    def kernel(me, hid, grad, gain_ref, wl, wr, *refs):
        gate_refs, up_refs, refs = refs[:count], refs[count : 2 * count], refs[2 * count :]
        out, back, back_low, normed, act, gate_back, up_back, gain_back = refs[:8]
        total, turned, gate_held, up_held = refs[8:]
        step = pl.program_id(0)
        w_gate = assemble(gate_held, gate_refs, gate_sources, me, 2, 1)
        w_up = assemble(up_held, up_refs, up_sources, me, 1, 2)

        @pl.when(step == 0)
        def _():
            value = hid[...]
            rms = lax.rsqrt(jnp.mean(value * value, axis=-1, keepdims=True) + epsilon)
            normed[...] = (value * rms * gain_ref[...]).astype(jnp.bfloat16)
            total[...] = jnp.zeros_like(total)
            turned[...] = jnp.zeros_like(turned)

        source, low = normed[...], grad[...]
        gate, up = bf_dot(source, w_gate), bf_dot(source, w_up)
        inner_grad = nt_dot(low[:, :half], wl[...]) + nt_dot(low[:, half:], wr[...])
        sig = jax.nn.sigmoid(gate)
        silu = gate * sig
        active = (silu * up).astype(jnp.bfloat16)
        gate_grad = (inner_grad * up * sig * (1.0 + gate * (1.0 - sig))).astype(jnp.bfloat16)
        up_grad = (inner_grad * silu).astype(jnp.bfloat16)
        act[...], gate_back[...], up_back[...] = active, gate_grad, up_grad
        total[:, :half] += bf_dot(active, wl[...])
        total[:, half:] += bf_dot(active, wr[...])
        turned[...] += nt_dot(gate_grad, w_gate) + nt_dot(up_grad, w_up)

        @pl.when(step == steps - 1)
        def _():
            value, back_in = hid[...], turned[...]
            rms = lax.rsqrt(jnp.mean(value * value, axis=-1, keepdims=True) + epsilon)
            out[...] = value + total[...]
            gain_back[...] = jnp.sum(back_in * value * rms, axis=0, keepdims=True)
            result = grad[...].astype(jnp.float32) + rms_back(back_in, value, rms, gain_ref[...])
            back[...] = result
            back_low[...] = result.astype(jnp.bfloat16)

    def whole(rows, columns):
        return pl.BlockSpec((rows, columns), lambda i, me: (0, 0))

    along = pl.BlockSpec((tile, half), lambda i, me: (i, 0))
    inner_spec = pl.BlockSpec((tokens, tile), lambda i, me: (0, i))
    inner_shape = jax.ShapeDtypeStruct((tokens, inner), jnp.bfloat16)
    arrays = [array for array, _, _ in gate_sources + up_sources]
    held = pltpu.VMEM(sizes + (block_rows, tile), jnp.bfloat16)
    return pl.pallas_call(
        kernel,
        out_shape=[
            jax.ShapeDtypeStruct((tokens, width), jnp.float32),
            jax.ShapeDtypeStruct((tokens, width), jnp.float32),
            jax.ShapeDtypeStruct((tokens, width), jnp.bfloat16),
            jax.ShapeDtypeStruct((tokens, width), jnp.bfloat16),
            inner_shape,
            inner_shape,
            inner_shape,
            jax.ShapeDtypeStruct((1, width), jnp.float32),
        ],
        grid_spec=pltpu.PrefetchScalarGridSpec(
            num_scalar_prefetch=1,
            grid=(steps,),
            in_specs=[whole(tokens, width), whole(tokens, width), whole(1, width), along, along]
            + [tile_spec(array, tile, lambda i, me: (0, 0, 0, 0, i)) for array in arrays],
            out_specs=[whole(tokens, width)] * 4 + [inner_spec] * 3 + [whole(1, width)],
            scratch_shapes=[
                pltpu.VMEM((tokens, width), jnp.float32),
                pltpu.VMEM((tokens, width), jnp.float32),
                held,
                held,
            ],
        ),
        compiler_params=pltpu.CompilerParams(vmem_limit_bytes=58 * 2**20),
        cost_estimate=takes(28),
    )(mine, hidden, out_grad, gain, down_left, down_right, *arrays)


def nt_dot(left, right):
    return lax.dot_general(left, right, (NT, ((), ())), preferred_element_type=jnp.float32)


def rms_back(grad_normed, source, inv_rms, gain_vec):
    scaled = grad_normed * gain_vec
    return inv_rms * (
        scaled - source * inv_rms * inv_rms * jnp.mean(scaled * source, axis=-1, keepdims=True)
    )


def local(
    inputs,
    doc_start,
    norm_gain,
    w_in,
    conv_weight,
    w_low,
    w_high,
    gate_bias,
    head_gain,
    w_out,
    ffn_gain,
    w_gate_up,
    w_down,
    out_grad,
):
    seq_count, block_len, model_width = inputs.shape
    row_count = seq_count * block_len
    key_width = HEADS * DK
    value_width = HEADS * DV
    conv_width = 2 * key_width + value_width
    block_start = lax.axis_index("seq") * block_len
    half = model_width // 2
    first_shard = by_head(w_in[:, :conv_width])
    taps = by_head(conv_weight)
    rest_shard = jnp.concatenate([w_in[:, conv_width:], w_out, w_down], axis=0)
    rest_cuts = [w_in.shape[0], w_out.shape[0], w_down.shape[0]]
    place = jnp.stack([block_start, lax.axis_index("seq") % GROUP]).astype(jnp.int32)
    starts = doc_start[:, :, None]
    gain_row = head_gain[None, :]
    axes = chip_axes()

    fast = gather_levels(first_shard)
    edge = shifted(inputs[:, block_len - HALO :, :], 1)
    wide = jnp.concatenate([edge, inputs], axis=1).astype(jnp.float32)
    wide_rms = lax.rsqrt(jnp.mean(wide * wide, axis=-1, keepdims=True) + epsilon)
    wide_normed = (wide * wide_rms * norm_gain).astype(jnp.bfloat16)
    layer_in = wide[:, HALO:].reshape(row_count, model_width)
    inv_rms = wide_rms[:, HALO:].reshape(row_count, 1)
    fast, wide_normed, rest_shard = together(fast, wide_normed, rest_shard)
    rest = gather_levels(rest_shard)
    fast = gather_first(fast)
    normed = wide_normed[:, HALO:].reshape(row_count, model_width)
    wide_rows = wide_normed.reshape(-1, model_width)
    lowrank = bf_dot(normed, w_low)
    gate_logit = (
        jnp.dot(lowrank, w_high, precision=highest, preferred_element_type=jnp.float32) + gate_bias
    )
    fast, gate_logit, rest[1] = together(fast, gate_logit, rest[1])
    fast = gather_second(fast)
    fast, rest[2], wide_shard = together(fast, rest[2], w_gate_up)
    fast = gather_cores(fast)
    wide_pieces = gather_levels(wide_shard)
    wide_mixed = projected(wide_rows, *[[(own, 0, 0), (other, 1, 0)] for own, other in fast])
    wide_mixed = wide_mixed.reshape(seq_count, HALO + block_len, conv_width)
    wide_mixed, rest = together(wide_mixed, rest)
    rest = gather_first(rest)
    logits = gate_logit.reshape(seq_count, block_len, key_width)
    local_out, reach, local_state, block_decay = mixer_forward(
        place, wide_mixed, taps, logits, starts
    )
    local_state, rest, wide_pieces[1] = together(local_state, rest, wide_pieces[1])
    got, _ = exchanged(local_state)
    got, rest = together(got, rest)
    rest = gather_second(rest)
    beyond = shifted(composed(place, got, False), GROUP)
    incoming = composed(place, got, False, beyond)
    incoming, rest, wide_pieces = together(incoming, rest, wide_pieces)
    wide_pieces = gather_first(wide_pieces)
    rest = gather_cores(rest)
    incoming, _ = exchanged(incoming)
    incoming, rest, wide_pieces = together(incoming, rest, wide_pieces)
    crossed = gather_second(wide_pieces)
    early = [swapped(pieces[0], 1) for pieces in crossed]
    incoming, fast = together(incoming, fast)
    [(left_full, right_full)] = gather_done(fast, [first_shard.shape[0]])
    (g_left, g_right), (out_left, out_right), (down_left, down_right) = gather_done(rest, rest_cuts)
    gate_cols = jnp.concatenate([bf_dot(normed, g_left), bf_dot(normed, g_right)], axis=1)
    gates = gate_cols.astype(jnp.bfloat16).reshape(seq_count, block_len, value_width)
    mixer_out, gated = mixer_output(place, local_out, reach, incoming, gates, gain_row)
    gated = gated.reshape(row_count, value_width)
    hidden_one = layer_in + jnp.concatenate(
        [bf_dot(gated, out_left), bf_dot(gated, out_right)], axis=1
    )
    hidden_one, crossed, early = together(hidden_one, crossed, early)
    gate_sources, up_sources = core_sources(crossed, early)
    out_rows_low = out_grad.reshape(row_count, model_width)
    (
        layer_out,
        hidden_grad,
        hidden_low,
        ffn_in,
        activation,
        gate_grad,
        up_grad,
        ffn_gain_row,
    ) = feed_forward(
        hidden_one, out_rows_low, ffn_gain[None, :], gate_sources, up_sources, down_left, down_right
    )
    gated_grad = nt_dot(hidden_low[:, :half], out_left) + nt_dot(hidden_low[:, half:], out_right)
    gated_grad = gated_grad.reshape(seq_count, block_len, value_width)
    mixer_grad, gate_vals_grad, state_term, head_gain_grad = mixer_output_back(
        place, mixer_out, reach, gated_grad, gates, gain_row, block_decay
    )
    gate_vals_grad = gate_vals_grad.reshape(row_count, value_width)

    state_term, gated, ffn_in, activation = together(state_term, gated, ffn_in, activation)
    got, (out_terms, wide_terms, down_terms) = exchanged(
        state_term,
        (
            (lambda: grad_products(gated, hidden_low),),
            (lambda _: grad_products(ffn_in, gate_grad, up_grad),),
            (lambda _: grad_products(activation, out_rows_low),),
        ),
    )
    wide_terms = cores_send([wide_terms])
    total = composed(place, got, True)
    total, parts, wide_terms = together(total, phase_parts(wide_terms, 0), wide_terms)
    wide_terms = phase_swap(wide_terms, 0, parts)
    beyond = shifted(total, -GROUP)
    g_terms = grad_products(normed, gate_vals_grad)
    beyond, g_terms, out_terms, down_terms = together(beyond, g_terms, out_terms, down_terms)
    rest_terms = cores_send([g_terms, out_terms, down_terms])
    outgoing = composed(place, got, True, beyond)
    shape = outgoing.shape
    outgoing = outgoing.reshape((2, 2, 2) + shape[1:])
    outgoing = jnp.stack(exchange_step(outgoing, 2, 1), axis=2)
    outgoing = jnp.stack(exchange_step(outgoing, 1, 2), axis=1)
    outgoing, wide_terms, rest_terms = together(outgoing, wide_terms, rest_terms)
    wide_terms = phase_send(wide_terms, 1)
    outgoing = jnp.stack(exchange_step(outgoing, 0, 4)).reshape(shape)
    outgoing, wide_terms = together(outgoing, wide_terms)
    wide_sums = level_sums(wide_terms)
    outgoing, wide_sums, rest_terms = together(outgoing, wide_sums, rest_terms)
    wide_own, wide_last = levels_send(wide_sums)
    rest_terms = phase_send(rest_terms, 0)
    backs = mixer_backward(
        place, wide_mixed, taps, logits, starts, mixer_grad, incoming, outgoing
    )
    backs, rest_terms, wide_last[0] = together(backs, rest_terms, wide_last[0])
    rest_terms = phase_send(rest_terms, 1)
    mixed_grad, back_edge, back_tail, tap_grads, logit_grad, gate_bias_grad = backs
    back_edge = shifted(back_edge.astype(jnp.bfloat16), -1).astype(jnp.float32)
    mixed_grad = lax.dynamic_update_slice(
        mixed_grad, (back_tail + back_edge).astype(jnp.bfloat16), (0, block_len - HALO, 0)
    )
    mixed_grad = mixed_grad.reshape(row_count, conv_width)
    small_rows, lowrank_grad = small_packed(
        logit_grad.reshape(row_count, key_width),
        lowrank,
        w_high,
        normed,
        tap_grads,
        gate_bias_grad.reshape(seq_count, key_width),
        head_gain_grad,
        ffn_gain_row,
    )
    normed_grad = (
        nt_dot(mixed_grad[:, : conv_width // 2], left_full)
        + nt_dot(mixed_grad[:, conv_width // 2 :], right_full)
        + nt_dot(gate_vals_grad[:, :half], g_left)
        + nt_dot(gate_vals_grad[:, half:], g_right)
        + nt_dot(lowrank_grad, w_low)
    )
    norm_gain_grad = jnp.sum(normed_grad * layer_in * inv_rms, axis=0)
    input_grad = hidden_grad + rms_back(normed_grad, layer_in, inv_rms, norm_gain)
    small_rows = lax.dynamic_update_slice(small_rows, norm_gain_grad[None, :], (34, 0))
    mixed_grad, small_rows, rest_terms, input_grad, wide_last[1] = together(
        mixed_grad, small_rows, rest_terms, input_grad, wide_last[1]
    )
    rest_sums = level_sums(rest_terms)
    small_rows = spread(small_rows, axes[3])
    mixed_grad, rest_sums, small_rows = together(mixed_grad, rest_sums, small_rows)
    rest_own, rest_last = levels_send(rest_sums)
    fast_terms = grad_products(normed, mixed_grad)
    small_rows = spread(sum(small_rows), axes[2])
    fast_terms, small_rows, wide_last[2] = together(fast_terms, small_rows, wide_last[2])
    fast_terms = cores_send([fast_terms])
    small_rows = spread(sum(small_rows), axes[1])
    fast_terms, small_rows = together(fast_terms, small_rows)
    fast_terms = phase_send(fast_terms, 0)
    small_rows = sum(small_rows)
    fast_terms, small_rows, rest_last[0] = together(fast_terms, small_rows, rest_last[0])
    fast_terms = phase_send(fast_terms, 1)
    fast_terms, rest_last[1] = together(fast_terms, rest_last[1])
    fast_own, fast_last = levels_send(level_sums(fast_terms))
    small_rows = [small_rows]
    small_own = sum(small_rows)
    small_parts = spread(small_own.astype(jnp.bfloat16), axes[0])
    norm_gain_grad, conv_weight_grad, w_low_grad, w_high_grad, *rows_found = small_unpacked(
        small_parts, key_width, w_high.shape[0]
    )
    gate_bias_grad, head_gain_grad, ffn_gain_grad = [row[0] for row in rows_found]
    rest_grad = reduced(rest_own, rest_last)
    w_gate_up_grad = reduced(wide_own, wide_last)
    fast_grad = by_kind(reduced(fast_own, fast_last))
    ends = [rest_cuts[0], rest_cuts[0] + rest_cuts[1]]
    w_in_grad = jnp.concatenate([fast_grad, rest_grad[: ends[0]]], axis=1)
    w_out_grad = rest_grad[ends[0] : ends[1]]
    w_down_grad = rest_grad[ends[1] :]
    return (
        layer_out.reshape(seq_count, block_len, model_width),
        input_grad.reshape(seq_count, block_len, model_width),
        norm_gain_grad[0],
        w_in_grad,
        conv_weight_grad,
        w_low_grad.T,
        w_high_grad,
        gate_bias_grad,
        head_gain_grad,
        w_out_grad,
        ffn_gain_grad,
        w_gate_up_grad,
        w_down_grad,
    )


def solution(mesh):
    placed = (
        P(None, "seq", None),
        P(None, "seq"),
        P(),
        P("seq", None),
        P(),
        P(),
        P(),
        P(),
        P(),
        P("seq", None),
        P(),
        P("seq", None),
        P("seq", None),
        P(None, "seq", None),
    )
    return jax.shard_map(
        local,
        mesh=mesh,
        in_specs=placed,
        out_specs=(
            P(None, "seq", None),
            P(None, "seq", None),
            P(),
            P("seq", None),
            P(),
            P(),
            P(),
            P(),
            P(),
            P("seq", None),
            P(),
            P("seq", None),
            P("seq", None),
        ),
        check_vma=False,
    )
```
